512 devices in a mesh: dp: 16 (over y_hi, x, core), fsdp: 32 (over y_lo, z).
Axes of the slice: x: 4, y: 8 (y_hi: 2, y_lo: 4; y = y_hi * 4 + y_lo), z: 8, core: 2. Of those that a mesh axis runs over, the one named last changes fastest.
Arguments:
- out_first: bfloat16 [4096, 4096], P('dp', 'fsdp'), may hold values from -6 to 6
- out_second: bfloat16 [4096, 4096], P('dp', 'fsdp'), may hold values from -160 to 160
- grad_first: bfloat16 [4096, 4096], P('dp', 'fsdp'), may hold values from -6 to 6
- grad_second: bfloat16 [4096, 4096], P('dp', 'fsdp'), may hold values from -6 to 6
- norm_gain: bfloat16 [4096], replicated, may hold values from 0.5 to 2
- query_proj: bfloat16 [4096, 4096], P(None, 'fsdp'), may hold values from -1 to 1
- key_proj: bfloat16 [4096, 4096], P(None, 'fsdp'), may hold values from -5 to 5
- value_proj: bfloat16 [4096, 4096], P(None, 'fsdp'), may hold values from -3 to 3
- output_proj: bfloat16 [4096, 4096], P('fsdp'), may hold values from -1 to 1
- adapter_down: bfloat16 [4096, 64], P('fsdp'), may hold values from -0.09375 to 0.09375
- adapter_up: bfloat16 [64, 4096], P(None, 'fsdp'), may hold values from -0.375 to 0.375
Outputs:
- in_first: bfloat16 [4096, 4096], P('dp', 'fsdp')
- in_second: bfloat16 [4096, 4096], P('dp', 'fsdp')
- first_grad: bfloat16 [4096, 4096], P('dp', 'fsdp')
- second_grad: bfloat16 [4096, 4096], P('dp', 'fsdp')
- down_grad: float32 [4096, 64], P('fsdp')
- up_grad: float32 [64, 4096], P(None, 'fsdp')
The draws below stay inside these ranges and needn't reach their ends.
All inputs are finite; a program needn't handle non-finite values.
Results may differ from the reference program's by a relative error of at most 0.035.
Values may be sent and summed in bfloat16 or wider, within the bound.
No kernel may reach another device: no remote copies, remote signals or barrier semaphores. Data moves between devices by JAX's collectives and lax.ppermute only.
A program may use at most 64 MiB of HBM per device.

```python
import math
import jax
import jax.numpy as jnp
from jax import lax

HEADS = 32
HEAD_DIM = 128
RANK = 64
TOK = 256
D = 4096
TOKENS = 4096
N_FSDP = 32


def shared_query(key):
    base_draw = jnp.clip(jax.random.normal(key, (D, D), jnp.float32), -5.0, 5.0)
    return base_draw * D ** (-0.5)


def stream_parts(key):
    key = jax.random.fold_in(key, 101)
    row_key, vector_key = jax.random.split(key)
    shared_rows = jnp.clip(jax.random.normal(row_key, (TOKENS, D), jnp.float32), -4.0, 4.0)
    common_vector = jnp.clip(jax.random.normal(vector_key, (1, D), jnp.float32), -3.0, 3.0)
    return (shared_rows, common_vector)


def value_output_parts(key):
    key = jax.random.fold_in(key, 102)
    base_key, fresh_key, pair_key = jax.random.split(key, 3)
    block_width = D // N_FSDP
    pairing = jax.random.permutation(pair_key, N_FSDP).astype(jnp.int32)
    block_ids = jnp.arange(D, dtype=jnp.int32) // block_width
    paired_rows = pairing[block_ids]
    spike_mask = jnp.where(block_ids[:, None] == paired_rows[None, :], 4.0, 1.0)
    value_base = jnp.clip(jax.random.normal(base_key, (D, D), jnp.float32), -4.0, 4.0) * (D // 16) ** (-0.5) * spike_mask
    fresh_part = jnp.clip(jax.random.normal(fresh_key, (D, D), jnp.float32), -4.0, 4.0) * D ** (-0.5) * spike_mask.T
    output_base = (0.5 * value_base.T + fresh_part) * 5.0 ** (-0.5)
    return (value_base, output_base)


def draw_query_proj(key, part):
    common = shared_query(key)
    return common.astype(jnp.bfloat16)


def draw_key_proj(key, part):
    key = jax.random.fold_in(key, 12)
    noise_key = jax.random.fold_in(key, 0)
    fresh = jnp.clip(jax.random.normal(noise_key, (D, D), jnp.float32), -5.0, 5.0) * D ** (-0.5)
    return fresh.astype(jnp.bfloat16)


def draw_value_proj(key, part):
    value_base, output_base = value_output_parts(key)
    return value_base.astype(jnp.bfloat16)


def draw_output_proj(key, part):
    value_base, output_base = value_output_parts(key)
    return output_base.astype(jnp.bfloat16)


def draw_out_second(key, part):
    shared_rows, common_vector = stream_parts(key)
    key = jax.random.fold_in(key, 21)
    row_key = jax.random.fold_in(key, 1)
    col_key = jax.random.fold_in(key, 2)
    row_scale = jnp.exp(jax.random.uniform(row_key, (TOKENS, 1), jnp.float32, math.log(0.3), math.log(3.0)))
    col_pos = jnp.arange(D, dtype=jnp.float32) / (D - 1)
    col_rand = jnp.exp(jax.random.uniform(col_key, (1, D), jnp.float32, math.log(0.3), math.log(3.0)))
    base_draw = shared_rows
    col_scale = col_rand * jnp.sqrt(1.0 + 2.0 * col_pos)[None, :]
    base_draw = base_draw + 0.5 * common_vector
    return (base_draw * row_scale * col_scale).astype(jnp.bfloat16)


def draw_grad_first(key, part):
    shared_rows, common_vector = stream_parts(key)
    key = jax.random.fold_in(key, 31)
    fresh = jnp.clip(jax.random.normal(key, (TOKENS, D), jnp.float32), -4.0, 4.0)
    return (0.6 * fresh + 0.5 * common_vector + 0.5 * shared_rows).astype(jnp.bfloat16)


def block_levels(own_key, extent, cuts, least, largest):
    gain = 1.0
    for dim, shards_of in cuts:
        draws = jax.random.uniform(jax.random.fold_in(jax.random.fold_in(own_key, 6), dim), (shards_of,), jnp.float32, least / len(cuts), largest / len(cuts))
        gain = gain * jnp.repeat(jnp.exp(draws), extent[dim] // shards_of).reshape((-1,) + (1,) * (len(extent) - 1 - dim))
    return gain


def normal_values(stream_key, extent, spread, bound, pieces=(), held_as=jnp.bfloat16):
    factor_of = block_levels(stream_key, extent, pieces, -0.22, 0.18) if pieces else 1.0
    values = jax.random.normal(stream_key, extent, jnp.float32) * spread * factor_of
    return jnp.minimum(jnp.maximum(values, -bound), bound).astype(held_as)


def setup_inputs(seed: int = 0) -> dict:
    key_list = jax.random.split(jax.random.key(seed), 12)
    out_first = normal_values(key_list[0], (TOKENS, D), 1.0, 6.0, ((0, 16), (1, 32)))
    out_second = draw_out_second(jax.random.fold_in(key_list[11], 71), 0)
    grad_first = draw_grad_first(jax.random.fold_in(key_list[11], 71), 0)
    grad_second = normal_values(key_list[3], (TOKENS, D), 1.0, 6.0, ((0, 16), (1, 32)))
    norm_gain = jnp.clip(jnp.exp(jax.random.uniform(key_list[4], (D,), jnp.float32, math.log(0.5), math.log(2.0))), 0.5, 2.0).astype(jnp.bfloat16)
    query_proj = draw_query_proj(jax.random.fold_in(key_list[11], 71), 0)
    key_proj = draw_key_proj(jax.random.fold_in(key_list[11], 71), 0)
    value_proj = draw_value_proj(jax.random.fold_in(key_list[11], 71), 0)
    output_proj = draw_output_proj(jax.random.fold_in(key_list[11], 71), 0)
    adapter_down = normal_values(key_list[9], (D, RANK), D ** -0.5, 0.09375, ((0, 32),))
    adapter_up = normal_values(key_list[10], (RANK, D), (D // 16) ** -0.5, 0.375, ((1, 32),))
    return {"out_first": out_first, "out_second": out_second, "grad_first": grad_first, "grad_second": grad_second, "norm_gain": norm_gain, "query_proj": query_proj, "key_proj": key_proj, "value_proj": value_proj, "output_proj": output_proj, "adapter_down": adapter_down, "adapter_up": adapter_up}


EPS = 1e-05
MASKED = -1e+30

def silu_slope(pre_act):
    logistic = jax.nn.sigmoid(pre_act)
    return logistic * (1.0 + pre_act * (1.0 - logistic))

def reference(out_first, out_second, grad_first, grad_second, norm_gain, query_proj, key_proj, value_proj, output_proj, adapter_down, adapter_up):
    token_count = out_first.shape[0]
    groups_all = token_count // TOK
    shard_width = D // N_FSDP
    score_scale = HEAD_DIM ** (-0.5)
    pre_act = jnp.dot(out_first, adapter_down, preferred_element_type=jnp.float32)
    activation = jax.nn.silu(pre_act).astype(jnp.bfloat16)
    in_second = (out_second.astype(jnp.float32) - jnp.dot(activation, adapter_up, preferred_element_type=jnp.float32)).astype(jnp.bfloat16)
    second_wide = in_second.astype(jnp.float32)
    inv_rms = lax.rsqrt(lax.optimization_barrier(jnp.mean(second_wide * second_wide, axis=1, keepdims=True)) + EPS)
    gain_wide = norm_gain.astype(jnp.float32)
    normed = (second_wide * inv_rms * gain_wide).astype(jnp.bfloat16)
    query_rows = jnp.dot(normed, query_proj, preferred_element_type=jnp.float32).astype(jnp.bfloat16)
    key_rows = jnp.dot(normed, key_proj, preferred_element_type=jnp.float32).astype(jnp.bfloat16)
    value_rows = jnp.dot(normed, value_proj, preferred_element_type=jnp.float32).astype(jnp.bfloat16)

    def by_heads(matrix):
        return matrix.reshape(groups_all, TOK, HEADS, HEAD_DIM).astype(jnp.float32)
    query_heads = by_heads(query_rows)
    key_heads = by_heads(key_rows)
    value_heads = by_heads(value_rows)
    query_pos = lax.broadcasted_iota(jnp.int32, (TOK, TOK), 0)
    key_pos = lax.broadcasted_iota(jnp.int32, (TOK, TOK), 1)
    allowed = key_pos <= query_pos
    scores = jnp.einsum('gqhd,gkhd->ghqk', query_heads, key_heads) * score_scale
    scores = jnp.where(allowed[None, None], scores, MASKED)
    row_peak = lax.optimization_barrier(jnp.max(scores, axis=-1, keepdims=True))
    weights = jnp.exp(scores - row_peak)
    attn_probs = (weights / lax.optimization_barrier(jnp.sum(weights, axis=-1, keepdims=True))).astype(jnp.bfloat16)
    prob_wide = attn_probs.astype(jnp.float32)
    context = jnp.einsum('ghqk,gkhd->gqhd', prob_wide, value_heads).astype(jnp.bfloat16).reshape(token_count, D)

    def block_sum(make_term):

        def add_block(running, block_index):
            block_start = block_index * shard_width
            partial_value = make_term(block_start).astype(jnp.bfloat16)
            partial_value = lax.optimization_barrier(partial_value)
            return (running + partial_value.astype(jnp.float32), None)
        running, unused = lax.scan(add_block, jnp.zeros((token_count, D), jnp.float32), jnp.arange(N_FSDP, dtype=jnp.int32))
        return running

    def attention_term(block_start):
        columns = lax.dynamic_slice_in_dim(context, block_start, shard_width, 1)
        rows_block = lax.dynamic_slice_in_dim(output_proj, block_start, shard_width, 0)
        return jnp.dot(columns, rows_block, preferred_element_type=jnp.float32)
    attn_out = block_sum(attention_term)
    in_first = (out_first.astype(jnp.float32) - attn_out).astype(jnp.bfloat16)
    back_sum = jnp.dot(grad_second, adapter_up.T, preferred_element_type=jnp.float32)
    pre_grad = (back_sum * silu_slope(pre_act)).astype(jnp.bfloat16)
    first_grad = (grad_first.astype(jnp.float32) + jnp.dot(pre_grad, adapter_down.T, preferred_element_type=jnp.float32)).astype(jnp.bfloat16)
    back_ctx = jnp.dot(first_grad, output_proj.T, preferred_element_type=jnp.float32).astype(jnp.bfloat16)
    ctx_heads = by_heads(back_ctx)
    value_grad = jnp.einsum('ghqk,gqhd->gkhd', prob_wide, ctx_heads).astype(jnp.bfloat16).reshape(token_count, D)
    prob_grad = jnp.einsum('gqhd,gkhd->ghqk', ctx_heads, value_heads)
    score_grad = (prob_wide * (prob_grad - lax.optimization_barrier(jnp.sum(prob_grad * prob_wide, axis=-1, keepdims=True))) * score_scale).astype(jnp.bfloat16)
    score_wide = score_grad.astype(jnp.float32)
    query_grad = jnp.einsum('ghqk,gkhd->gqhd', score_wide, key_heads).astype(jnp.bfloat16).reshape(token_count, D)
    key_grad = jnp.einsum('ghqk,gqhd->gkhd', score_wide, query_heads).astype(jnp.bfloat16).reshape(token_count, D)

    def input_term(block_start):

        def one_product(grads, weight):
            grad_block = lax.dynamic_slice_in_dim(grads, block_start, shard_width, 1)
            weight_block = lax.dynamic_slice_in_dim(weight, block_start, shard_width, 1)
            return lax.dot_general(grad_block, weight_block, (((1,), (1,)), ((), ())), preferred_element_type=jnp.float32)
        return one_product(query_grad, query_proj) + one_product(key_grad, key_proj) + one_product(value_grad, value_proj)
    norm_grad = block_sum(input_term)
    gain_grad = gain_wide * norm_grad
    row_stat = lax.optimization_barrier(jnp.mean(gain_grad * second_wide, axis=1, keepdims=True))
    second_grad = (grad_second.astype(jnp.float32) + inv_rms * (gain_grad - second_wide * row_stat * inv_rms * inv_rms)).astype(jnp.bfloat16)
    down_grad = jnp.dot(out_first.T, pre_grad, preferred_element_type=jnp.float32)
    up_grad = jnp.dot(activation.T, grad_second, preferred_element_type=jnp.float32)
    return (in_first, in_second, first_grad, second_grad, down_grad, up_grad)
```

```python
import functools

import jax
import jax.numpy as jnp
from jax import lax
from jax.experimental import pallas as pl
from jax.experimental.pallas import tpu as pltpu
from jax.sharding import Mesh, PartitionSpec as P

HEAD_DIM = 128
RANK = 64
EPS = 1e-05
MASKED = -1e30

QUAD = ("yb", "zb")
OCTET = ("ya", "za")
PLANE = ("ya", "yb", "za", "zb")
SEQS = ("yh", "x", "c")
F32 = jnp.float32
BF16 = jnp.bfloat16


def dot(a, b, dims=((1,), (0,)), precision=None):
    return lax.dot_general(a, b, (dims, ((), ())), preferred_element_type=F32, precision=precision)


NT = ((1,), (1,))
TN = ((0,), (0,))


def row_sums(wide):
    sums = dot(jnp.ones((8, 128), F32), wide, NT, lax.Precision.HIGHEST)
    lead = sums.astype(BF16)
    rest = (sums - lead.astype(F32)).astype(BF16)
    return lead, rest


def to_column(row):
    return jnp.broadcast_to(row, (128, row.shape[1])).T


def call(body, out_shapes, interpret, **kwargs):
    return pl.pallas_call(
        body,
        out_shape=out_shapes,
        compiler_params=pltpu.CompilerParams(vmem_limit_bytes=48 * 1024 * 1024),
        interpret=interpret,
        **kwargs,
    )


def bottleneck_kernel(first_ref, second_ref, down_ref, up_ref, out_ref):
    out_ref[:, :RANK] = dot(first_ref[...], down_ref[...])
    out_ref[:, RANK:] = dot(second_ref[...], up_ref[...], NT)


def project_kernel(
    sums_ref, gathered_ref, gain_ref, weights_ref, first_ref, second_ref, gfirst_ref, gsecond_ref, up_ref, downt_ref,
    partial_ref, in_second_ref, first_grad_ref, adapters_ref, x_ref, g_ref,
):
    seq = first_ref.shape[0]
    sums = sums_ref[...]
    pre_act = sums[:, :RANK]
    back_sum = pltpu.roll(sums, RANK, 1)[:, :RANK]
    logistic = 1.0 / (1.0 + jnp.exp(-pre_act))
    activation = (pre_act * logistic).astype(BF16)
    pre_grad = (back_sum * (logistic * (1.0 + pre_act * (1.0 - logistic)))).astype(BF16)

    def reconstruct(rows, up):
        return (rows.astype(F32) - dot(activation, up)).astype(BF16)

    def back(rows, downt):
        return (rows.astype(F32) + dot(pre_grad, downt)).astype(BF16)

    in_second_ref[...] = reconstruct(second_ref[...], up_ref[...])
    first_grad_ref[...] = back(gfirst_ref[...], downt_ref[...])
    adapters_ref[:RANK] = dot(pre_grad, first_ref[...], TN)
    adapters_ref[RANK:] = dot(activation, gsecond_ref[...], TN)
    squares = jnp.zeros((seq, 128), F32)
    for f in range(8):
        lanes = slice(f * 128, f * 128 + 128)
        wide = reconstruct(gathered_ref[f, :seq], gathered_ref[f, 2 * seq : 2 * seq + RANK]).astype(F32)
        squares = squares + wide * wide
        x_ref[:, lanes] = (wide * gain_ref[f : f + 1, :]).astype(BF16)
        g_ref[:, lanes] = back(gathered_ref[f, seq : 2 * seq], gathered_ref[f, 2 * seq + RANK :])
    lead, rest = row_sums(squares)
    for h in range(4):
        qkv = dot(x_ref[:, :512], weights_ref[0, h, :, :384]) + dot(x_ref[:, 512:], weights_ref[1, h, :, :384])
        ctx = dot(g_ref[:, :512], weights_ref[0, h, :, 384:]) + dot(g_ref[:, 512:], weights_ref[1, h, :, 384:])
        partial_ref[h, :seq, :384] = qkv.astype(BF16)
        partial_ref[h, :seq, 384:] = ctx.astype(BF16)
        partial_ref[h, seq:, :seq] = jnp.concatenate([lead, rest], 0)
        partial_ref[h, seq:, seq:] = jnp.zeros((16, 512 - seq), BF16)


def attention_kernel(width, partial_ref, out_ref, inv_ref):
    seq = inv_ref.shape[0]
    scale = HEAD_DIM ** (-0.5)

    def total(lo, hi):
        rows = partial_ref[0, :seq, lo:hi].astype(F32)
        for s in range(1, 4):
            rows = rows + partial_ref[s, :seq, lo:hi].astype(F32)
        return rows

    square = jnp.zeros((1, seq), F32)
    for s in range(4):
        tail = partial_ref[s, seq:, :seq].astype(F32)
        square = square + tail[:1] + tail[8:9]
    inv = to_column(lax.rsqrt(square / width + EPS))
    inv_ref[...] = inv
    query_wide, key_wide, value_wide = total(0, 128) * inv, total(128, 256) * inv, total(256, 384) * inv
    query, key, value = query_wide.astype(BF16), key_wide.astype(BF16), value_wide.astype(BF16)
    back_ctx = total(384, 512).astype(BF16)
    scores = dot(query, key, NT) * scale
    query_pos = lax.broadcasted_iota(jnp.int32, (seq, seq), 0)
    key_pos = lax.broadcasted_iota(jnp.int32, (seq, seq), 1)
    scores = jnp.where(key_pos <= query_pos, scores, MASKED)
    weights = jnp.exp(scores - jnp.max(scores, axis=1, keepdims=True))
    probs = (weights / jnp.sum(weights, axis=1, keepdims=True)).astype(BF16)
    context = dot(probs, value).astype(BF16)
    value_grad = dot(probs, back_ctx, TN).astype(BF16)
    prob_grad = dot(back_ctx, value, NT)
    prob_wide = probs.astype(F32)
    inner = jnp.sum(prob_grad * prob_wide, axis=1, keepdims=True)
    score_grad = (prob_wide * (prob_grad - inner) * scale).astype(BF16)
    query_grad = dot(score_grad, key).astype(BF16)
    key_grad = dot(score_grad, query, TN).astype(BF16)
    stat = (
        query_grad.astype(F32) * query_wide + key_grad.astype(F32) * key_wide + value_grad.astype(F32) * value_wide
    )
    lead, rest = row_sums(stat)
    tail = jnp.concatenate([lead, rest], 0)
    for s in range(4):
        out_ref[s, :seq, :128] = query_grad
        out_ref[s, :seq, 128:256] = key_grad
        out_ref[s, :seq, 256:384] = value_grad
        out_ref[s, :seq, 384:] = context
        out_ref[s, seq:, :seq] = tail
        out_ref[s, seq:, seq:] = jnp.zeros((16, 512 - seq), BF16)


def spread_kernel(grads_ref, weights_ref, out_ref):
    seq = grads_ref.shape[1] - 16
    stat = jnp.zeros((8, seq), F32)
    for h in range(4):
        tail = grads_ref[h, seq:, :seq].astype(F32)
        stat = stat + tail[:8] + tail[8:]
    lead = stat.astype(BF16)
    rest = (stat - lead.astype(F32)).astype(BF16)
    tail = jnp.concatenate([lead, rest], 0)
    for y in range(2):
        norm = jnp.zeros((seq, 512), F32)
        attn = jnp.zeros((seq, 512), F32)
        for h in range(4):
            norm = norm + dot(grads_ref[h, :seq, :384], weights_ref[y, h, :, :384], NT)
            attn = attn + dot(grads_ref[h, :seq, 384:], weights_ref[y, h, :, 384:], NT)
        for z in range(4):
            lanes = slice(z * 128, z * 128 + 128)
            out_ref[y * 4 + z, :seq] = attn[:, lanes].astype(BF16)
            out_ref[y * 4 + z, seq : 2 * seq] = norm[:, lanes].astype(BF16)
            out_ref[y * 4 + z, 2 * seq : 2 * seq + 16] = tail[:, :128]
            out_ref[y * 4 + z, 2 * seq + 16 :] = tail[:, 128:]


def finish_kernel(width, terms_ref, inv_ref, first_ref, in_second_ref, gsecond_ref, gain_ref, in_first_ref, second_grad_ref):
    seq = first_ref.shape[0]
    total = terms_ref[0].astype(F32)
    for s in range(1, 8):
        total = total + terms_ref[s].astype(F32)
    in_first_ref[...] = (first_ref[...].astype(F32) - total[:seq]).astype(BF16)
    halves = [total[2 * seq + i : 2 * seq + i + 1] + total[2 * seq + i + 8 : 2 * seq + i + 9] for i in (0, 16)]
    stat = jnp.concatenate([to_column(half) for half in halves], 0) / width
    inv = inv_ref[...]
    gain_grad = gain_ref[...] * total[seq : 2 * seq]
    second = in_second_ref[...].astype(F32)
    second_grad_ref[...] = (gsecond_ref[...].astype(F32) + inv * (gain_grad - second * stat * inv)).astype(BF16)


def shards(
    interpret,
    out_first,
    out_second,
    grad_first,
    grad_second,
    norm_gain,
    query_proj,
    key_proj,
    value_proj,
    output_proj,
    adapter_down,
    adapter_up,
):
    seq = out_first.shape[0]
    width = query_proj.shape[0]
    shape = jax.ShapeDtypeStruct
    core = lax.axis_index("c")

    def cut(matrix):
        half = lax.dynamic_slice_in_dim(matrix, core * (width // 2), width // 2)
        return half.reshape(2, 4, 2, 128, 128).transpose(0, 2, 1, 3, 4).reshape(4, 512, 128)

    pieces = jnp.concatenate([cut(query_proj), cut(key_proj), cut(value_proj), cut(output_proj.T)], 2)
    heads = lax.all_to_all(pieces, QUAD, 0, 0)
    weights = lax.all_to_all(jnp.broadcast_to(heads[None], (2, 4, 512, 512)), "c", 0, 0)

    down_t = adapter_down.T
    streams = jnp.concatenate([out_second, grad_first, adapter_up, down_t], 0)
    gathered = lax.all_gather(streams, OCTET, axis=0)

    partial = call(bottleneck_kernel, shape((seq, 128), F32), interpret)(out_first, grad_second, adapter_down, adapter_up)
    terms = lax.all_to_all(partial.reshape(32, seq // 32, 128), PLANE, 0, 0)
    mine = jnp.sum(terms, 0)
    sums = lax.all_to_all(jnp.broadcast_to(mine[None], terms.shape), PLANE, 0, 0).reshape(seq, 128)

    gain = norm_gain.astype(F32).reshape(2, 2, 4, 2, 128)
    gain = lax.dynamic_index_in_dim(gain, lax.axis_index("yb"), 1, False)
    gain = lax.dynamic_index_in_dim(gain, lax.axis_index("zb"), 2, False).reshape(8, 128)
    gain_local = lax.dynamic_slice_in_dim(gain, lax.axis_index(OCTET), 1)

    projected, in_second, first_grad, adapters = call(
        project_kernel,
        (
            shape((4, seq + 16, 512), BF16),
            shape((seq, 128), BF16),
            shape((seq, 128), BF16),
            shape((2 * RANK, 128), F32),
        ),
        interpret,
        scratch_shapes=[pltpu.VMEM((seq, 1024), BF16), pltpu.VMEM((seq, 1024), BF16)],
    )(sums, gathered, gain, weights, out_first, out_second, grad_first, grad_second, adapter_up, down_t)
    adapter_grads = jnp.sum(lax.all_gather(adapters, SEQS, axis=0), 0)

    projected = lax.all_to_all(projected, QUAD, 0, 0)
    grads, inv_rms = call(
        functools.partial(attention_kernel, width),
        (shape((4, seq + 16, 512), BF16), shape((seq, 128), F32)),
        interpret,
    )(projected)
    grads = lax.all_to_all(grads, QUAD, 0, 0)
    outward = call(spread_kernel, shape((8, 2 * seq + 32, 128), BF16), interpret)(grads, weights)
    inward = lax.all_to_all(outward, OCTET, 0, 0)
    in_first, second_grad = call(
        functools.partial(finish_kernel, width),
        (shape((seq, 128), BF16), shape((seq, 128), BF16)),
        interpret,
    )(inward, inv_rms, out_first, in_second, grad_second, gain_local)
    return (in_first, in_second, first_grad, second_grad, adapter_grads[:RANK].T, adapter_grads[RANK:])


def over(mesh, interpret=False):
    rows, columns = P(SEQS, PLANE), P(None, PLANE)
    return jax.shard_map(
        functools.partial(shards, interpret),
        mesh=mesh,
        in_specs=(rows, rows, rows, rows, P(), columns, columns, columns, P(PLANE, None), P(PLANE, None), columns),
        out_specs=(rows, rows, rows, rows, P(PLANE, None), columns),
        check_vma=False,
    )


def solution(mesh):
    devices = mesh.devices.reshape(2, 4, 2, 2, 2, 4, 2)
    return over(Mesh(devices, SEQS + PLANE))
```

```python
import functools

import jax
import jax.numpy as jnp
from jax import lax
from jax.experimental import pallas as pl
from jax.experimental.pallas import tpu as pltpu
from jax.sharding import Mesh, PartitionSpec as P

HEAD_DIM = 128
RANK = 64
EPS = 1e-05
MASKED = -1e30

QUAD = ("yb", "zb")
OCTET = ("ya", "za")
PLANE = ("ya", "yb", "za", "zb")
SEQS = ("yh", "x", "c")
F32 = jnp.float32
BF16 = jnp.bfloat16


def dot(a, b, dims=((1,), (0,)), precision=None):
    return lax.dot_general(a, b, (dims, ((), ())), preferred_element_type=F32, precision=precision)


NT = ((1,), (1,))
TN = ((0,), (0,))


def row_sums(wide):
    sums = dot(jnp.ones((8, 128), F32), wide, NT, lax.Precision.HIGHEST)
    lead = sums.astype(BF16)
    rest = (sums - lead.astype(F32)).astype(BF16)
    return lead, rest


def to_column(row):
    return jnp.broadcast_to(row, (128, row.shape[1])).T


def call(body, out_shapes, interpret, **kwargs):
    return pl.pallas_call(
        body,
        out_shape=out_shapes,
        compiler_params=pltpu.CompilerParams(vmem_limit_bytes=48 * 1024 * 1024),
        interpret=interpret,
        **kwargs,
    )


def prepare_kernel(
    first_ref, second_ref, gfirst_ref, gsecond_ref, down_ref, up_ref,
    streams_ref, partial_ref, first, gsecond, down, up, downt, sems,
):
    seq = first.shape[0]
    copies = [
        pltpu.make_async_copy(src, dst, sems.at[i])
        for i, (src, dst) in enumerate(
            (
                (down_ref, down),
                (up_ref, up),
                (first_ref, first),
                (gsecond_ref, gsecond),
                (second_ref, streams_ref.at[:seq]),
                (gfirst_ref, streams_ref.at[seq : 2 * seq]),
                (up_ref, streams_ref.at[2 * seq : 2 * seq + RANK]),
            )
        )
    ]
    for copy in copies:
        copy.start()
    copies[0].wait()
    eye = (
        lax.broadcasted_iota(jnp.int32, (128, 128), 0) == lax.broadcasted_iota(jnp.int32, (128, 128), 1)
    ).astype(BF16)
    downt[...] = dot(down[...], eye, TN).astype(BF16)
    last = pltpu.make_async_copy(downt, streams_ref.at[2 * seq + RANK :], sems.at[7])
    last.start()
    for copy in copies[1:4]:
        copy.wait()
    partial_ref[:, :RANK] = dot(first[...], down[...])
    partial_ref[:, RANK:] = dot(gsecond[...], up[...], NT)
    for copy in copies[4:]:
        copy.wait()
    last.wait()


def pack_kernel(place_ref, query_ref, key_ref, value_ref, output_ref, own_ref, one_ref, two_ref, three_ref, sems):
    core, quad = place_ref[0], place_ref[1]
    copies = []

    def copy(src, dst):
        copies.append(pltpu.make_async_copy(src, dst, sems.at[len(copies)]))
        copies[-1].start()

    for k, piece in ((1, one_ref), (2, two_ref), (3, three_ref)):
        yb, zb = lax.div(quad, 2) ^ (k // 2), lax.rem(quad, 2) ^ (k % 2)
        for w, matrix in enumerate((query_ref, key_ref, value_ref)):
            copy(matrix.at[core, yb, :, zb], piece.at[:, :, w * 128 : w * 128 + 128])
        for z in range(4):
            start = (((core * 2 + yb) * 4 + z) * 2 + zb) * 128
            copy(output_ref.at[:, pl.ds(pl.multiple_of(start, 128), 128)], piece.at[z, :, 384:])
    yb, zb = lax.div(quad, 2), lax.rem(quad, 2)
    for w, matrix in enumerate((query_ref, key_ref, value_ref)):
        copy(matrix.at[:, yb, :, zb], own_ref.at[:, :, :, w * 128 : w * 128 + 128])
    for y in range(2):
        for z in range(4):
            start = (((y * 2 + yb) * 4 + z) * 2 + zb) * 128
            copy(output_ref.at[:, pl.ds(pl.multiple_of(start, 128), 128)], own_ref.at[y, z, :, 384:])
    for each in copies:
        each.wait()


PACK_COPIES = 3 * (3 + 4) + 3 + 8


def adapter_kernel(
    sums_ref, first_ref, second_ref, gfirst_ref, gsecond_ref, up_ref, down_ref,
    activation_ref, pre_grad_ref, in_second_ref, first_grad_ref, adapters_ref,
):
    sums = sums_ref[...]
    pre_act = sums[:, :RANK]
    back_sum = pltpu.roll(sums, RANK, 1)[:, :RANK]
    logistic = 1.0 / (1.0 + jnp.exp(-pre_act))
    activation = (pre_act * logistic).astype(BF16)
    pre_grad = (back_sum * (logistic * (1.0 + pre_act * (1.0 - logistic)))).astype(BF16)
    activation_ref[...] = activation
    pre_grad_ref[...] = pre_grad
    in_second_ref[...] = (second_ref[...].astype(F32) - dot(activation, up_ref[...])).astype(BF16)
    first_grad_ref[...] = (gfirst_ref[...].astype(F32) + dot(pre_grad, down_ref[...], NT)).astype(BF16)
    adapters_ref[:RANK] = dot(pre_grad, first_ref[...], TN)
    adapters_ref[RANK:] = dot(activation, gsecond_ref[...], TN)


def project_kernel(
    place_ref, activation_ref, pre_grad_ref, gathered_ref, gain_ref, *refs,
):
    own_ref, here_refs, there_refs, (partial_ref, x_ref, g_ref) = refs[0], refs[1:4], refs[4:7], refs[7:]
    core, quad = place_ref[0], place_ref[1]
    seq = activation_ref.shape[0]
    activation, pre_grad = activation_ref[...], pre_grad_ref[...]
    squares = jnp.zeros((seq, 128), F32)
    for f in range(8):
        y, lanes = f // 4, slice(f % 4 * 128, f % 4 * 128 + 128)
        rows = gathered_ref[f, :seq].astype(F32)
        wide = (rows - dot(activation, gathered_ref[f, 2 * seq : 2 * seq + RANK])).astype(BF16).astype(F32)
        squares = squares + wide * wide
        x_ref[y, :, lanes] = (wide * gain_ref[f : f + 1, :]).astype(BF16)
        rows = gathered_ref[f, seq : 2 * seq].astype(F32)
        g_ref[y, :, lanes] = (rows + dot(pre_grad, gathered_ref[f, 2 * seq + RANK :])).astype(BF16)
    lead, rest = row_sums(squares)
    tail = jnp.concatenate([lead, rest], 0)
    for k in range(4):
        h = quad ^ k
        if k:
            halves = [(core, here_refs[k - 1]), (1 - core, there_refs[k - 1])]
        else:
            halves = [(0, own_ref.at[0]), (1, own_ref.at[1])]
        qkv = jnp.zeros((seq, 384), F32)
        ctx = jnp.zeros((seq, 128), F32)
        for y, piece in halves:
            qkv = qkv + dot(x_ref[y], piece[:, :, :384].reshape(512, 384))
            for z in range(4):
                ctx = ctx + dot(g_ref[y, :, z * 128 : z * 128 + 128], piece[z, :, 384:], NT)
        partial_ref[h, :seq, :384] = qkv.astype(BF16)
        partial_ref[h, :seq, 384:] = ctx.astype(BF16)
        partial_ref[h, seq:, :seq] = tail
        partial_ref[h, seq:, seq:] = jnp.zeros((16, 512 - seq), BF16)


def attention_kernel(width, partial_ref, out_ref, inv_ref):
    seq = inv_ref.shape[0]
    scale = HEAD_DIM ** (-0.5)

    def total(lo, hi):
        rows = partial_ref[0, :seq, lo:hi].astype(F32)
        for s in range(1, 4):
            rows = rows + partial_ref[s, :seq, lo:hi].astype(F32)
        return rows

    square = jnp.zeros((1, seq), F32)
    for s in range(4):
        tail = partial_ref[s, seq:, :seq].astype(F32)
        square = square + tail[:1] + tail[8:9]
    inv = to_column(lax.rsqrt(square / width + EPS))
    inv_ref[...] = inv
    query_wide, key_wide, value_wide = total(0, 128) * inv, total(128, 256) * inv, total(256, 384) * inv
    query, key, value = query_wide.astype(BF16), key_wide.astype(BF16), value_wide.astype(BF16)
    back_ctx = total(384, 512).astype(BF16)
    scores = dot(query, key, NT) * scale
    query_pos = lax.broadcasted_iota(jnp.int32, (seq, seq), 0)
    key_pos = lax.broadcasted_iota(jnp.int32, (seq, seq), 1)
    scores = jnp.where(key_pos <= query_pos, scores, MASKED)
    weights = jnp.exp(scores - jnp.max(scores, axis=1, keepdims=True))
    probs = (weights / jnp.sum(weights, axis=1, keepdims=True)).astype(BF16)
    context = dot(probs, value).astype(BF16)
    value_grad = dot(probs, back_ctx, TN).astype(BF16)
    prob_grad = dot(back_ctx, value, NT)
    prob_wide = probs.astype(F32)
    inner = jnp.sum(prob_grad * prob_wide, axis=1, keepdims=True)
    score_grad = (prob_wide * (prob_grad - inner) * scale).astype(BF16)
    query_grad = dot(score_grad, key).astype(BF16)
    key_grad = dot(score_grad, query, TN).astype(BF16)
    stat = (
        query_grad.astype(F32) * query_wide + key_grad.astype(F32) * key_wide + value_grad.astype(F32) * value_wide
    )
    lead, rest = row_sums(stat)
    tail = jnp.concatenate([lead, rest], 0)
    for s in range(4):
        out_ref[s, :seq, :128] = query_grad
        out_ref[s, :seq, 128:256] = key_grad
        out_ref[s, :seq, 256:384] = value_grad
        out_ref[s, :seq, 384:] = context
        out_ref[s, seq:, :seq] = tail
        out_ref[s, seq:, seq:] = jnp.zeros((16, 512 - seq), BF16)


def spread_kernel(place_ref, grads_ref, *refs):
    own_ref, here_refs, there_refs, out_ref = refs[0], refs[1:4], refs[4:7], refs[7]
    core, quad = place_ref[0], place_ref[1]
    seq = grads_ref.shape[1] - 16
    stat = jnp.zeros((8, seq), F32)
    for h in range(4):
        tail = grads_ref[h, seq:, :seq].astype(F32)
        stat = stat + tail[:8] + tail[8:]
    lead = stat.astype(BF16)
    rest = (stat - lead.astype(F32)).astype(BF16)
    tail = jnp.concatenate([lead, rest], 0)
    for other in range(2):
        y = core ^ other
        norm = jnp.zeros((seq, 512), F32)
        attn = [jnp.zeros((seq, 128), F32)] * 4
        for k in range(4):
            h = quad ^ k
            piece = (there_refs if other else here_refs)[k - 1] if k else own_ref.at[y]
            norm = norm + dot(grads_ref[h, :seq, :384], piece[:, :, :384].reshape(512, 384), NT)
            context = grads_ref[h, :seq, 384:]
            attn = [attn[z] + dot(context, piece[z, :, 384:]) for z in range(4)]
        for z in range(4):
            out_ref[y * 4 + z, :seq] = attn[z].astype(BF16)
            out_ref[y * 4 + z, seq : 2 * seq] = norm[:, z * 128 : z * 128 + 128].astype(BF16)
            out_ref[y * 4 + z, 2 * seq : 2 * seq + 16] = tail[:, :128]
            out_ref[y * 4 + z, 2 * seq + 16 :] = tail[:, 128:]


def finish_kernel(width, terms_ref, inv_ref, first_ref, in_second_ref, gsecond_ref, gain_ref, in_first_ref, second_grad_ref):
    seq = first_ref.shape[0]
    total = terms_ref[0].astype(F32)
    for s in range(1, 8):
        total = total + terms_ref[s].astype(F32)
    in_first_ref[...] = (first_ref[...].astype(F32) - total[:seq]).astype(BF16)
    halves = [total[2 * seq + i : 2 * seq + i + 1] + total[2 * seq + i + 8 : 2 * seq + i + 9] for i in (0, 16)]
    stat = jnp.concatenate([to_column(half) for half in halves], 0) / width
    inv = inv_ref[...]
    gain_grad = gain_ref[...] * total[seq : 2 * seq]
    second = in_second_ref[...].astype(F32)
    second_grad_ref[...] = (gsecond_ref[...].astype(F32) + inv * (gain_grad - second * stat * inv)).astype(BF16)


def shards(
    interpret,
    out_first,
    out_second,
    grad_first,
    grad_second,
    norm_gain,
    query_proj,
    key_proj,
    value_proj,
    output_proj,
    adapter_down,
    adapter_up,
):
    seq = out_first.shape[0]
    width = query_proj.shape[0]
    shape = jax.ShapeDtypeStruct
    core, quad = lax.axis_index("c"), lax.axis_index(QUAD)
    place = jnp.stack([core, quad]).astype(jnp.int32)
    smem, anywhere, vmem = (pl.BlockSpec(memory_space=m) for m in (pltpu.SMEM, pl.ANY, pltpu.VMEM))

    streams, partial = call(
        prepare_kernel,
        (shape((2 * seq + 2 * RANK, 128), BF16), shape((seq, 128), F32)),
        interpret,
        in_specs=[anywhere] * 6,
        out_specs=(anywhere, vmem),
        scratch_shapes=[
            pltpu.VMEM((seq, 128), BF16),
            pltpu.VMEM((seq, 128), BF16),
            pltpu.VMEM((128, RANK), BF16),
            pltpu.VMEM((RANK, 128), BF16),
            pltpu.VMEM((RANK, 128), BF16),
            pltpu.SemaphoreType.DMA((8,)),
        ],
    )(out_first, out_second, grad_first, grad_second, adapter_down, adapter_up)
    gathered = lax.all_gather(streams, OCTET, axis=0)
    terms = lax.all_to_all(partial.reshape(32, seq // 32, 128), PLANE, 0, 0)
    mine = jnp.sum(terms, 0)
    sums = lax.all_to_all(jnp.broadcast_to(mine[None], terms.shape), PLANE, 0, 0).reshape(seq, 128)

    tiles = (2, 2, 4, 2, 128, 128)
    own, *sent = call(
        pack_kernel,
        (shape((2, 4, 128, 512), BF16),) + (shape((4, 128, 512), BF16),) * 3,
        interpret,
        in_specs=[smem] + [anywhere] * 4,
        out_specs=(anywhere,) * 4,
        scratch_shapes=[pltpu.SemaphoreType.DMA((PACK_COPIES,))],
    )(place, query_proj.reshape(tiles), key_proj.reshape(tiles), value_proj.reshape(tiles), output_proj)
    here = [lax.ppermute(piece, QUAD, [(i, i ^ k) for i in range(4)]) for k, piece in enumerate(sent, 1)]
    there = [lax.ppermute(piece, "c", [(0, 1), (1, 0)]) for piece in here]
    weights = (own, *here, *there)

    gain = norm_gain.astype(F32).reshape(2, 2, 4, 2, 128)
    gain = lax.dynamic_index_in_dim(gain, lax.axis_index("yb"), 1, False)
    gain = lax.dynamic_index_in_dim(gain, lax.axis_index("zb"), 2, False).reshape(8, 128)
    gain_local = lax.dynamic_slice_in_dim(gain, lax.axis_index(OCTET), 1)

    activation, pre_grad, in_second, first_grad, adapters = call(
        adapter_kernel,
        (
            shape((seq, RANK), BF16),
            shape((seq, RANK), BF16),
            shape((seq, 128), BF16),
            shape((seq, 128), BF16),
            shape((2 * RANK, 128), F32),
        ),
        interpret,
    )(sums, out_first, out_second, grad_first, grad_second, adapter_up, adapter_down)
    adapter_grads = jnp.sum(lax.all_gather(adapters, SEQS, axis=0), 0)

    projected = call(
        project_kernel,
        shape((4, seq + 16, 512), BF16),
        interpret,
        in_specs=[smem] + [vmem] * 11,
        scratch_shapes=[pltpu.VMEM((2, seq, 512), BF16), pltpu.VMEM((2, seq, 512), BF16)],
    )(place, activation, pre_grad, gathered, gain, *weights)
    projected = lax.all_to_all(projected, QUAD, 0, 0)
    grads, inv_rms = call(
        functools.partial(attention_kernel, width),
        (shape((4, seq + 16, 512), BF16), shape((seq, 128), F32)),
        interpret,
    )(projected)
    grads = lax.all_to_all(grads, QUAD, 0, 0)
    outward = call(
        spread_kernel,
        shape((8, 2 * seq + 32, 128), BF16),
        interpret,
        in_specs=[smem] + [vmem] * 8,
    )(place, grads, *weights)
    inward = lax.all_to_all(outward, OCTET, 0, 0)
    in_first, second_grad = call(
        functools.partial(finish_kernel, width),
        (shape((seq, 128), BF16), shape((seq, 128), BF16)),
        interpret,
    )(inward, inv_rms, out_first, in_second, grad_second, gain_local)
    return (in_first, in_second, first_grad, second_grad, adapter_grads[:RANK].T, adapter_grads[RANK:])


def over(mesh, interpret=False):
    rows, columns = P(SEQS, PLANE), P(None, PLANE)
    return jax.shard_map(
        functools.partial(shards, interpret),
        mesh=mesh,
        in_specs=(rows, rows, rows, rows, P(), columns, columns, columns, P(PLANE, None), P(PLANE, None), columns),
        out_specs=(rows, rows, rows, rows, P(PLANE, None), columns),
        check_vma=False,
    )


def solution(mesh):
    devices = mesh.devices.reshape(2, 4, 2, 2, 2, 4, 2)
    return over(Mesh(devices, SEQS + PLANE))
```

```python
import functools

import jax
import jax.numpy as jnp
from jax import lax
from jax.experimental import pallas as pl
from jax.experimental.pallas import tpu as pltpu
from jax.sharding import Mesh, PartitionSpec as P

HEAD_DIM = 128
RANK = 64
EPS = 1e-05
MASKED = -1e30

QUAD = ("yb", "zb")
OCTET = ("ya", "za")
PLANE = ("ya", "yb", "za", "zb")
SEQS = ("yh", "x", "c")
F32 = jnp.float32
BF16 = jnp.bfloat16


def dot(a, b, dims=((1,), (0,)), precision=None):
    return lax.dot_general(a, b, (dims, ((), ())), preferred_element_type=F32, precision=precision)


NT = ((1,), (1,))
TN = ((0,), (0,))


def row_sums(wide):
    sums = dot(jnp.ones((8, 128), F32), wide, NT, lax.Precision.HIGHEST)
    lead = sums.astype(BF16)
    rest = (sums - lead.astype(F32)).astype(BF16)
    return lead, rest


def to_column(row):
    return jnp.broadcast_to(row, (128, row.shape[1])).T


def call(body, out_shapes, interpret, **kwargs):
    return pl.pallas_call(
        body,
        out_shape=out_shapes,
        compiler_params=pltpu.CompilerParams(vmem_limit_bytes=48 * 1024 * 1024),
        interpret=interpret,
        **kwargs,
    )


def fetch(pairs, sems):
    copies = [pltpu.make_async_copy(src, dst, sems.at[i]) for i, (src, dst) in enumerate(pairs)]
    for copy in copies:
        copy.start()
    return copies


def prepare_kernel(
    first_ref, second_ref, gfirst_ref, gsecond_ref, downt_ref, up_ref,
    streams_ref, partial_ref, first, gsecond, downt, up, sems,
):
    seq = first.shape[0]
    copies = fetch(
        (
            (second_ref, streams_ref.at[:seq]),
            (gfirst_ref, streams_ref.at[seq : 2 * seq]),
            (up_ref, streams_ref.at[2 * seq : 2 * seq + RANK]),
            (downt_ref, streams_ref.at[2 * seq + RANK :]),
            (downt_ref, downt),
            (up_ref, up),
            (first_ref, first),
            (gsecond_ref, gsecond),
        ),
        sems,
    )
    for copy in copies[4:]:
        copy.wait()
    partial_ref[:, :RANK] = dot(first[...], downt[...], NT)
    partial_ref[:, RANK:] = dot(gsecond[...], up[...], NT)
    for copy in copies[:4]:
        copy.wait()


def pack_kernel(place_ref, query_ref, key_ref, value_ref, output_ref, own_ref, one_ref, two_ref, three_ref, sems):
    core, quad, plane = place_ref[0], place_ref[1], place_ref[2]
    copies = []

    def copy(src, dst):
        copies.append(pltpu.make_async_copy(src, dst, sems.at[len(copies)]))
        copies[-1].start()

    for k, piece in ((1, one_ref), (2, two_ref), (3, three_ref)):
        yb, zb = lax.div(quad, 2) ^ (k // 2), lax.rem(quad, 2) ^ (k % 2)
        for w, matrix in enumerate((query_ref, key_ref, value_ref)):
            copy(matrix.at[core, yb, plane, zb], piece.at[:, w * 128 : w * 128 + 128])
        start = (((core * 2 + yb) * 4 + plane) * 2 + zb) * 128
        copy(output_ref.at[:, pl.ds(pl.multiple_of(start, 128), 128)], piece.at[:, 384:])
    yb, zb = lax.div(quad, 2), lax.rem(quad, 2)
    for w, matrix in enumerate((query_ref, key_ref, value_ref)):
        copy(matrix.at[:, yb, :, zb], own_ref.at[:, :, :, w * 128 : w * 128 + 128])
    for y in range(2):
        for z in range(4):
            start = (((y * 2 + yb) * 4 + z) * 2 + zb) * 128
            copy(output_ref.at[:, pl.ds(pl.multiple_of(start, 128), 128)], own_ref.at[y, z, :, 384:])
    for each in copies:
        each.wait()


PACK_COPIES = 3 * (3 + 1) + 3 + 8


def add_up_kernel(terms_ref, out_ref):
    total = jnp.sum(terms_ref[...], 0)
    for i in range(out_ref.shape[0]):
        out_ref[i] = total


def adapter_kernel(
    sums_ref, first_ref, second_ref, gfirst_ref, gsecond_ref, up_ref, downt_ref,
    activation_ref, pre_grad_ref, in_second_ref, first_grad_ref, adapters_ref,
    first, second, gfirst, gsecond, up, downt, sems,
):
    copies = fetch(
        (
            (up_ref, up),
            (downt_ref, downt),
            (second_ref, second),
            (gfirst_ref, gfirst),
            (first_ref, first),
            (gsecond_ref, gsecond),
        ),
        sems,
    )
    sums = sums_ref[...]
    pre_act = sums[:, :RANK]
    back_sum = pltpu.roll(sums, RANK, 1)[:, :RANK]
    logistic = 1.0 / (1.0 + jnp.exp(-pre_act))
    activation = (pre_act * logistic).astype(BF16)
    pre_grad = (back_sum * (logistic * (1.0 + pre_act * (1.0 - logistic)))).astype(BF16)
    activation_ref[...] = activation
    pre_grad_ref[...] = pre_grad
    for copy in copies:
        copy.wait()
    in_second_ref[...] = (second[...].astype(F32) - dot(activation, up[...])).astype(BF16)
    first_grad_ref[...] = (gfirst[...].astype(F32) + dot(pre_grad, downt[...])).astype(BF16)
    adapters_ref[:RANK] = dot(pre_grad, first[...], TN)
    adapters_ref[RANK:] = dot(activation, gsecond[...], TN)


def pieces_of(place_ref, refs):
    own_ref, here_refs, there_refs = refs[0], refs[1:5], refs[5:9]
    core, plane = place_ref[0], place_ref[2]
    tiles = []
    for side, held in enumerate((here_refs, there_refs)):
        for step in range(4):
            y, z = core ^ side, lax.rem(plane + 4 - step, 4)

            def read(k, columns, y=y, z=z, ref=held[step]):
                return ref[k - 1, :, columns] if k else own_ref[y, z, :, columns]

            tiles.append((y * 4 + z, read))
    return tiles


QKV, OUT = slice(0, 384), slice(384, 512)


def project_kernel(
    place_ref, activation_ref, pre_grad_ref, gathered_ref, gain_ref, adapters_ref, arrived_ref, *refs,
):
    partial_ref, adapters_out_ref, x_ref, g_ref = refs[9:]
    quad = place_ref[1]
    seq = activation_ref.shape[0]
    activation, pre_grad = activation_ref[...], pre_grad_ref[...]
    squares = jnp.zeros((seq, 128), F32)
    for f in range(8):
        rows = gathered_ref[f, :seq].astype(F32)
        wide = (rows - dot(activation, gathered_ref[f, 2 * seq : 2 * seq + RANK])).astype(BF16).astype(F32)
        squares = squares + wide * wide
        x_ref[f] = (wide * gain_ref[f : f + 1, :]).astype(BF16)
        rows = gathered_ref[f, seq : 2 * seq].astype(F32)
        g_ref[f] = (rows + dot(pre_grad, gathered_ref[f, 2 * seq + RANK :])).astype(BF16)
    lead, rest = row_sums(squares)
    tail = jnp.concatenate([lead, rest], 0)
    tiles = pieces_of(place_ref, refs[:9])
    for k in range(4):
        h = quad ^ k
        qkv = jnp.zeros((seq, 384), F32)
        ctx = jnp.zeros((seq, 128), F32)
        for f, read in tiles:
            qkv = qkv + dot(x_ref[f], read(k, QKV))
            ctx = ctx + dot(g_ref[f], read(k, OUT), NT)
        partial_ref[h, :seq, :384] = qkv.astype(BF16)
        partial_ref[h, :seq, 384:] = ctx.astype(BF16)
        partial_ref[h, seq:, :seq] = tail
        partial_ref[h, seq:, seq:] = jnp.zeros((16, 512 - seq), BF16)
    adapters_out_ref[...] = adapters_ref[...] + arrived_ref[...]


def attention_kernel(width, partial_ref, adapters_ref, arrived_ref, out_ref, inv_ref, adapters_out_ref):
    adapters_out_ref[...] = adapters_ref[...] + arrived_ref[...]
    seq = inv_ref.shape[0]
    scale = HEAD_DIM ** (-0.5)

    def total(lo, hi):
        rows = partial_ref[0, :seq, lo:hi].astype(F32)
        for s in range(1, 4):
            rows = rows + partial_ref[s, :seq, lo:hi].astype(F32)
        return rows

    square = jnp.zeros((1, seq), F32)
    for s in range(4):
        tail = partial_ref[s, seq:, :seq].astype(F32)
        square = square + tail[:1] + tail[8:9]
    inv = to_column(lax.rsqrt(square / width + EPS))
    inv_ref[...] = inv
    query_wide, key_wide, value_wide = total(0, 128) * inv, total(128, 256) * inv, total(256, 384) * inv
    query, key, value = query_wide.astype(BF16), key_wide.astype(BF16), value_wide.astype(BF16)
    back_ctx = total(384, 512).astype(BF16)
    scores = dot(query, key, NT) * scale
    query_pos = lax.broadcasted_iota(jnp.int32, (seq, seq), 0)
    key_pos = lax.broadcasted_iota(jnp.int32, (seq, seq), 1)
    scores = jnp.where(key_pos <= query_pos, scores, MASKED)
    weights = jnp.exp(scores - jnp.max(scores, axis=1, keepdims=True))
    probs = (weights / jnp.sum(weights, axis=1, keepdims=True)).astype(BF16)
    context = dot(probs, value).astype(BF16)
    value_grad = dot(probs, back_ctx, TN).astype(BF16)
    prob_grad = dot(back_ctx, value, NT)
    prob_wide = probs.astype(F32)
    inner = jnp.sum(prob_grad * prob_wide, axis=1, keepdims=True)
    score_grad = (prob_wide * (prob_grad - inner) * scale).astype(BF16)
    query_grad = dot(score_grad, key).astype(BF16)
    key_grad = dot(score_grad, query, TN).astype(BF16)
    stat = (
        query_grad.astype(F32) * query_wide + key_grad.astype(F32) * key_wide + value_grad.astype(F32) * value_wide
    )
    lead, rest = row_sums(stat)
    tail = jnp.concatenate([lead, rest], 0)
    for s in range(4):
        out_ref[s, :seq, :128] = query_grad
        out_ref[s, :seq, 128:256] = key_grad
        out_ref[s, :seq, 256:384] = value_grad
        out_ref[s, :seq, 384:] = context
        out_ref[s, seq:, :seq] = tail
        out_ref[s, seq:, seq:] = jnp.zeros((16, 512 - seq), BF16)


def spread_kernel(place_ref, grads_ref, adapters_ref, arrived_ref, *refs):
    out_ref, adapters_out_ref = refs[9:]
    adapters_out_ref[...] = adapters_ref[...] + arrived_ref[...]
    quad = place_ref[1]
    seq = grads_ref.shape[1] - 16
    stat = jnp.zeros((8, seq), F32)
    for h in range(4):
        tail = grads_ref[h, seq:, :seq].astype(F32)
        stat = stat + tail[:8] + tail[8:]
    lead = stat.astype(BF16)
    rest = (stat - lead.astype(F32)).astype(BF16)
    tail = jnp.concatenate([lead, rest], 0)
    for f, read in pieces_of(place_ref, refs[:9]):
        norm = jnp.zeros((seq, 128), F32)
        attn = jnp.zeros((seq, 128), F32)
        for k in range(4):
            h = quad ^ k
            norm = norm + dot(grads_ref[h, :seq, QKV], read(k, QKV), NT)
            attn = attn + dot(grads_ref[h, :seq, OUT], read(k, OUT))
        out_ref[f, :seq] = attn.astype(BF16)
        out_ref[f, seq : 2 * seq] = norm.astype(BF16)
        out_ref[f, 2 * seq : 2 * seq + 16] = tail[:, :128]
        out_ref[f, 2 * seq + 16 :] = tail[:, 128:]


def finish_kernel(
    width, terms_ref, inv_ref, first_ref, in_second_ref, gsecond_ref, gain_ref, adapters_ref, arrived_ref,
    in_first_ref, second_grad_ref, down_grad_ref, up_grad_ref,
):
    down_grad_ref[...] = adapters_ref[:RANK] + arrived_ref[:RANK]
    up_grad_ref[...] = adapters_ref[RANK:] + arrived_ref[RANK:]
    seq = first_ref.shape[0]
    total = terms_ref[0].astype(F32)
    for s in range(1, 8):
        total = total + terms_ref[s].astype(F32)
    in_first_ref[...] = (first_ref[...].astype(F32) - total[:seq]).astype(BF16)
    halves = [total[2 * seq + i : 2 * seq + i + 1] + total[2 * seq + i + 8 : 2 * seq + i + 9] for i in (0, 16)]
    stat = jnp.concatenate([to_column(half) for half in halves], 0) / width
    inv = inv_ref[...]
    gain_grad = gain_ref[...] * total[seq : 2 * seq]
    second = in_second_ref[...].astype(F32)
    second_grad_ref[...] = (gsecond_ref[...].astype(F32) + inv * (gain_grad - second * stat * inv)).astype(BF16)


def shards(
    interpret,
    out_first,
    out_second,
    grad_first,
    grad_second,
    norm_gain,
    query_proj,
    key_proj,
    value_proj,
    output_proj,
    adapter_down,
    adapter_up,
):
    seq = out_first.shape[0]
    width = query_proj.shape[0]
    shape = jax.ShapeDtypeStruct
    core, quad, plane = lax.axis_index("c"), lax.axis_index(QUAD), lax.axis_index("x")
    place = jnp.stack([core, quad, plane]).astype(jnp.int32)
    smem, hbm, vmem = (pl.BlockSpec(memory_space=m) for m in (pltpu.SMEM, pltpu.HBM, pltpu.VMEM))
    down_t = adapter_down.T
    streams_shape, block, grads_block = shape((2 * seq + 2 * RANK, 128), BF16), shape((seq, 128), BF16), shape((2 * RANK, 128), F32)
    local_scratch = [pltpu.VMEM((seq, 128), BF16)] * 4
    adapter_scratch = [pltpu.VMEM((RANK, 128), BF16)] * 2

    def swap(array, axis, bit=1):
        size = 4 if axis in ("x", QUAD) else 2
        return lax.ppermute(array, axis, [(i, i ^ bit) for i in range(size)])

    streams, partial = call(
        prepare_kernel,
        (streams_shape, shape((seq, 128), F32)),
        interpret,
        in_specs=[hbm] * 6,
        out_specs=(hbm, vmem),
        scratch_shapes=[*local_scratch[:2], *adapter_scratch, pltpu.SemaphoreType.DMA((8,))],
    )(out_first, out_second, grad_first, grad_second, down_t, adapter_up)
    gathered = lax.all_gather(streams, OCTET, axis=0)

    tiles = (2, 2, 4, 2, 128, 128)
    own, *sent = call(
        pack_kernel,
        (shape((2, 4, 128, 512), BF16),) + (shape((128, 512), BF16),) * 3,
        interpret,
        in_specs=[smem] + [hbm] * 4,
        scratch_shapes=[pltpu.SemaphoreType.DMA((PACK_COPIES,))],
        out_specs=(hbm,) + (vmem,) * 3,
    )(place, query_proj.reshape(tiles), key_proj.reshape(tiles), value_proj.reshape(tiles), output_proj)
    fetched = jnp.stack([swap(piece, QUAD, k) for k, piece in enumerate(sent, 1)])

    terms = lax.all_to_all(partial.reshape(32, seq // 32, 128), PLANE, 0, 0)
    mine = call(add_up_kernel, shape(terms.shape, F32), interpret)(terms)
    fetched, _ = lax.optimization_barrier((fetched, mine))
    here = [fetched] + [lax.ppermute(fetched, "x", [(i, (i + s) % 4) for i in range(4)]) for s in (1, 2, 3)]
    sums = lax.all_to_all(mine, PLANE, 0, 0).reshape(seq, 128)
    here = [lax.optimization_barrier((piece, sums))[0] for piece in here]
    weights = (own, *here, *(swap(piece, "c") for piece in here))

    gain = norm_gain.astype(F32).reshape(2, 2, 4, 2, 128)
    gain = lax.dynamic_index_in_dim(gain, lax.axis_index("yb"), 1, False)
    gain = lax.dynamic_index_in_dim(gain, lax.axis_index("zb"), 2, False).reshape(8, 128)
    gain_local = lax.dynamic_slice_in_dim(gain, lax.axis_index(OCTET), 1)

    activation, pre_grad, in_second, first_grad, adapters = call(
        adapter_kernel,
        (shape((seq, RANK), BF16), shape((seq, RANK), BF16), block, block, grads_block),
        interpret,
        in_specs=[vmem] + [hbm] * 6,
        scratch_shapes=[*local_scratch, *adapter_scratch, pltpu.SemaphoreType.DMA((6,))],
    )(sums, out_first, out_second, grad_first, grad_second, adapter_up, down_t)

    quads = shape((4, seq + 16, 512), BF16)
    projected, adapters = call(
        project_kernel,
        (quads, grads_block),
        interpret,
        in_specs=[smem] + [vmem] * 15,
        scratch_shapes=[pltpu.VMEM((8, seq, 128), BF16), pltpu.VMEM((8, seq, 128), BF16)],
    )(place, activation, pre_grad, gathered, gain, adapters, swap(adapters, "c"), *weights)
    projected = lax.all_to_all(projected, QUAD, 0, 0)
    grads, inv_rms, adapters = call(
        functools.partial(attention_kernel, width), (quads, shape((seq, 128), F32), grads_block), interpret
    )(projected, adapters, swap(adapters, "x", 1))
    grads = lax.all_to_all(grads, QUAD, 0, 0)
    outward, adapters = call(
        spread_kernel,
        (shape((8, 2 * seq + 32, 128), BF16), grads_block),
        interpret,
        in_specs=[smem] + [vmem] * 12,
    )(place, grads, adapters, swap(adapters, "x", 2), *weights)
    inward = lax.all_to_all(outward, OCTET, 0, 0)
    in_first, second_grad, down_grad, up_grad = call(
        functools.partial(finish_kernel, width),
        (block, block, shape((RANK, 128), F32), shape((RANK, 128), F32)),
        interpret,
    )(inward, inv_rms, out_first, in_second, grad_second, gain_local, adapters, swap(adapters, "yh"))
    return (in_first, in_second, first_grad, second_grad, down_grad.T, up_grad)


def over(mesh, interpret=False):
    rows, columns = P(SEQS, PLANE), P(None, PLANE)
    return jax.shard_map(
        functools.partial(shards, interpret),
        mesh=mesh,
        in_specs=(rows, rows, rows, rows, P(), columns, columns, columns, P(PLANE, None), P(PLANE, None), columns),
        out_specs=(rows, rows, rows, rows, P(PLANE, None), columns),
        check_vma=False,
    )


def solution(mesh):
    devices = mesh.devices.reshape(2, 4, 2, 2, 2, 4, 2)
    return over(Mesh(devices, SEQS + PLANE))
```

```python
import functools

import jax
import jax.numpy as jnp
from jax import lax
from jax.experimental import pallas as pl
from jax.experimental.pallas import tpu as pltpu
from jax.sharding import Mesh, PartitionSpec as P

HEAD_DIM = 128
RANK = 64
EPS = 1e-05
MASKED = -1e30

QUAD = ("yb", "zb")
OCTET = ("ya", "za")
PLANE = ("ya", "yb", "za", "zb")
SEQS = ("yh", "x", "c")
F32 = jnp.float32
BF16 = jnp.bfloat16


def dot(a, b, dims=((1,), (0,)), precision=None):
    return lax.dot_general(a, b, (dims, ((), ())), preferred_element_type=F32, precision=precision)


NT = ((1,), (1,))
TN = ((0,), (0,))


def row_sums(wide):
    sums = dot(jnp.ones((8, 128), F32), wide, NT, lax.Precision.HIGHEST)
    lead = sums.astype(BF16)
    rest = (sums - lead.astype(F32)).astype(BF16)
    return lead, rest


def to_column(row):
    return jnp.broadcast_to(row, (128, row.shape[1])).T


def call(body, out_shapes, interpret, vmem=16, **kwargs):
    return pl.pallas_call(
        body,
        out_shape=out_shapes,
        compiler_params=pltpu.CompilerParams(vmem_limit_bytes=vmem * 1024 * 1024),
        interpret=interpret,
        **kwargs,
    )


def fetch(pairs, sems):
    copies = [pltpu.make_async_copy(src, dst, sems.at[i]) for i, (src, dst) in enumerate(pairs)]
    for copy in copies:
        copy.start()
    return copies


def bottleneck_kernel(first_ref, gsecond_ref, downt_ref, up_ref, partial_ref, first, gsecond, downt, up, sems):
    copies = fetch(((downt_ref, downt), (up_ref, up), (first_ref, first), (gsecond_ref, gsecond)), sems)
    for copy in copies:
        copy.wait()
    partial_ref[:, :RANK] = dot(first[...], downt[...], NT)
    partial_ref[:, RANK:] = dot(gsecond[...], up[...], NT)


def pack_kernel(place_ref, query_ref, key_ref, value_ref, output_ref, out_ref, sems):
    core, plane = place_ref[0], place_ref[1]
    pairs = []
    for place in range(4):
        yb, zb = place // 2, place % 2
        for w, matrix in enumerate((query_ref, key_ref, value_ref)):
            pairs.append((matrix.at[core, yb, plane, zb], out_ref.at[place, :, w * 128 : w * 128 + 128]))
        start = (((core * 2 + yb) * 4 + plane) * 2 + zb) * 128
        pairs.append((output_ref.at[:, pl.ds(pl.multiple_of(start, 128), 128)], out_ref.at[place, :, OUT]))
    for copy in fetch(pairs, sems):
        copy.wait()


def add_up_kernel(terms_ref, out_ref):
    total = jnp.sum(terms_ref[...], 0)
    for i in range(out_ref.shape[0]):
        out_ref[i] = total


def adapter_kernel(
    sums_ref, first_ref, second_ref, gfirst_ref, gsecond_ref, up_ref, downt_ref,
    shared_ref, in_second_ref, first_grad_ref, adapters_ref,
    first, second, gfirst, gsecond, up, downt, sems,
):
    seq = first.shape[0]
    copies = fetch(
        (
            (up_ref, up),
            (downt_ref, downt),
            (second_ref, second),
            (gfirst_ref, gfirst),
            (first_ref, first),
            (gsecond_ref, gsecond),
        ),
        sems,
    )
    sums = sums_ref[...]
    pre_act = sums[:, :RANK]
    back_sum = pltpu.roll(sums, RANK, 1)[:, :RANK]
    logistic = 1.0 / (1.0 + jnp.exp(-pre_act))
    activation = (pre_act * logistic).astype(BF16)
    pre_grad = (back_sum * (logistic * (1.0 + pre_act * (1.0 - logistic)))).astype(BF16)
    for copy in copies:
        copy.wait()
    in_second = (second[...].astype(F32) - dot(activation, up[...])).astype(BF16)
    first_grad = (gfirst[...].astype(F32) + dot(pre_grad, downt[...])).astype(BF16)
    in_second_ref[...] = in_second
    first_grad_ref[...] = first_grad
    for s in range(8):
        shared_ref[s, :seq] = in_second
        shared_ref[s, seq:] = first_grad
    adapters_ref[:RANK] = dot(pre_grad, first[...], TN)
    adapters_ref[RANK:] = dot(activation, gsecond[...], TN)


def tiles_of(place_ref, refs):
    core, plane = place_ref[0], place_ref[1]
    return [((core ^ (i // 4)) * 4 + lax.rem(plane + 4 - i % 4, 4), ref) for i, ref in enumerate(refs)]


QKV, OUT = slice(0, 384), slice(384, 512)


def project_kernel(place_ref, gathered_ref, gain_ref, *refs):
    partial_ref, x_ref = refs[8:]
    seq = x_ref.shape[1]
    squares = jnp.zeros((seq, 128), F32)
    for f in range(8):
        wide = gathered_ref[f, :seq].astype(F32)
        squares = squares + wide * wide
        x_ref[f] = (wide * gain_ref[f : f + 1, :]).astype(BF16)
    lead, rest = row_sums(squares)
    tail = jnp.concatenate([lead, rest], 0)
    tiles = tiles_of(place_ref, refs[:8])
    for h in range(4):
        qkv = jnp.zeros((seq, 384), F32)
        ctx = jnp.zeros((seq, 128), F32)
        for f, ref in tiles:
            qkv = qkv + dot(x_ref[f], ref[h, :, QKV])
            ctx = ctx + dot(gathered_ref[f, seq:], ref[h, :, OUT], NT)
        partial_ref[h, :seq, QKV] = qkv.astype(BF16)
        partial_ref[h, :seq, OUT] = ctx.astype(BF16)
        partial_ref[h, seq:, :seq] = tail
        partial_ref[h, seq:, seq:] = jnp.zeros((16, 512 - seq), BF16)


def attention_kernel(width, partial_ref, adapters_ref, arrived_ref, out_ref, inv_ref, adapters_out_ref):
    adapters_out_ref[...] = adapters_ref[...] + arrived_ref[...]
    seq = inv_ref.shape[0]
    scale = HEAD_DIM ** (-0.5)

    def total(lo, hi):
        rows = partial_ref[0, :seq, lo:hi].astype(F32)
        for s in range(1, 4):
            rows = rows + partial_ref[s, :seq, lo:hi].astype(F32)
        return rows

    square = jnp.zeros((1, seq), F32)
    for s in range(4):
        tail = partial_ref[s, seq:, :seq].astype(F32)
        square = square + tail[:1] + tail[8:9]
    inv = to_column(lax.rsqrt(square / width + EPS))
    inv_ref[...] = inv
    query_wide, key_wide, value_wide = total(0, 128) * inv, total(128, 256) * inv, total(256, 384) * inv
    query, key, value = query_wide.astype(BF16), key_wide.astype(BF16), value_wide.astype(BF16)
    back_ctx = total(384, 512).astype(BF16)
    scores = dot(query, key, NT) * scale
    query_pos = lax.broadcasted_iota(jnp.int32, (seq, seq), 0)
    key_pos = lax.broadcasted_iota(jnp.int32, (seq, seq), 1)
    scores = jnp.where(key_pos <= query_pos, scores, MASKED)
    weights = jnp.exp(scores - jnp.max(scores, axis=1, keepdims=True))
    probs = (weights / jnp.sum(weights, axis=1, keepdims=True)).astype(BF16)
    context = dot(probs, value).astype(BF16)
    value_grad = dot(probs, back_ctx, TN).astype(BF16)
    prob_grad = dot(back_ctx, value, NT)
    prob_wide = probs.astype(F32)
    inner = jnp.sum(prob_grad * prob_wide, axis=1, keepdims=True)
    score_grad = (prob_wide * (prob_grad - inner) * scale).astype(BF16)
    query_grad = dot(score_grad, key).astype(BF16)
    key_grad = dot(score_grad, query, TN).astype(BF16)
    stat = (
        query_grad.astype(F32) * query_wide + key_grad.astype(F32) * key_wide + value_grad.astype(F32) * value_wide
    )
    lead, rest = row_sums(stat)
    tail = jnp.concatenate([lead, rest], 0)
    for s in range(4):
        out_ref[s, :seq, :128] = query_grad
        out_ref[s, :seq, 128:256] = key_grad
        out_ref[s, :seq, 256:384] = value_grad
        out_ref[s, :seq, 384:] = context
        out_ref[s, seq:, :seq] = tail
        out_ref[s, seq:, seq:] = jnp.zeros((16, 512 - seq), BF16)


def spread_kernel(place_ref, grads_ref, adapters_ref, arrived_ref, *refs):
    out_ref, adapters_out_ref = refs[8:]
    adapters_out_ref[...] = adapters_ref[...] + arrived_ref[...]
    seq = grads_ref.shape[1] - 16
    stat = jnp.zeros((8, seq), F32)
    for h in range(4):
        tail = grads_ref[h, seq:, :seq].astype(F32)
        stat = stat + tail[:8] + tail[8:]
    lead = stat.astype(BF16)
    rest = (stat - lead.astype(F32)).astype(BF16)
    tail = jnp.concatenate([lead, rest], 0)
    for f, ref in tiles_of(place_ref, refs[:8]):
        norm = jnp.zeros((seq, 128), F32)
        attn = jnp.zeros((seq, 128), F32)
        for h in range(4):
            norm = norm + dot(grads_ref[h, :seq, QKV], ref[h, :, QKV], NT)
            attn = attn + dot(grads_ref[h, :seq, OUT], ref[h, :, OUT])
        out_ref[f, :seq] = attn.astype(BF16)
        out_ref[f, seq : 2 * seq] = norm.astype(BF16)
        out_ref[f, 2 * seq : 2 * seq + 16] = tail[:, :128]
        out_ref[f, 2 * seq + 16 :] = tail[:, 128:]


def finish_kernel(
    width, terms_ref, inv_ref, first_ref, in_second_ref, gsecond_ref, gain_ref, in_first_ref, second_grad_ref
):
    seq = first_ref.shape[0]
    total = terms_ref[0].astype(F32)
    for s in range(1, 8):
        total = total + terms_ref[s].astype(F32)
    in_first_ref[...] = (first_ref[...].astype(F32) - total[:seq]).astype(BF16)
    halves = [total[2 * seq + i : 2 * seq + i + 1] + total[2 * seq + i + 8 : 2 * seq + i + 9] for i in (0, 16)]
    stat = jnp.concatenate([to_column(half) for half in halves], 0) / width
    inv = inv_ref[...]
    gain_grad = gain_ref[...] * total[seq : 2 * seq]
    second = in_second_ref[...].astype(F32)
    second_grad_ref[...] = (gsecond_ref[...].astype(F32) + inv * (gain_grad - second * stat * inv)).astype(BF16)


def shards(
    interpret,
    out_first,
    out_second,
    grad_first,
    grad_second,
    norm_gain,
    query_proj,
    key_proj,
    value_proj,
    output_proj,
    adapter_down,
    adapter_up,
):
    seq = out_first.shape[0]
    width = query_proj.shape[0]
    shape = jax.ShapeDtypeStruct
    place = jnp.stack([lax.axis_index("c"), lax.axis_index("x")]).astype(jnp.int32)
    smem, hbm, vmem = (pl.BlockSpec(memory_space=m) for m in (pltpu.SMEM, pltpu.HBM, pltpu.VMEM))
    down_t = adapter_down.T
    block, grads_block = shape((seq, 128), BF16), shape((2 * RANK, 128), F32)
    local_scratch = [pltpu.VMEM((seq, 128), BF16)] * 4
    adapter_scratch = [pltpu.VMEM((RANK, 128), BF16)] * 2

    def swap(array, axis, bit=1):
        return lax.ppermute(array, axis, [(i, i ^ bit) for i in range(4 if axis == "x" else 2)])

    partial = call(
        bottleneck_kernel,
        shape((seq, 128), F32),
        interpret,
        56,
        in_specs=[hbm] * 4,
        scratch_shapes=[*local_scratch[:2], *adapter_scratch, pltpu.SemaphoreType.DMA((4,))],
    )(out_first, grad_second, down_t, adapter_up)
    terms = lax.all_to_all(partial.reshape(32, seq // 32, 128), PLANE, 0, 0)
    mine = call(add_up_kernel, shape(terms.shape, F32), interpret)(terms)

    tiles = (2, 2, 4, 2, 128, 128)
    pieces = call(
        pack_kernel,
        shape((4, 128, 512), BF16),
        interpret,
        56,
        in_specs=[smem] + [hbm] * 4,
        scratch_shapes=[pltpu.SemaphoreType.DMA((16,))],
    )(place, query_proj.reshape(tiles), key_proj.reshape(tiles), value_proj.reshape(tiles), output_proj)
    pieces, _ = lax.optimization_barrier((pieces, mine))
    fetched = lax.all_to_all(pieces, QUAD, 0, 0)
    mine, _ = lax.optimization_barrier((mine, fetched))
    here = [fetched] + [lax.ppermute(fetched, "x", [(i, (i + s) % 4) for i in range(4)]) for s in (1, 2, 3)]
    sums = lax.all_to_all(mine, PLANE, 0, 0).reshape(seq, 128)

    gain = norm_gain.astype(F32).reshape(2, 2, 4, 2, 128)
    gain = lax.dynamic_index_in_dim(gain, lax.axis_index("yb"), 1, False)
    gain = lax.dynamic_index_in_dim(gain, lax.axis_index("zb"), 2, False).reshape(8, 128)
    gain_local = lax.dynamic_slice_in_dim(gain, lax.axis_index(OCTET), 1)

    shared, in_second, first_grad, adapters = call(
        adapter_kernel,
        (shape((8, 2 * seq, 128), BF16), block, block, grads_block),
        interpret,
        in_specs=[vmem] + [hbm] * 6,
        scratch_shapes=[*local_scratch, *adapter_scratch, pltpu.SemaphoreType.DMA((6,))],
    )(sums, out_first, out_second, grad_first, grad_second, adapter_up, down_t)
    gathered = lax.all_to_all(shared, OCTET, 0, 0)
    here = [lax.optimization_barrier((piece, shared))[0] for piece in here]
    weights = (*here, *(swap(piece, "c") for piece in here))

    adapters = adapters + swap(adapters, "yh")
    adapters = adapters + swap(adapters, "x", 2)
    gathered, adapters = lax.optimization_barrier((gathered, adapters))

    quads = shape((4, seq + 16, 512), BF16)
    projected = call(
        project_kernel,
        quads,
        interpret,
        in_specs=[smem] + [vmem] * 10,
        scratch_shapes=[pltpu.VMEM((8, seq, 128), BF16)],
    )(place, gathered, gain, *weights)
    projected = lax.all_to_all(projected, QUAD, 0, 0)
    grads, inv_rms, adapters = call(
        functools.partial(attention_kernel, width), (quads, shape((seq, 128), F32), grads_block), interpret
    )(projected, adapters, swap(adapters, "x", 1))
    grads = lax.all_to_all(grads, QUAD, 0, 0)
    outward, adapters = call(
        spread_kernel,
        (shape((8, 2 * seq + 32, 128), BF16), grads_block),
        interpret,
        in_specs=[smem] + [vmem] * 11,
    )(place, grads, adapters, swap(adapters, "c"), *weights)
    inward = lax.all_to_all(outward, OCTET, 0, 0)
    in_first, second_grad = call(functools.partial(finish_kernel, width), (block, block), interpret)(
        inward, inv_rms, out_first, in_second, grad_second, gain_local
    )
    return (in_first, in_second, first_grad, second_grad, adapters[:RANK].T, adapters[RANK:])


def over(mesh, interpret=False):
    rows, columns = P(SEQS, PLANE), P(None, PLANE)
    return jax.shard_map(
        functools.partial(shards, interpret),
        mesh=mesh,
        in_specs=(rows, rows, rows, rows, P(), columns, columns, columns, P(PLANE, None), P(PLANE, None), columns),
        out_specs=(rows, rows, rows, rows, P(PLANE, None), columns),
        check_vma=False,
    )


def solution(mesh):
    devices = mesh.devices.reshape(2, 4, 2, 2, 2, 4, 2)
    return over(Mesh(devices, SEQS + PLANE))
```

```python
import functools

import jax
import jax.numpy as jnp
from jax import lax
from jax.experimental import pallas as pl
from jax.experimental.pallas import tpu as pltpu
from jax.sharding import Mesh, PartitionSpec as P

HEAD_DIM = 128
RANK = 64
EPS = 1e-05
MASKED = -1e30

QUAD = ("yb", "zb")
OCTET = ("ya", "za")
PLANE = ("ya", "yb", "za", "zb")
SEQS = ("yh", "x", "c")
QKV, OUT = slice(0, 384), slice(384, 512)
F32 = jnp.float32
BF16 = jnp.bfloat16


def dot(a, b, dims=((1,), (0,)), precision=None):
    return lax.dot_general(a, b, (dims, ((), ())), preferred_element_type=F32, precision=precision)


NT = ((1,), (1,))
TN = ((0,), (0,))


def row_sums(wide):
    sums = dot(jnp.ones((8, 128), F32), wide, NT, lax.Precision.HIGHEST)
    lead = sums.astype(BF16)
    rest = (sums - lead.astype(F32)).astype(BF16)
    return lead, rest


def to_column(row):
    return jnp.broadcast_to(row, (128, row.shape[1])).T


def call(body, out_shapes, interpret, vmem=16, **kwargs):
    return pl.pallas_call(
        body,
        out_shape=out_shapes,
        compiler_params=pltpu.CompilerParams(vmem_limit_bytes=vmem * 1024 * 1024),
        interpret=interpret,
        **kwargs,
    )


def fetch(pairs, sems):
    copies = [pltpu.make_async_copy(src, dst, sems.at[i]) for i, (src, dst) in enumerate(pairs)]
    for copy in copies:
        copy.start()
    return copies


def bottleneck_kernel(first_ref, gsecond_ref, downt_ref, up_ref, partial_ref, first, gsecond, downt, up, sems):
    copies = fetch(((downt_ref, downt), (up_ref, up), (first_ref, first), (gsecond_ref, gsecond)), sems)
    for copy in copies:
        copy.wait()
    partial_ref[:, :RANK] = dot(first[...], downt[...], NT)
    partial_ref[:, RANK:] = dot(gsecond[...], up[...], NT)


def pack_kernel(place_ref, query_ref, key_ref, value_ref, output_ref, one_ref, two_ref, three_ref, sems):
    core, quad, plane = place_ref[0], place_ref[1], place_ref[2]
    pairs = []
    for k, piece in ((1, one_ref), (2, two_ref), (3, three_ref)):
        yb, zb = lax.div(quad, 2) ^ (k // 2), lax.rem(quad, 2) ^ (k % 2)
        for w, matrix in enumerate((query_ref, key_ref, value_ref)):
            pairs.append((matrix.at[core, yb, plane, zb], piece.at[:, w * 128 : w * 128 + 128]))
        start = (((core * 2 + yb) * 4 + plane) * 2 + zb) * 128
        pairs.append((output_ref.at[:, pl.ds(pl.multiple_of(start, 128), 128)], piece.at[:, OUT]))
    for copy in fetch(pairs, sems):
        copy.wait()


def assemble_kernel(place_ref, query_ref, key_ref, value_ref, output_ref, *refs):
    pieces, (out_ref, own_out, sems) = refs[:8], refs[8:]
    core, quad, plane = place_ref[0], place_ref[1], place_ref[2]
    yb, zb = lax.div(quad, 2), lax.rem(quad, 2)
    pairs = []
    for y in range(2):
        for w, matrix in enumerate((query_ref, key_ref, value_ref)):
            pairs.append(
                (matrix.at[y, yb, :, zb], out_ref.at[quad, y * 4 : y * 4 + 4, :, w * 128 : w * 128 + 128])
            )
        for z in range(4):
            start = (((y * 2 + yb) * 4 + z) * 2 + zb) * 128
            pairs.append((output_ref.at[:, pl.ds(pl.multiple_of(start, 128), 128)], own_out.at[y * 4 + z]))
    copies = fetch(pairs, sems)
    eye = (
        lax.broadcasted_iota(jnp.int32, (128, 128), 0) == lax.broadcasted_iota(jnp.int32, (128, 128), 1)
    ).astype(BF16)
    for i, ref in enumerate(pieces):
        f = (core ^ (i // 4)) * 4 + lax.rem(plane + 4 - i % 4, 4)
        for k in (1, 2, 3):
            out_ref[quad ^ k, f, :, QKV] = ref[k - 1, :, QKV]
            out_ref[quad ^ k, f, :, OUT] = dot(eye, ref[k - 1, :, OUT], NT).astype(BF16)
    for copy in copies:
        copy.wait()
    for f in range(8):
        out_ref[quad, f, :, OUT] = dot(eye, own_out[f], NT).astype(BF16)


def add_up_kernel(terms_ref, out_ref):
    total = jnp.sum(terms_ref[...], 0)
    for i in range(out_ref.shape[0]):
        out_ref[i] = total


def adapter_kernel(
    sums_ref, first_ref, second_ref, gfirst_ref, gsecond_ref, up_ref, downt_ref,
    shared_ref, in_second_ref, first_grad_ref, adapters_ref,
    first, second, gfirst, gsecond, up, downt, both, sems,
):
    seq = first.shape[0]
    copies = fetch(
        (
            (up_ref, up),
            (downt_ref, downt),
            (second_ref, second),
            (gfirst_ref, gfirst),
            (first_ref, first),
            (gsecond_ref, gsecond),
        ),
        sems,
    )
    sums = sums_ref[...]
    pre_act = sums[:, :RANK]
    back_sum = pltpu.roll(sums, RANK, 1)[:, :RANK]
    logistic = 1.0 / (1.0 + jnp.exp(-pre_act))
    activation = (pre_act * logistic).astype(BF16)
    pre_grad = (back_sum * (logistic * (1.0 + pre_act * (1.0 - logistic)))).astype(BF16)
    for copy in copies:
        copy.wait()
    both[:seq] = (second[...].astype(F32) - dot(activation, up[...])).astype(BF16)
    both[seq:] = (gfirst[...].astype(F32) + dot(pre_grad, downt[...])).astype(BF16)
    copies = fetch([(both, shared_ref.at[s]) for s in range(8)], sems)
    in_second_ref[...] = both[:seq]
    first_grad_ref[...] = both[seq:]
    adapters_ref[:RANK] = dot(pre_grad, first[...], TN)
    adapters_ref[RANK:] = dot(activation, gsecond[...], TN)
    for copy in copies:
        copy.wait()


def project_kernel(gathered_ref, gain_ref, weights_ref, partial_ref, weights, x_ref, g_ref, out, in_sems, out_sems):
    seq = x_ref.shape[0]
    arriving = fetch([(weights_ref.at[h], weights.at[h]) for h in range(4)], in_sems)
    squares = jnp.zeros((seq, 128), F32)
    for f in range(8):
        lanes = slice(f * 128, f * 128 + 128)
        wide = gathered_ref[f, :seq].astype(F32)
        squares = squares + wide * wide
        x_ref[:, lanes] = (wide * gain_ref[f : f + 1, :]).astype(BF16)
        g_ref[:, lanes] = gathered_ref[f, seq:]
    lead, rest = row_sums(squares)
    tail = jnp.concatenate([lead, rest], 0)
    leaving = []
    for h in range(4):
        arriving[h].wait()
        out[h, :seq, QKV] = dot(x_ref[...], weights[h, :, :, QKV].reshape(1024, 384)).astype(BF16)
        out[h, :seq, OUT] = dot(g_ref[...], weights[h, :, :, OUT].reshape(1024, 128)).astype(BF16)
        out[h, seq:, :seq] = tail
        out[h, seq:, seq:] = jnp.zeros((16, 512 - seq), BF16)
        leaving.append(pltpu.make_async_copy(out.at[h], partial_ref.at[h], out_sems.at[h]))
        leaving[-1].start()
    for copy in leaving:
        copy.wait()


def attention_kernel(width, partial_ref, adapters_ref, arrived_ref, grads_ref, inv_ref, adapters_out_ref, out, sems):
    adapters_out_ref[...] = adapters_ref[...] + arrived_ref[...]
    seq = inv_ref.shape[0]
    scale = HEAD_DIM ** (-0.5)

    def total(lo, hi):
        rows = partial_ref[0, :seq, lo:hi].astype(F32)
        for s in range(1, 4):
            rows = rows + partial_ref[s, :seq, lo:hi].astype(F32)
        return rows

    square = jnp.zeros((1, seq), F32)
    for s in range(4):
        tail = partial_ref[s, seq:, :seq].astype(F32)
        square = square + tail[:1] + tail[8:9]
    inv = to_column(lax.rsqrt(square / width + EPS))
    inv_ref[...] = inv
    query_wide, key_wide, value_wide = total(0, 128) * inv, total(128, 256) * inv, total(256, 384) * inv
    query, key, value = query_wide.astype(BF16), key_wide.astype(BF16), value_wide.astype(BF16)
    back_ctx = total(384, 512).astype(BF16)
    scores = dot(query, key, NT) * scale
    query_pos = lax.broadcasted_iota(jnp.int32, (seq, seq), 0)
    key_pos = lax.broadcasted_iota(jnp.int32, (seq, seq), 1)
    scores = jnp.where(key_pos <= query_pos, scores, MASKED)
    weights = jnp.exp(scores - jnp.max(scores, axis=1, keepdims=True))
    probs = (weights / jnp.sum(weights, axis=1, keepdims=True)).astype(BF16)
    context = dot(probs, value).astype(BF16)
    value_grad = dot(probs, back_ctx, TN).astype(BF16)
    prob_grad = dot(back_ctx, value, NT)
    prob_wide = probs.astype(F32)
    inner = jnp.sum(prob_grad * prob_wide, axis=1, keepdims=True)
    score_grad = (prob_wide * (prob_grad - inner) * scale).astype(BF16)
    query_grad = dot(score_grad, key).astype(BF16)
    key_grad = dot(score_grad, query, TN).astype(BF16)
    stat = (
        query_grad.astype(F32) * query_wide + key_grad.astype(F32) * key_wide + value_grad.astype(F32) * value_wide
    )
    lead, rest = row_sums(stat)
    tail = jnp.concatenate([lead, rest], 0)
    out[:seq, :128] = query_grad
    out[:seq, 128:256] = key_grad
    out[:seq, 256:384] = value_grad
    out[:seq, OUT] = context
    out[seq:, :seq] = tail
    out[seq:, seq:] = jnp.zeros((16, 512 - seq), BF16)
    for copy in fetch([(out, grads_ref.at[s]) for s in range(4)], sems):
        copy.wait()


def spread_kernel(
    grads_ref, adapters_ref, arrived_ref, weights_ref, terms_ref, adapters_out_ref,
    weights, norm, attn, out, in_sems, out_sems,
):
    arriving = fetch([(weights_ref.at[h], weights.at[h]) for h in range(4)], in_sems)
    adapters_out_ref[...] = adapters_ref[...] + arrived_ref[...]
    seq = grads_ref.shape[1] - 16
    stat = jnp.zeros((8, seq), F32)
    for h in range(4):
        tail = grads_ref[h, seq:, :seq].astype(F32)
        stat = stat + tail[:8] + tail[8:]
    lead = stat.astype(BF16)
    rest = (stat - lead.astype(F32)).astype(BF16)
    tail = jnp.concatenate([lead, rest], 0)
    for h in range(4):
        arriving[h].wait()
        into_norm = dot(grads_ref[h, :seq, QKV], weights[h, :, :, QKV].reshape(1024, 384), NT)
        into_attn = dot(grads_ref[h, :seq, OUT], weights[h, :, :, OUT].reshape(1024, 128), NT)
        norm[...] = norm[...] + into_norm if h else into_norm
        attn[...] = attn[...] + into_attn if h else into_attn
    leaving = []
    for f in range(8):
        lanes = slice(f * 128, f * 128 + 128)
        out[f, :seq] = attn[:, lanes].astype(BF16)
        out[f, seq : 2 * seq] = norm[:, lanes].astype(BF16)
        out[f, 2 * seq : 2 * seq + 16] = tail[:, :128]
        out[f, 2 * seq + 16 :] = tail[:, 128:]
        leaving.append(pltpu.make_async_copy(out.at[f], terms_ref.at[f], out_sems.at[f]))
        leaving[-1].start()
    for copy in leaving:
        copy.wait()


def finish_kernel(
    width, terms_ref, inv_ref, first_ref, in_second_ref, gsecond_ref, gain_ref, adapters_ref, arrived_ref,
    in_first_ref, second_grad_ref, down_grad_ref, up_grad_ref,
):
    down_grad_ref[...] = adapters_ref[:RANK] + arrived_ref[:RANK]
    up_grad_ref[...] = adapters_ref[RANK:] + arrived_ref[RANK:]
    seq = first_ref.shape[0]
    total = terms_ref[0].astype(F32)
    for s in range(1, 8):
        total = total + terms_ref[s].astype(F32)
    in_first_ref[...] = (first_ref[...].astype(F32) - total[:seq]).astype(BF16)
    halves = [total[2 * seq + i : 2 * seq + i + 1] + total[2 * seq + i + 8 : 2 * seq + i + 9] for i in (0, 16)]
    stat = jnp.concatenate([to_column(half) for half in halves], 0) / width
    inv = inv_ref[...]
    gain_grad = gain_ref[...] * total[seq : 2 * seq]
    second = in_second_ref[...].astype(F32)
    second_grad_ref[...] = (gsecond_ref[...].astype(F32) + inv * (gain_grad - second * stat * inv)).astype(BF16)


def shards(
    interpret,
    out_first,
    out_second,
    grad_first,
    grad_second,
    norm_gain,
    query_proj,
    key_proj,
    value_proj,
    output_proj,
    adapter_down,
    adapter_up,
):
    seq = out_first.shape[0]
    width = query_proj.shape[0]
    shape = jax.ShapeDtypeStruct
    place = jnp.stack([lax.axis_index("c"), lax.axis_index(QUAD), lax.axis_index("x")]).astype(jnp.int32)
    smem, hbm, vmem = (pl.BlockSpec(memory_space=m) for m in (pltpu.SMEM, pltpu.HBM, pltpu.VMEM))
    down_t = adapter_down.T
    block, grads_block = shape((seq, 128), BF16), shape((2 * RANK, 128), F32)
    local_scratch = [pltpu.VMEM((seq, 128), BF16)] * 4
    adapter_scratch = [pltpu.VMEM((RANK, 128), BF16)] * 2

    def swap(array, axis, bit=1):
        return lax.ppermute(array, axis, [(i, i ^ bit) for i in range(4 if axis in ("x", QUAD) else 2)])

    partial = call(
        bottleneck_kernel,
        shape((seq, 128), F32),
        interpret,
        56,
        in_specs=[hbm] * 4,
        scratch_shapes=[*local_scratch[:2], *adapter_scratch, pltpu.SemaphoreType.DMA((4,))],
    )(out_first, grad_second, down_t, adapter_up)
    terms = lax.all_to_all(partial.reshape(32, seq // 32, 128), PLANE, 0, 0)
    mine = call(add_up_kernel, shape(terms.shape, F32), interpret)(terms)

    tiles = (2, 2, 4, 2, 128, 128)
    matrices = (query_proj.reshape(tiles), key_proj.reshape(tiles), value_proj.reshape(tiles), output_proj)
    pieces = call(
        pack_kernel,
        (shape((128, 512), BF16),) * 3,
        interpret,
        56,
        in_specs=[smem] + [hbm] * 4,
        scratch_shapes=[pltpu.SemaphoreType.DMA((12,))],
    )(place, *matrices)
    fetched = jnp.stack([swap(piece, QUAD, k) for k, piece in enumerate(pieces, 1)])
    mine, fetched = lax.optimization_barrier((mine, fetched))
    moved = [lax.ppermute(fetched, "x", [(i, (i + s) % 4) for i in range(4)]) for s in (1, 2, 3)]
    sums = lax.all_to_all(mine, PLANE, 0, 0).reshape(seq, 128)
    sums, moved[0], moved[2] = lax.optimization_barrier((sums, moved[0], moved[2]))

    gain = norm_gain.astype(F32).reshape(2, 2, 4, 2, 128)
    gain = lax.dynamic_index_in_dim(gain, lax.axis_index("yb"), 1, False)
    gain = lax.dynamic_index_in_dim(gain, lax.axis_index("zb"), 2, False).reshape(8, 128)
    gain_local = lax.dynamic_slice_in_dim(gain, lax.axis_index(OCTET), 1)

    shared, in_second, first_grad, adapters = call(
        adapter_kernel,
        (shape((8, 2 * seq, 128), BF16), block, block, grads_block),
        interpret,
        56,
        in_specs=[vmem] + [hbm] * 6,
        out_specs=(hbm, vmem, vmem, vmem),
        scratch_shapes=[
            *local_scratch, *adapter_scratch, pltpu.VMEM((2 * seq, 128), BF16), pltpu.SemaphoreType.DMA((8,))
        ],
    )(sums, out_first, out_second, grad_first, grad_second, adapter_up, down_t)
    gathered = lax.all_to_all(shared, OCTET, 0, 0)
    here = [lax.optimization_barrier((piece, shared))[0] for piece in (fetched, *moved)]
    weights = call(
        assemble_kernel,
        shape((4, 8, 128, 512), BF16),
        interpret,
        in_specs=[smem] + [hbm] * 4 + [vmem] * 8,
        scratch_shapes=[pltpu.VMEM((8, 128, 128), BF16), pltpu.SemaphoreType.DMA((14,))],
    )(place, *matrices, *here, *(swap(piece, "c") for piece in here))

    adapters = adapters + swap(adapters, "yh")
    gathered, adapters = lax.optimization_barrier((gathered, adapters))

    quads = shape((4, seq + 16, 512), BF16)
    held = pltpu.VMEM((4, 8, 128, 512), BF16)
    projected = call(
        project_kernel,
        quads,
        interpret,
        48,
        in_specs=[vmem, vmem, hbm],
        out_specs=hbm,
        scratch_shapes=[
            held,
            pltpu.VMEM((seq, 1024), BF16),
            pltpu.VMEM((seq, 1024), BF16),
            pltpu.VMEM(quads.shape, BF16),
            pltpu.SemaphoreType.DMA((4,)),
            pltpu.SemaphoreType.DMA((4,)),
        ],
    )(gathered, gain, weights)
    projected = lax.all_to_all(projected, QUAD, 0, 0)
    grads, inv_rms, adapters = call(
        functools.partial(attention_kernel, width),
        (quads, shape((seq, 128), F32), grads_block),
        interpret,
        48,
        out_specs=(hbm, vmem, vmem),
        scratch_shapes=[pltpu.VMEM(quads.shape[1:], BF16), pltpu.SemaphoreType.DMA((4,))],
    )(projected, adapters, swap(adapters, "x", 2))
    grads = lax.all_to_all(grads, QUAD, 0, 0)
    octets = shape((8, 2 * seq + 32, 128), BF16)
    outward, adapters = call(
        spread_kernel,
        (octets, grads_block),
        interpret,
        48,
        in_specs=[vmem, vmem, vmem, hbm],
        out_specs=(hbm, vmem),
        scratch_shapes=[
            held,
            pltpu.VMEM((seq, 1024), F32),
            pltpu.VMEM((seq, 1024), F32),
            pltpu.VMEM(octets.shape, BF16),
            pltpu.SemaphoreType.DMA((4,)),
            pltpu.SemaphoreType.DMA((8,)),
        ],
    )(grads, adapters, swap(adapters, "x", 1), weights)
    inward = lax.all_to_all(outward, OCTET, 0, 0)
    in_first, second_grad, down_grad, up_grad = call(
        functools.partial(finish_kernel, width),
        (block, block, shape((RANK, 128), F32), shape((RANK, 128), F32)),
        interpret,
    )(inward, inv_rms, out_first, in_second, grad_second, gain_local, adapters, swap(adapters, "c"))
    return (in_first, in_second, first_grad, second_grad, down_grad.T, up_grad)


def over(mesh, interpret=False):
    rows, columns = P(SEQS, PLANE), P(None, PLANE)
    return jax.shard_map(
        functools.partial(shards, interpret),
        mesh=mesh,
        in_specs=(rows, rows, rows, rows, P(), columns, columns, columns, P(PLANE, None), P(PLANE, None), columns),
        out_specs=(rows, rows, rows, rows, P(PLANE, None), columns),
        check_vma=False,
    )


def solution(mesh):
    devices = mesh.devices.reshape(2, 4, 2, 2, 2, 4, 2)
    return over(Mesh(devices, SEQS + PLANE))
```

```python
import functools

import jax
import jax.numpy as jnp
from jax import lax
from jax.experimental import pallas as pl
from jax.experimental.pallas import tpu as pltpu
from jax.sharding import Mesh, PartitionSpec as P

HEAD_DIM = 128
RANK = 64
EPS = 1e-05
MASKED = -1e30

QUAD = ("yb", "zb")
OCTET = ("ya", "za")
PLANE = ("ya", "yb", "za", "zb")
SEQS = ("yh", "x", "c")
QKV, OUT = slice(0, 384), slice(384, 512)
F32 = jnp.float32
BF16 = jnp.bfloat16


def dot(a, b, dims=((1,), (0,)), precision=None):
    return lax.dot_general(a, b, (dims, ((), ())), preferred_element_type=F32, precision=precision)


NT = ((1,), (1,))
TN = ((0,), (0,))


def row_sums(wide):
    sums = dot(jnp.ones((8, 128), F32), wide, NT, lax.Precision.HIGHEST)
    lead = sums.astype(BF16)
    rest = (sums - lead.astype(F32)).astype(BF16)
    return lead, rest


def to_column(row):
    return jnp.broadcast_to(row, (128, row.shape[1])).T


def call(body, out_shapes, interpret, vmem=16, **kwargs):
    return pl.pallas_call(
        body,
        out_shape=out_shapes,
        compiler_params=pltpu.CompilerParams(vmem_limit_bytes=vmem * 1024 * 1024),
        interpret=interpret,
        **kwargs,
    )


def fetch(pairs, sems):
    copies = [pltpu.make_async_copy(src, dst, sems.at[i]) for i, (src, dst) in enumerate(pairs)]
    for copy in copies:
        copy.start()
    return copies


def bottleneck_kernel(first_ref, gsecond_ref, downt_ref, up_ref, partial_ref, first, gsecond, downt, up, sems):
    copies = fetch(((downt_ref, downt), (up_ref, up), (first_ref, first), (gsecond_ref, gsecond)), sems)
    for copy in copies:
        copy.wait()
    partial_ref[:, :RANK] = dot(first[...], downt[...], NT)
    partial_ref[:, RANK:] = dot(gsecond[...], up[...], NT)


def pack_kernel(place_ref, query_ref, key_ref, value_ref, output_ref, one_ref, two_ref, three_ref, sems):
    core, quad = place_ref[0], place_ref[1]
    pairs = []
    for k, piece in ((1, one_ref), (2, two_ref), (3, three_ref)):
        yb, zb = lax.div(quad, 2) ^ (k // 2), lax.rem(quad, 2) ^ (k % 2)
        for w, matrix in enumerate((query_ref, key_ref, value_ref)):
            pairs.append((matrix.at[core, yb, :, zb], piece.at[:, :, w * 128 : w * 128 + 128]))
        for z in range(4):
            start = (((core * 2 + yb) * 4 + z) * 2 + zb) * 128
            pairs.append((output_ref.at[:, pl.ds(pl.multiple_of(start, 128), 128)], piece.at[z, :, OUT]))
    for copy in fetch(pairs, sems):
        copy.wait()


def assemble_kernel(place_ref, query_ref, key_ref, value_ref, output_ref, *refs):
    pieces, (stored_ref, out_ref, own_out, sems, store_sems) = refs[:6], refs[6:]
    core, quad = place_ref[0], place_ref[1]
    yb, zb = lax.div(quad, 2), lax.rem(quad, 2)
    pairs = []
    for y in range(2):
        for w, matrix in enumerate((query_ref, key_ref, value_ref)):
            pairs.append(
                (matrix.at[y, yb, :, zb], out_ref.at[quad, y * 4 : y * 4 + 4, :, w * 128 : w * 128 + 128])
            )
        for z in range(4):
            start = (((y * 2 + yb) * 4 + z) * 2 + zb) * 128
            pairs.append((output_ref.at[:, pl.ds(pl.multiple_of(start, 128), 128)], own_out.at[y * 4 + z]))
    copies = fetch(pairs, sems)
    eye = (
        lax.broadcasted_iota(jnp.int32, (128, 128), 0) == lax.broadcasted_iota(jnp.int32, (128, 128), 1)
    ).astype(BF16)
    stores = []
    for k in (1, 2, 3):
        h = quad ^ k
        for side in range(2):
            ref = pieces[side * 3 + k - 1]
            for z in range(4):
                f = (core ^ side) * 4 + z
                out_ref[h, f, :, QKV] = ref[z, :, QKV]
                out_ref[h, f, :, OUT] = dot(eye, ref[z, :, OUT], NT).astype(BF16)
        stores.append(pltpu.make_async_copy(out_ref.at[h], stored_ref.at[h], store_sems.at[k]))
        stores[-1].start()
    for copy in copies:
        copy.wait()
    for f in range(8):
        out_ref[quad, f, :, OUT] = dot(eye, own_out[f], NT).astype(BF16)
    stores.append(pltpu.make_async_copy(out_ref.at[quad], stored_ref.at[quad], store_sems.at[0]))
    stores[-1].start()
    for store in stores:
        store.wait()


def add_up_kernel(terms_ref, out_ref):
    total = jnp.sum(terms_ref[...], 0)
    for i in range(out_ref.shape[0]):
        out_ref[i] = total


def adapter_kernel(
    sums_ref, first_ref, second_ref, gfirst_ref, gsecond_ref, up_ref, downt_ref,
    shared_ref, in_second_ref, first_grad_ref, adapters_ref,
):
    seq = first_ref.shape[0]
    sums = sums_ref[...]
    pre_act = sums[:, :RANK]
    back_sum = pltpu.roll(sums, RANK, 1)[:, :RANK]
    logistic = 1.0 / (1.0 + jnp.exp(-pre_act))
    activation = (pre_act * logistic).astype(BF16)
    pre_grad = (back_sum * (logistic * (1.0 + pre_act * (1.0 - logistic)))).astype(BF16)
    in_second = (second_ref[...].astype(F32) - dot(activation, up_ref[...])).astype(BF16)
    first_grad = (gfirst_ref[...].astype(F32) + dot(pre_grad, downt_ref[...])).astype(BF16)
    in_second_ref[...] = in_second
    first_grad_ref[...] = first_grad
    for s in range(8):
        shared_ref[s, :seq] = in_second
        shared_ref[s, seq:] = first_grad
    adapters_ref[:RANK] = dot(pre_grad, first_ref[...], TN)
    adapters_ref[RANK:] = dot(activation, gsecond_ref[...], TN)


def project_kernel(
    gathered_ref, gain_ref, adapters_ref, arrived_ref, weights_ref, partial_ref, adapters_out_ref,
    weights, x_ref, g_ref, out, in_sems, out_sems,
):
    seq = x_ref.shape[0]
    arriving = fetch([(weights_ref.at[h], weights.at[h]) for h in range(4)], in_sems)
    adapters_out_ref[...] = adapters_ref[...] + arrived_ref[...]
    squares = jnp.zeros((seq, 128), F32)
    for f in range(8):
        lanes = slice(f * 128, f * 128 + 128)
        wide = gathered_ref[f, :seq].astype(F32)
        squares = squares + wide * wide
        x_ref[:, lanes] = (wide * gain_ref[f : f + 1, :]).astype(BF16)
        g_ref[:, lanes] = gathered_ref[f, seq:]
    lead, rest = row_sums(squares)
    tail = jnp.concatenate([lead, rest], 0)
    leaving = []
    for h in range(4):
        arriving[h].wait()
        out[h, :seq, QKV] = dot(x_ref[...], weights[h, :, :, QKV].reshape(1024, 384)).astype(BF16)
        out[h, :seq, OUT] = dot(g_ref[...], weights[h, :, :, OUT].reshape(1024, 128)).astype(BF16)
        out[h, seq:, :seq] = tail
        out[h, seq:, seq:] = jnp.zeros((16, 512 - seq), BF16)
        leaving.append(pltpu.make_async_copy(out.at[h], partial_ref.at[h], out_sems.at[h]))
        leaving[-1].start()
    for copy in leaving:
        copy.wait()


def attention_kernel(width, partial_ref, adapters_ref, arrived_ref, grads_ref, inv_ref, adapters_out_ref, out, sems):
    adapters_out_ref[...] = adapters_ref[...] + arrived_ref[...]
    seq = inv_ref.shape[0]
    scale = HEAD_DIM ** (-0.5)

    def total(lo, hi):
        rows = partial_ref[0, :seq, lo:hi].astype(F32)
        for s in range(1, 4):
            rows = rows + partial_ref[s, :seq, lo:hi].astype(F32)
        return rows

    square = jnp.zeros((1, seq), F32)
    for s in range(4):
        tail = partial_ref[s, seq:, :seq].astype(F32)
        square = square + tail[:1] + tail[8:9]
    inv = to_column(lax.rsqrt(square / width + EPS))
    inv_ref[...] = inv
    query_wide, key_wide, value_wide = total(0, 128) * inv, total(128, 256) * inv, total(256, 384) * inv
    query, key, value = query_wide.astype(BF16), key_wide.astype(BF16), value_wide.astype(BF16)
    back_ctx = total(384, 512).astype(BF16)
    scores = dot(query, key, NT) * scale
    query_pos = lax.broadcasted_iota(jnp.int32, (seq, seq), 0)
    key_pos = lax.broadcasted_iota(jnp.int32, (seq, seq), 1)
    scores = jnp.where(key_pos <= query_pos, scores, MASKED)
    weights = jnp.exp(scores - jnp.max(scores, axis=1, keepdims=True))
    probs = (weights / jnp.sum(weights, axis=1, keepdims=True)).astype(BF16)
    context = dot(probs, value).astype(BF16)
    value_grad = dot(probs, back_ctx, TN).astype(BF16)
    prob_grad = dot(back_ctx, value, NT)
    prob_wide = probs.astype(F32)
    inner = jnp.sum(prob_grad * prob_wide, axis=1, keepdims=True)
    score_grad = (prob_wide * (prob_grad - inner) * scale).astype(BF16)
    query_grad = dot(score_grad, key).astype(BF16)
    key_grad = dot(score_grad, query, TN).astype(BF16)
    stat = (
        query_grad.astype(F32) * query_wide + key_grad.astype(F32) * key_wide + value_grad.astype(F32) * value_wide
    )
    lead, rest = row_sums(stat)
    tail = jnp.concatenate([lead, rest], 0)
    out[:seq, :128] = query_grad
    out[:seq, 128:256] = key_grad
    out[:seq, 256:384] = value_grad
    out[:seq, OUT] = context
    out[seq:, :seq] = tail
    out[seq:, seq:] = jnp.zeros((16, 512 - seq), BF16)
    for copy in fetch([(out, grads_ref.at[s]) for s in range(4)], sems):
        copy.wait()


def spread_kernel(
    grads_ref, adapters_ref, arrived_ref, weights_ref, terms_ref, adapters_out_ref,
    weights, norm, attn, out, in_sems, out_sems,
):
    arriving = fetch([(weights_ref.at[h], weights.at[h]) for h in range(4)], in_sems)
    adapters_out_ref[...] = adapters_ref[...] + arrived_ref[...]
    seq = grads_ref.shape[1] - 16
    stat = jnp.zeros((8, seq), F32)
    for h in range(4):
        tail = grads_ref[h, seq:, :seq].astype(F32)
        stat = stat + tail[:8] + tail[8:]
    lead = stat.astype(BF16)
    rest = (stat - lead.astype(F32)).astype(BF16)
    tail = jnp.concatenate([lead, rest], 0)
    for h in range(4):
        arriving[h].wait()
        into_norm = dot(grads_ref[h, :seq, QKV], weights[h, :, :, QKV].reshape(1024, 384), NT)
        into_attn = dot(grads_ref[h, :seq, OUT], weights[h, :, :, OUT].reshape(1024, 128), NT)
        norm[...] = norm[...] + into_norm if h else into_norm
        attn[...] = attn[...] + into_attn if h else into_attn
    leaving = []
    for f in range(8):
        lanes = slice(f * 128, f * 128 + 128)
        out[f, :seq] = attn[:, lanes].astype(BF16)
        out[f, seq : 2 * seq] = norm[:, lanes].astype(BF16)
        out[f, 2 * seq : 2 * seq + 16] = tail[:, :128]
        out[f, 2 * seq + 16 :] = tail[:, 128:]
        leaving.append(pltpu.make_async_copy(out.at[f], terms_ref.at[f], out_sems.at[f]))
        leaving[-1].start()
    for copy in leaving:
        copy.wait()


def finish_kernel(
    width, terms_ref, inv_ref, first_ref, in_second_ref, gsecond_ref, gain_ref, adapters_ref, arrived_ref,
    in_first_ref, second_grad_ref, down_grad_ref, up_grad_ref,
):
    down_grad_ref[...] = adapters_ref[:RANK] + arrived_ref[:RANK]
    up_grad_ref[...] = adapters_ref[RANK:] + arrived_ref[RANK:]
    seq = first_ref.shape[0]
    total = terms_ref[0].astype(F32)
    for s in range(1, 8):
        total = total + terms_ref[s].astype(F32)
    in_first_ref[...] = (first_ref[...].astype(F32) - total[:seq]).astype(BF16)
    halves = [total[2 * seq + i : 2 * seq + i + 1] + total[2 * seq + i + 8 : 2 * seq + i + 9] for i in (0, 16)]
    stat = jnp.concatenate([to_column(half) for half in halves], 0) / width
    inv = inv_ref[...]
    gain_grad = gain_ref[...] * total[seq : 2 * seq]
    second = in_second_ref[...].astype(F32)
    second_grad_ref[...] = (gsecond_ref[...].astype(F32) + inv * (gain_grad - second * stat * inv)).astype(BF16)


def shards(
    interpret,
    out_first,
    out_second,
    grad_first,
    grad_second,
    norm_gain,
    query_proj,
    key_proj,
    value_proj,
    output_proj,
    adapter_down,
    adapter_up,
):
    seq = out_first.shape[0]
    width = query_proj.shape[0]
    shape = jax.ShapeDtypeStruct
    place = jnp.stack([lax.axis_index("c"), lax.axis_index(QUAD)]).astype(jnp.int32)
    smem, hbm, vmem = (pl.BlockSpec(memory_space=m) for m in (pltpu.SMEM, pltpu.HBM, pltpu.VMEM))
    down_t = adapter_down.T
    block, grads_block = shape((seq, 128), BF16), shape((2 * RANK, 128), F32)

    def swap(array, axis, bit=1):
        return lax.ppermute(array, axis, [(i, i ^ bit) for i in range(4 if axis in ("x", QUAD) else 2)])

    partial = call(
        bottleneck_kernel,
        shape((seq, 128), F32),
        interpret,
        56,
        in_specs=[hbm] * 4,
        scratch_shapes=[pltpu.VMEM((seq, 128), BF16)] * 2
        + [pltpu.VMEM((RANK, 128), BF16)] * 2
        + [pltpu.SemaphoreType.DMA((4,))],
    )(out_first, grad_second, down_t, adapter_up)
    terms = lax.all_to_all(partial.reshape(32, seq // 32, 128), PLANE, 0, 0)
    mine = call(add_up_kernel, shape(terms.shape, F32), interpret)(terms)

    tiles = (2, 2, 4, 2, 128, 128)
    matrices = (query_proj.reshape(tiles), key_proj.reshape(tiles), value_proj.reshape(tiles), output_proj)
    pieces = call(
        pack_kernel,
        (shape((4, 128, 512), BF16),) * 3,
        interpret,
        56,
        in_specs=[smem] + [hbm] * 4,
        scratch_shapes=[pltpu.SemaphoreType.DMA((21,))],
    )(place, *matrices)
    here = [swap(piece, QUAD, k) for k, piece in enumerate(pieces, 1)]
    sums = lax.all_to_all(mine, PLANE, 0, 0).reshape(seq, 128)
    sums, *here = lax.optimization_barrier((sums, *here))
    held = pltpu.VMEM((4, 8, 128, 512), BF16)

    gain = norm_gain.astype(F32).reshape(2, 2, 4, 2, 128)
    gain = lax.dynamic_index_in_dim(gain, lax.axis_index("yb"), 1, False)
    gain = lax.dynamic_index_in_dim(gain, lax.axis_index("zb"), 2, False).reshape(8, 128)
    gain_local = lax.dynamic_slice_in_dim(gain, lax.axis_index(OCTET), 1)

    shared, in_second, first_grad, adapters = call(
        adapter_kernel,
        (shape((8, 2 * seq, 128), BF16), block, block, grads_block),
        interpret,
    )(sums, out_first, out_second, grad_first, grad_second, adapter_up, down_t)
    gathered = lax.all_to_all(shared, OCTET, 0, 0)
    weights = call(
        assemble_kernel,
        shape((4, 8, 128, 512), BF16),
        interpret,
        54,
        in_specs=[smem] + [hbm] * 4 + [vmem] * 6,
        out_specs=hbm,
        scratch_shapes=[
            held,
            pltpu.VMEM((8, 128, 128), BF16),
            pltpu.SemaphoreType.DMA((14,)),
            pltpu.SemaphoreType.DMA((4,)),
        ],
    )(place, *matrices, *here, *(swap(piece, "c") for piece in here))

    quads = shape((4, seq + 16, 512), BF16)
    projected, adapters = call(
        project_kernel,
        (quads, grads_block),
        interpret,
        48,
        in_specs=[vmem] * 4 + [hbm],
        out_specs=(hbm, vmem),
        scratch_shapes=[
            held,
            pltpu.VMEM((seq, 1024), BF16),
            pltpu.VMEM((seq, 1024), BF16),
            pltpu.VMEM(quads.shape, BF16),
            pltpu.SemaphoreType.DMA((4,)),
            pltpu.SemaphoreType.DMA((4,)),
        ],
    )(gathered, gain, adapters, swap(adapters, "yh"), weights)
    projected = lax.all_to_all(projected, QUAD, 0, 0)
    grads, inv_rms, adapters = call(
        functools.partial(attention_kernel, width),
        (quads, shape((seq, 128), F32), grads_block),
        interpret,
        48,
        out_specs=(hbm, vmem, vmem),
        scratch_shapes=[pltpu.VMEM(quads.shape[1:], BF16), pltpu.SemaphoreType.DMA((4,))],
    )(projected, adapters, swap(adapters, "x", 2))
    grads = lax.all_to_all(grads, QUAD, 0, 0)
    octets = shape((8, 2 * seq + 32, 128), BF16)
    outward, adapters = call(
        spread_kernel,
        (octets, grads_block),
        interpret,
        48,
        in_specs=[vmem, vmem, vmem, hbm],
        out_specs=(hbm, vmem),
        scratch_shapes=[
            held,
            pltpu.VMEM((seq, 1024), F32),
            pltpu.VMEM((seq, 1024), F32),
            pltpu.VMEM(octets.shape, BF16),
            pltpu.SemaphoreType.DMA((4,)),
            pltpu.SemaphoreType.DMA((8,)),
        ],
    )(grads, adapters, swap(adapters, "x", 1), weights)
    inward = lax.all_to_all(outward, OCTET, 0, 0)
    in_first, second_grad, down_grad, up_grad = call(
        functools.partial(finish_kernel, width),
        (block, block, shape((RANK, 128), F32), shape((RANK, 128), F32)),
        interpret,
    )(inward, inv_rms, out_first, in_second, grad_second, gain_local, adapters, swap(adapters, "c"))
    return (in_first, in_second, first_grad, second_grad, down_grad.T, up_grad)


def over(mesh, interpret=False):
    rows, columns = P(SEQS, PLANE), P(None, PLANE)
    return jax.shard_map(
        functools.partial(shards, interpret),
        mesh=mesh,
        in_specs=(rows, rows, rows, rows, P(), columns, columns, columns, P(PLANE, None), P(PLANE, None), columns),
        out_specs=(rows, rows, rows, rows, P(PLANE, None), columns),
        check_vma=False,
    )


def solution(mesh):
    devices = mesh.devices.reshape(2, 4, 2, 2, 2, 4, 2)
    return over(Mesh(devices, SEQS + PLANE))
```

```python
import functools

import jax
import jax.numpy as jnp
from jax import lax
from jax.experimental import pallas as pl
from jax.experimental.pallas import tpu as pltpu
from jax.sharding import Mesh, PartitionSpec as P

HEAD_DIM = 128
RANK = 64
EPS = 1e-05
MASKED = -1e30

QUAD = ("yb", "zb")
OCTET = ("ya", "za")
PLANE = ("ya", "yb", "za", "zb")
SEQS = ("yh", "x", "c")
QKV, OUT = slice(0, 384), slice(384, 512)
F32 = jnp.float32
BF16 = jnp.bfloat16


def dot(a, b, dims=((1,), (0,)), precision=None):
    return lax.dot_general(a, b, (dims, ((), ())), preferred_element_type=F32, precision=precision)


NT = ((1,), (1,))
TN = ((0,), (0,))


def row_sums(wide):
    sums = dot(jnp.ones((8, 128), F32), wide, NT, lax.Precision.HIGHEST)
    lead = sums.astype(BF16)
    rest = (sums - lead.astype(F32)).astype(BF16)
    return lead, rest


def to_column(row):
    return jnp.broadcast_to(row, (128, row.shape[1])).T


def call(body, out_shapes, interpret, vmem=16, **kwargs):
    return pl.pallas_call(
        body,
        out_shape=out_shapes,
        compiler_params=pltpu.CompilerParams(vmem_limit_bytes=vmem * 1024 * 1024),
        interpret=interpret,
        **kwargs,
    )


def fetch(pairs, sems):
    copies = [pltpu.make_async_copy(src, dst, sems.at[i]) for i, (src, dst) in enumerate(pairs)]
    for copy in copies:
        copy.start()
    return copies


def bottleneck_kernel(first_ref, gsecond_ref, downt_ref, up_ref, partial_ref, first, gsecond, downt, up, sems):
    copies = fetch(((downt_ref, downt), (up_ref, up), (first_ref, first), (gsecond_ref, gsecond)), sems)
    for copy in copies:
        copy.wait()
    partial_ref[:, :RANK] = dot(first[...], downt[...], NT)
    partial_ref[:, RANK:] = dot(gsecond[...], up[...], NT)


def pack_kernel(place_ref, query_ref, key_ref, value_ref, output_ref, one_ref, two_ref, three_ref, sems):
    core, quad, plane = place_ref[0], place_ref[1], place_ref[2]
    pairs = []
    for k, piece in ((1, one_ref), (2, two_ref), (3, three_ref)):
        yb, zb = lax.div(quad, 2) ^ (k // 2), lax.rem(quad, 2) ^ (k % 2)
        for w, matrix in enumerate((query_ref, key_ref, value_ref)):
            pairs.append((matrix.at[core, yb, plane, zb], piece.at[:, w * 128 : w * 128 + 128]))
        start = (((core * 2 + yb) * 4 + plane) * 2 + zb) * 128
        pairs.append((output_ref.at[:, pl.ds(pl.multiple_of(start, 128), 128)], piece.at[:, OUT]))
    for copy in fetch(pairs, sems):
        copy.wait()


def assemble_kernel(place_ref, query_ref, key_ref, value_ref, output_ref, *refs):
    pieces, (stored_ref, out_ref, own_out, sems, store_sems) = refs[:8], refs[8:]
    core, quad, plane = place_ref[0], place_ref[1], place_ref[2]
    yb, zb = lax.div(quad, 2), lax.rem(quad, 2)
    pairs = []
    for y in range(2):
        for w, matrix in enumerate((query_ref, key_ref, value_ref)):
            pairs.append(
                (matrix.at[y, yb, :, zb], out_ref.at[quad, y * 4 : y * 4 + 4, :, w * 128 : w * 128 + 128])
            )
        for z in range(4):
            start = (((y * 2 + yb) * 4 + z) * 2 + zb) * 128
            pairs.append((output_ref.at[:, pl.ds(pl.multiple_of(start, 128), 128)], own_out.at[y * 4 + z]))
    copies = fetch(pairs, sems)
    eye = (
        lax.broadcasted_iota(jnp.int32, (128, 128), 0) == lax.broadcasted_iota(jnp.int32, (128, 128), 1)
    ).astype(BF16)
    stores = []
    for k in (1, 2, 3):
        h = quad ^ k
        for i, ref in enumerate(pieces):
            f = (core ^ (i // 4)) * 4 + lax.rem(plane + 4 - i % 4, 4)
            out_ref[h, f, :, QKV] = ref[k - 1, :, QKV]
            out_ref[h, f, :, OUT] = dot(eye, ref[k - 1, :, OUT], NT).astype(BF16)
        stores.append(pltpu.make_async_copy(out_ref.at[h], stored_ref.at[h], store_sems.at[k]))
        stores[-1].start()
    for copy in copies:
        copy.wait()
    for f in range(8):
        out_ref[quad, f, :, OUT] = dot(eye, own_out[f], NT).astype(BF16)
    stores.append(pltpu.make_async_copy(out_ref.at[quad], stored_ref.at[quad], store_sems.at[0]))
    stores[-1].start()
    for store in stores:
        store.wait()


def add_up_kernel(terms_ref, out_ref):
    total = jnp.sum(terms_ref[...], 0)
    for i in range(out_ref.shape[0]):
        out_ref[i] = total


def adapter_kernel(
    sums_ref, first_ref, second_ref, gfirst_ref, gsecond_ref, up_ref, downt_ref,
    shared_ref, in_second_ref, first_grad_ref, adapters_ref,
):
    seq = first_ref.shape[0]
    sums = sums_ref[...]
    pre_act = sums[:, :RANK]
    back_sum = pltpu.roll(sums, RANK, 1)[:, :RANK]
    logistic = 1.0 / (1.0 + jnp.exp(-pre_act))
    activation = (pre_act * logistic).astype(BF16)
    pre_grad = (back_sum * (logistic * (1.0 + pre_act * (1.0 - logistic)))).astype(BF16)
    in_second = (second_ref[...].astype(F32) - dot(activation, up_ref[...])).astype(BF16)
    first_grad = (gfirst_ref[...].astype(F32) + dot(pre_grad, downt_ref[...])).astype(BF16)
    in_second_ref[...] = in_second
    first_grad_ref[...] = first_grad
    for s in range(8):
        shared_ref[s, :seq] = in_second
        shared_ref[s, seq:] = first_grad
    adapters_ref[:RANK] = dot(pre_grad, first_ref[...], TN)
    adapters_ref[RANK:] = dot(activation, gsecond_ref[...], TN)


def project_kernel(
    gathered_ref, gain_ref, adapters_ref, arrived_ref, weights_ref, partial_ref, adapters_out_ref,
    weights, x_ref, g_ref, out, in_sems, out_sems,
):
    seq = x_ref.shape[0]
    arriving = fetch([(weights_ref.at[h], weights.at[h]) for h in range(4)], in_sems)
    adapters_out_ref[...] = adapters_ref[...] + arrived_ref[...]
    squares = jnp.zeros((seq, 128), F32)
    for f in range(8):
        lanes = slice(f * 128, f * 128 + 128)
        wide = gathered_ref[f, :seq].astype(F32)
        squares = squares + wide * wide
        x_ref[:, lanes] = (wide * gain_ref[f : f + 1, :]).astype(BF16)
        g_ref[:, lanes] = gathered_ref[f, seq:]
    lead, rest = row_sums(squares)
    tail = jnp.concatenate([lead, rest], 0)
    leaving = []
    for h in range(4):
        arriving[h].wait()
        out[h, :seq, QKV] = dot(x_ref[...], weights[h, :, :, QKV].reshape(1024, 384)).astype(BF16)
        out[h, :seq, OUT] = dot(g_ref[...], weights[h, :, :, OUT].reshape(1024, 128)).astype(BF16)
        out[h, seq:, :seq] = tail
        out[h, seq:, seq:] = jnp.zeros((16, 512 - seq), BF16)
        leaving.append(pltpu.make_async_copy(out.at[h], partial_ref.at[h], out_sems.at[h]))
        leaving[-1].start()
    for copy in leaving:
        copy.wait()


def attention_kernel(width, partial_ref, grads_ref, inv_ref, out, sems):
    seq = inv_ref.shape[0]
    scale = HEAD_DIM ** (-0.5)

    def total(lo, hi):
        rows = partial_ref[0, :seq, lo:hi].astype(F32)
        for s in range(1, 4):
            rows = rows + partial_ref[s, :seq, lo:hi].astype(F32)
        return rows

    square = jnp.zeros((1, seq), F32)
    for s in range(4):
        tail = partial_ref[s, seq:, :seq].astype(F32)
        square = square + tail[:1] + tail[8:9]
    inv = to_column(lax.rsqrt(square / width + EPS))
    inv_ref[...] = inv
    query_wide, key_wide, value_wide = total(0, 128) * inv, total(128, 256) * inv, total(256, 384) * inv
    query, key, value = query_wide.astype(BF16), key_wide.astype(BF16), value_wide.astype(BF16)
    back_ctx = total(384, 512).astype(BF16)
    scores = dot(query, key, NT) * scale
    query_pos = lax.broadcasted_iota(jnp.int32, (seq, seq), 0)
    key_pos = lax.broadcasted_iota(jnp.int32, (seq, seq), 1)
    scores = jnp.where(key_pos <= query_pos, scores, MASKED)
    weights = jnp.exp(scores - jnp.max(scores, axis=1, keepdims=True))
    probs = (weights / jnp.sum(weights, axis=1, keepdims=True)).astype(BF16)
    context = dot(probs, value).astype(BF16)
    value_grad = dot(probs, back_ctx, TN).astype(BF16)
    prob_grad = dot(back_ctx, value, NT)
    prob_wide = probs.astype(F32)
    inner = jnp.sum(prob_grad * prob_wide, axis=1, keepdims=True)
    score_grad = (prob_wide * (prob_grad - inner) * scale).astype(BF16)
    query_grad = dot(score_grad, key).astype(BF16)
    key_grad = dot(score_grad, query, TN).astype(BF16)
    stat = (
        query_grad.astype(F32) * query_wide + key_grad.astype(F32) * key_wide + value_grad.astype(F32) * value_wide
    )
    lead, rest = row_sums(stat)
    tail = jnp.concatenate([lead, rest], 0)
    out[:seq, :128] = query_grad
    out[:seq, 128:256] = key_grad
    out[:seq, 256:384] = value_grad
    out[:seq, OUT] = context
    out[seq:, :seq] = tail
    out[seq:, seq:] = jnp.zeros((16, 512 - seq), BF16)
    for copy in fetch([(out, grads_ref.at[s]) for s in range(4)], sems):
        copy.wait()


def spread_kernel(
    grads_ref, adapters_ref, weights_ref, terms_ref, adapters_out_ref,
    weights, norm, attn, out, in_sems, out_sems,
):
    arriving = fetch([(weights_ref.at[h], weights.at[h]) for h in range(4)], in_sems)
    adapters_out_ref[...] = adapters_ref[...]
    seq = grads_ref.shape[1] - 16
    stat = jnp.zeros((8, seq), F32)
    for h in range(4):
        tail = grads_ref[h, seq:, :seq].astype(F32)
        stat = stat + tail[:8] + tail[8:]
    halves = []
    for lanes in (slice(0, 128), slice(128, 256)):
        lead = stat[:4, lanes].astype(BF16)
        halves += [lead, (stat[:4, lanes] - lead.astype(F32)).astype(BF16)]
    tail = jnp.concatenate([half.astype(F32) for half in halves], 0).astype(BF16)
    for h in range(4):
        arriving[h].wait()
        into_norm = dot(grads_ref[h, :seq, QKV], weights[h, :, :, QKV].reshape(1024, 384), NT)
        into_attn = dot(grads_ref[h, :seq, OUT], weights[h, :, :, OUT].reshape(1024, 128), NT)
        norm[...] = norm[...] + into_norm if h else into_norm
        attn[...] = attn[...] + into_attn if h else into_attn
    leaving = []
    for f in range(8):
        lanes = slice(f * 128, f * 128 + 128)
        out[f, :seq] = attn[:, lanes].astype(BF16)
        out[f, seq : 2 * seq] = norm[:, lanes].astype(BF16)
        out[f, 2 * seq :] = tail
        leaving.append(pltpu.make_async_copy(out.at[f], terms_ref.at[f], out_sems.at[f]))
        leaving[-1].start()
    for copy in leaving:
        copy.wait()


def finish_kernel(
    width, terms_ref, inv_ref, first_ref, in_second_ref, gsecond_ref, gain_ref, adapters_ref, arrived_ref,
    in_first_ref, second_grad_ref, down_grad_ref, up_grad_ref,
):
    down_grad_ref[...] = adapters_ref[:RANK] + arrived_ref[:RANK]
    up_grad_ref[...] = adapters_ref[RANK:] + arrived_ref[RANK:]
    seq = first_ref.shape[0]
    total = terms_ref[0].astype(F32)
    for s in range(1, 8):
        total = total + terms_ref[s].astype(F32)
    in_first_ref[...] = (first_ref[...].astype(F32) - total[:seq]).astype(BF16)
    halves = [total[2 * seq + i : 2 * seq + i + 1] + total[2 * seq + i + 4 : 2 * seq + i + 5] for i in (0, 8)]
    stat = jnp.concatenate([to_column(half) for half in halves], 0) / width
    inv = inv_ref[...]
    gain_grad = gain_ref[...] * total[seq : 2 * seq]
    second = in_second_ref[...].astype(F32)
    second_grad_ref[...] = (gsecond_ref[...].astype(F32) + inv * (gain_grad - second * stat * inv)).astype(BF16)


def shards(
    interpret,
    out_first,
    out_second,
    grad_first,
    grad_second,
    norm_gain,
    query_proj,
    key_proj,
    value_proj,
    output_proj,
    adapter_down,
    adapter_up,
):
    seq = out_first.shape[0]
    width = query_proj.shape[0]
    shape = jax.ShapeDtypeStruct
    place = jnp.stack([lax.axis_index("c"), lax.axis_index(QUAD), lax.axis_index("x")]).astype(jnp.int32)
    smem, hbm, vmem = (pl.BlockSpec(memory_space=m) for m in (pltpu.SMEM, pltpu.HBM, pltpu.VMEM))
    down_t = adapter_down.T
    block, grads_block = shape((seq, 128), BF16), shape((2 * RANK, 128), F32)

    def swap(array, axis, bit=1):
        return lax.ppermute(array, axis, [(i, i ^ bit) for i in range(4 if axis in ("x", QUAD) else 2)])

    partial = call(
        bottleneck_kernel,
        shape((seq, 128), F32),
        interpret,
        56,
        in_specs=[hbm] * 4,
        scratch_shapes=[pltpu.VMEM((seq, 128), BF16)] * 2
        + [pltpu.VMEM((RANK, 128), BF16)] * 2
        + [pltpu.SemaphoreType.DMA((4,))],
    )(out_first, grad_second, down_t, adapter_up)
    terms = lax.all_to_all(partial.reshape(32, seq // 32, 128), PLANE, 0, 0)
    mine = call(add_up_kernel, shape(terms.shape, F32), interpret)(terms)

    tiles = (2, 2, 4, 2, 128, 128)
    matrices = (query_proj.reshape(tiles), key_proj.reshape(tiles), value_proj.reshape(tiles), output_proj)
    pieces = call(
        pack_kernel,
        (shape((128, 512), BF16),) * 3,
        interpret,
        56,
        in_specs=[smem] + [hbm] * 4,
        scratch_shapes=[pltpu.SemaphoreType.DMA((12,))],
    )(place, *matrices)
    fetched = jnp.stack([swap(piece, QUAD, k) for k, piece in enumerate(pieces, 1)])
    mine, fetched = lax.optimization_barrier((mine, fetched))
    here = [fetched] + [lax.ppermute(fetched, "x", [(i, (i + s) % 4) for i in range(4)]) for s in (1, 3, 2)]
    here = [here[0], here[1], here[3], here[2]]
    sums = lax.all_to_all(mine, PLANE, 0, 0).reshape(seq, 128)
    held = pltpu.VMEM((4, 8, 128, 512), BF16)

    gain = norm_gain.astype(F32).reshape(2, 2, 4, 2, 128)
    gain = lax.dynamic_index_in_dim(gain, lax.axis_index("yb"), 1, False)
    gain = lax.dynamic_index_in_dim(gain, lax.axis_index("zb"), 2, False).reshape(8, 128)
    gain_local = lax.dynamic_slice_in_dim(gain, lax.axis_index(OCTET), 1)

    shared, in_second, first_grad, adapters = call(
        adapter_kernel,
        (shape((8, 2 * seq, 128), BF16), block, block, grads_block),
        interpret,
    )(sums, out_first, out_second, grad_first, grad_second, adapter_up, down_t)
    gathered = lax.all_to_all(shared, OCTET, 0, 0)
    weights = call(
        assemble_kernel,
        shape((4, 8, 128, 512), BF16),
        interpret,
        54,
        in_specs=[smem] + [hbm] * 4 + [vmem] * 8,
        out_specs=hbm,
        scratch_shapes=[
            held,
            pltpu.VMEM((8, 128, 128), BF16),
            pltpu.SemaphoreType.DMA((14,)),
            pltpu.SemaphoreType.DMA((4,)),
        ],
    )(place, *matrices, *here, *(swap(piece, "c") for piece in here))

    quads = shape((4, seq + 16, 512), BF16)
    projected, adapters = call(
        project_kernel,
        (quads, grads_block),
        interpret,
        48,
        in_specs=[vmem] * 4 + [hbm],
        out_specs=(hbm, vmem),
        scratch_shapes=[
            held,
            pltpu.VMEM((seq, 1024), BF16),
            pltpu.VMEM((seq, 1024), BF16),
            pltpu.VMEM(quads.shape, BF16),
            pltpu.SemaphoreType.DMA((4,)),
            pltpu.SemaphoreType.DMA((4,)),
        ],
    )(gathered, gain, adapters, swap(adapters, "c"), weights)
    projected = lax.all_to_all(projected, QUAD, 0, 0)
    grads, inv_rms = call(
        functools.partial(attention_kernel, width),
        (quads, shape((seq, 128), F32)),
        interpret,
        48,
        out_specs=(hbm, vmem),
        scratch_shapes=[pltpu.VMEM(quads.shape[1:], BF16), pltpu.SemaphoreType.DMA((4,))],
    )(projected)
    grads = lax.all_to_all(grads, QUAD, 0, 0)
    octets = shape((8, 2 * seq + 16, 128), BF16)
    outward, adapters = call(
        spread_kernel,
        (octets, grads_block),
        interpret,
        48,
        in_specs=[vmem, vmem, hbm],
        out_specs=(hbm, vmem),
        scratch_shapes=[
            held,
            pltpu.VMEM((seq, 1024), F32),
            pltpu.VMEM((seq, 1024), F32),
            pltpu.VMEM(octets.shape, BF16),
            pltpu.SemaphoreType.DMA((4,)),
            pltpu.SemaphoreType.DMA((8,)),
        ],
    )(grads, adapters, weights)
    inward = lax.all_to_all(outward, OCTET, 0, 0)
    adapters = adapters + swap(adapters, "x", 2)
    adapters = adapters + swap(adapters, "x", 1)
    in_first, second_grad, down_grad, up_grad = call(
        functools.partial(finish_kernel, width),
        (block, block, shape((RANK, 128), F32), shape((RANK, 128), F32)),
        interpret,
    )(inward, inv_rms, out_first, in_second, grad_second, gain_local, adapters, swap(adapters, "yh"))
    return (in_first, in_second, first_grad, second_grad, down_grad.T, up_grad)


def over(mesh, interpret=False):
    rows, columns = P(SEQS, PLANE), P(None, PLANE)
    return jax.shard_map(
        functools.partial(shards, interpret),
        mesh=mesh,
        in_specs=(rows, rows, rows, rows, P(), columns, columns, columns, P(PLANE, None), P(PLANE, None), columns),
        out_specs=(rows, rows, rows, rows, P(PLANE, None), columns),
        check_vma=False,
    )


def solution(mesh):
    devices = mesh.devices.reshape(2, 4, 2, 2, 2, 4, 2)
    return over(Mesh(devices, SEQS + PLANE))
```

```python
import functools

import jax
import jax.numpy as jnp
from jax import lax
from jax.experimental import pallas as pl
from jax.experimental.pallas import tpu as pltpu
from jax.sharding import Mesh, PartitionSpec as P

HEAD_DIM = 128
RANK = 64
EPS = 1e-05
MASKED = -1e30

QUAD = ("yb", "zb")
OCTET = ("ya", "za")
PLANE = ("ya", "yb", "za", "zb")
SEQS = ("yh", "x", "c")
QKV, OUT = slice(0, 384), slice(384, 512)
F32 = jnp.float32
BF16 = jnp.bfloat16


def dot(a, b, dims=((1,), (0,)), precision=None):
    return lax.dot_general(a, b, (dims, ((), ())), preferred_element_type=F32, precision=precision)


NT = ((1,), (1,))
TN = ((0,), (0,))


def row_sums(wide):
    sums = dot(jnp.ones((8, 128), F32), wide, NT, lax.Precision.HIGHEST)
    lead = sums.astype(BF16)
    rest = (sums - lead.astype(F32)).astype(BF16)
    return lead, rest


def to_column(row):
    return jnp.broadcast_to(row, (128, row.shape[1])).T


def call(body, out_shapes, interpret, vmem=16, **kwargs):
    return pl.pallas_call(
        body,
        out_shape=out_shapes,
        compiler_params=pltpu.CompilerParams(vmem_limit_bytes=vmem * 1024 * 1024),
        interpret=interpret,
        **kwargs,
    )


def fetch(pairs, sems):
    copies = [pltpu.make_async_copy(src, dst, sems.at[i]) for i, (src, dst) in enumerate(pairs)]
    for copy in copies:
        copy.start()
    return copies


def bottleneck_kernel(first_ref, gsecond_ref, downt_ref, up_ref, partial_ref, first, gsecond, downt, up, sems):
    copies = fetch(((downt_ref, downt), (up_ref, up), (first_ref, first), (gsecond_ref, gsecond)), sems)
    for copy in copies:
        copy.wait()
    partial_ref[:, :RANK] = dot(first[...], downt[...], NT)
    partial_ref[:, RANK:] = dot(gsecond[...], up[...], NT)


def pack_kernel(
    place_ref, query_ref, key_ref, value_ref, output_ref, own_ref, one_ref, two_ref, three_ref, outs, sems, out_sems
):
    core, quad, plane = place_ref[0], place_ref[1], place_ref[2]
    pairs, out_pairs, targets = [], [], []

    def out_tile(y, yb, z, zb, target):
        start = (((y * 2 + yb) * 4 + z) * 2 + zb) * 128
        out_pairs.append((output_ref.at[:, pl.ds(pl.multiple_of(start, 128), 128)], outs.at[len(targets)]))
        targets.append(target)

    for k, piece in ((1, one_ref), (2, two_ref), (3, three_ref)):
        yb, zb = lax.div(quad, 2) ^ (k // 2), lax.rem(quad, 2) ^ (k % 2)
        for w, matrix in enumerate((query_ref, key_ref, value_ref)):
            pairs.append((matrix.at[core, yb, plane, zb], piece.at[:, w * 128 : w * 128 + 128]))
        out_tile(core, yb, plane, zb, piece)
    yb, zb = lax.div(quad, 2), lax.rem(quad, 2)
    for y in range(2):
        for w, matrix in enumerate((query_ref, key_ref, value_ref)):
            pairs.append((matrix.at[y, yb, :, zb], own_ref.at[y * 4 : y * 4 + 4, :, w * 128 : w * 128 + 128]))
        for z in range(4):
            out_tile(y, yb, z, zb, own_ref.at[y * 4 + z])
    out_copies = fetch(out_pairs, out_sems)
    copies = fetch(pairs, sems)
    eye = (
        lax.broadcasted_iota(jnp.int32, (128, 128), 0) == lax.broadcasted_iota(jnp.int32, (128, 128), 1)
    ).astype(BF16)
    for i, (copy, target) in enumerate(zip(out_copies, targets)):
        copy.wait()
        target[:, OUT] = dot(eye, outs[i], NT).astype(BF16)
    for copy in copies:
        copy.wait()


def gather_weights(place_ref, refs, weights, sems):
    core, plane = place_ref[0], place_ref[2]
    pairs = [(refs[0], weights.at[0])]
    for k in range(1, 4):
        for i, ref in enumerate(refs[1:]):
            f = (core ^ (i // 4)) * 4 + lax.rem(plane + 4 - i % 4, 4)
            pairs.append((ref.at[k - 1], weights.at[k, f]))
    copies = fetch(pairs, sems)
    return [copies[:1]] + [copies[8 * k - 7 : 8 * k + 1] for k in range(1, 4)]


def add_up_kernel(terms_ref, out_ref):
    total = jnp.sum(terms_ref[...], 0)
    for i in range(out_ref.shape[0]):
        out_ref[i] = total


def adapter_kernel(
    sums_ref, first_ref, second_ref, gfirst_ref, gsecond_ref, up_ref, downt_ref,
    shared_ref, in_second_ref, first_grad_ref, adapters_ref,
):
    seq = first_ref.shape[0]
    sums = sums_ref[...]
    pre_act = sums[:, :RANK]
    back_sum = pltpu.roll(sums, RANK, 1)[:, :RANK]
    logistic = 1.0 / (1.0 + jnp.exp(-pre_act))
    activation = (pre_act * logistic).astype(BF16)
    pre_grad = (back_sum * (logistic * (1.0 + pre_act * (1.0 - logistic)))).astype(BF16)
    in_second = (second_ref[...].astype(F32) - dot(activation, up_ref[...])).astype(BF16)
    first_grad = (gfirst_ref[...].astype(F32) + dot(pre_grad, downt_ref[...])).astype(BF16)
    in_second_ref[...] = in_second
    first_grad_ref[...] = first_grad
    for s in range(8):
        shared_ref[s, :seq] = in_second
        shared_ref[s, seq:] = first_grad
    adapters_ref[:RANK] = dot(pre_grad, first_ref[...], TN)
    adapters_ref[RANK:] = dot(activation, gsecond_ref[...], TN)


def project_kernel(place_ref, gathered_ref, gain_ref, adapters_ref, arrived_ref, *refs):
    partial_ref, adapters_out_ref, weights, x_ref, g_ref, out, in_sems, out_sems = refs[9:]
    seq, quad = x_ref.shape[0], place_ref[1]
    arriving = gather_weights(place_ref, refs[:9], weights, in_sems)
    adapters_out_ref[...] = adapters_ref[...] + arrived_ref[...]
    squares = jnp.zeros((seq, 128), F32)
    for f in range(8):
        lanes = slice(f * 128, f * 128 + 128)
        wide = gathered_ref[f, :seq].astype(F32)
        squares = squares + wide * wide
        x_ref[:, lanes] = (wide * gain_ref[f : f + 1, :]).astype(BF16)
        g_ref[:, lanes] = gathered_ref[f, seq:]
    lead, rest = row_sums(squares)
    tail = jnp.concatenate([lead, rest], 0)
    leaving = []
    for k in range(4):
        h = quad ^ k
        for copy in arriving[k]:
            copy.wait()
        out[k, :seq, QKV] = dot(x_ref[...], weights[k, :, :, QKV].reshape(1024, 384)).astype(BF16)
        out[k, :seq, OUT] = dot(g_ref[...], weights[k, :, :, OUT].reshape(1024, 128)).astype(BF16)
        out[k, seq:, :seq] = tail
        out[k, seq:, seq:] = jnp.zeros((16, 512 - seq), BF16)
        leaving.append(pltpu.make_async_copy(out.at[k], partial_ref.at[h], out_sems.at[k]))
        leaving[-1].start()
    for copy in leaving:
        copy.wait()


def attention_kernel(width, partial_ref, grads_ref, inv_ref, out, sems):
    seq = inv_ref.shape[0]
    scale = HEAD_DIM ** (-0.5)

    def total(lo, hi):
        rows = partial_ref[0, :seq, lo:hi].astype(F32)
        for s in range(1, 4):
            rows = rows + partial_ref[s, :seq, lo:hi].astype(F32)
        return rows

    square = jnp.zeros((1, seq), F32)
    for s in range(4):
        tail = partial_ref[s, seq:, :seq].astype(F32)
        square = square + tail[:1] + tail[8:9]
    inv = to_column(lax.rsqrt(square / width + EPS))
    inv_ref[...] = inv
    query_wide, key_wide, value_wide = total(0, 128) * inv, total(128, 256) * inv, total(256, 384) * inv
    query, key, value = query_wide.astype(BF16), key_wide.astype(BF16), value_wide.astype(BF16)
    back_ctx = total(384, 512).astype(BF16)
    scores = dot(query, key, NT) * scale
    query_pos = lax.broadcasted_iota(jnp.int32, (seq, seq), 0)
    key_pos = lax.broadcasted_iota(jnp.int32, (seq, seq), 1)
    scores = jnp.where(key_pos <= query_pos, scores, MASKED)
    weights = jnp.exp(scores - jnp.max(scores, axis=1, keepdims=True))
    probs = (weights / jnp.sum(weights, axis=1, keepdims=True)).astype(BF16)
    context = dot(probs, value).astype(BF16)
    value_grad = dot(probs, back_ctx, TN).astype(BF16)
    prob_grad = dot(back_ctx, value, NT)
    prob_wide = probs.astype(F32)
    inner = jnp.sum(prob_grad * prob_wide, axis=1, keepdims=True)
    score_grad = (prob_wide * (prob_grad - inner) * scale).astype(BF16)
    query_grad = dot(score_grad, key).astype(BF16)
    key_grad = dot(score_grad, query, TN).astype(BF16)
    stat = (
        query_grad.astype(F32) * query_wide + key_grad.astype(F32) * key_wide + value_grad.astype(F32) * value_wide
    )
    lead, rest = row_sums(stat)
    tail = jnp.concatenate([lead, rest], 0)
    out[:seq, :128] = query_grad
    out[:seq, 128:256] = key_grad
    out[:seq, 256:384] = value_grad
    out[:seq, OUT] = context
    out[seq:, :seq] = tail
    out[seq:, seq:] = jnp.zeros((16, 512 - seq), BF16)
    for copy in fetch([(out, grads_ref.at[s]) for s in range(4)], sems):
        copy.wait()


def spread_kernel(place_ref, grads_ref, adapters_ref, *refs):
    terms_ref, adapters_out_ref, weights, norm, attn, out, in_sems, out_sems = refs[9:]
    quad = place_ref[1]
    arriving = gather_weights(place_ref, refs[:9], weights, in_sems)
    adapters_out_ref[...] = adapters_ref[...]
    seq = grads_ref.shape[1] - 16
    stat = jnp.zeros((8, seq), F32)
    for h in range(4):
        tail = grads_ref[h, seq:, :seq].astype(F32)
        stat = stat + tail[:8] + tail[8:]
    halves = []
    for lanes in (slice(0, 128), slice(128, 256)):
        lead = stat[:4, lanes].astype(BF16)
        halves += [lead, (stat[:4, lanes] - lead.astype(F32)).astype(BF16)]
    tail = jnp.concatenate([half.astype(F32) for half in halves], 0).astype(BF16)
    for k in range(4):
        h = quad ^ k
        for copy in arriving[k]:
            copy.wait()
        into_norm = dot(grads_ref[h, :seq, QKV], weights[k, :, :, QKV].reshape(1024, 384), NT)
        into_attn = dot(grads_ref[h, :seq, OUT], weights[k, :, :, OUT].reshape(1024, 128), NT)
        norm[...] = norm[...] + into_norm if k else into_norm
        attn[...] = attn[...] + into_attn if k else into_attn
    leaving = []
    for f in range(8):
        lanes = slice(f * 128, f * 128 + 128)
        out[f, :seq] = attn[:, lanes].astype(BF16)
        out[f, seq : 2 * seq] = norm[:, lanes].astype(BF16)
        out[f, 2 * seq :] = tail
        leaving.append(pltpu.make_async_copy(out.at[f], terms_ref.at[f], out_sems.at[f]))
        leaving[-1].start()
    for copy in leaving:
        copy.wait()


def finish_kernel(
    width, terms_ref, inv_ref, first_ref, in_second_ref, gsecond_ref, gain_ref, adapters_ref, arrived_ref,
    in_first_ref, second_grad_ref, down_grad_ref, up_grad_ref,
):
    down_grad_ref[...] = adapters_ref[:RANK] + arrived_ref[:RANK]
    up_grad_ref[...] = adapters_ref[RANK:] + arrived_ref[RANK:]
    seq = first_ref.shape[0]
    total = terms_ref[0].astype(F32)
    for s in range(1, 8):
        total = total + terms_ref[s].astype(F32)
    in_first_ref[...] = (first_ref[...].astype(F32) - total[:seq]).astype(BF16)
    halves = [total[2 * seq + i : 2 * seq + i + 1] + total[2 * seq + i + 4 : 2 * seq + i + 5] for i in (0, 8)]
    stat = jnp.concatenate([to_column(half) for half in halves], 0) / width
    inv = inv_ref[...]
    gain_grad = gain_ref[...] * total[seq : 2 * seq]
    second = in_second_ref[...].astype(F32)
    second_grad_ref[...] = (gsecond_ref[...].astype(F32) + inv * (gain_grad - second * stat * inv)).astype(BF16)


def shards(
    interpret,
    out_first,
    out_second,
    grad_first,
    grad_second,
    norm_gain,
    query_proj,
    key_proj,
    value_proj,
    output_proj,
    adapter_down,
    adapter_up,
):
    seq = out_first.shape[0]
    width = query_proj.shape[0]
    shape = jax.ShapeDtypeStruct
    place = jnp.stack([lax.axis_index("c"), lax.axis_index(QUAD), lax.axis_index("x")]).astype(jnp.int32)
    smem, hbm, vmem = (pl.BlockSpec(memory_space=m) for m in (pltpu.SMEM, pltpu.HBM, pltpu.VMEM))
    down_t = adapter_down.T
    block, grads_block = shape((seq, 128), BF16), shape((2 * RANK, 128), F32)

    def swap(array, axis, bit=1):
        return lax.ppermute(array, axis, [(i, i ^ bit) for i in range(4 if axis in ("x", QUAD) else 2)])

    partial = call(
        bottleneck_kernel,
        shape((seq, 128), F32),
        interpret,
        56,
        in_specs=[hbm] * 4,
        scratch_shapes=[pltpu.VMEM((seq, 128), BF16)] * 2
        + [pltpu.VMEM((RANK, 128), BF16)] * 2
        + [pltpu.SemaphoreType.DMA((4,))],
    )(out_first, grad_second, down_t, adapter_up)
    terms = lax.all_to_all(partial.reshape(32, seq // 32, 128), PLANE, 0, 0)
    mine = call(add_up_kernel, shape(terms.shape, F32), interpret)(terms)

    tiles = (2, 2, 4, 2, 128, 128)
    matrices = (query_proj.reshape(tiles), key_proj.reshape(tiles), value_proj.reshape(tiles), output_proj)
    own, *pieces = call(
        pack_kernel,
        (shape((8, 128, 512), BF16),) + (shape((128, 512), BF16),) * 3,
        interpret,
        56,
        in_specs=[smem] + [hbm] * 4,
        scratch_shapes=[
            pltpu.VMEM((11, 128, 128), BF16),
            pltpu.SemaphoreType.DMA((15,)),
            pltpu.SemaphoreType.DMA((11,)),
        ],
    )(place, *matrices)
    fetched = jnp.stack([swap(piece, QUAD, k) for k, piece in enumerate(pieces, 1)])
    mine, fetched = lax.optimization_barrier((mine, fetched))
    here = [fetched] + [lax.ppermute(fetched, "x", [(i, (i + s) % 4) for i in range(4)]) for s in (1, 3, 2)]
    here = [here[0], here[1], here[3], here[2]]
    sums = lax.all_to_all(mine, PLANE, 0, 0).reshape(seq, 128)
    held = pltpu.VMEM((4, 8, 128, 512), BF16)

    gain = norm_gain.astype(F32).reshape(2, 2, 4, 2, 128)
    gain = lax.dynamic_index_in_dim(gain, lax.axis_index("yb"), 1, False)
    gain = lax.dynamic_index_in_dim(gain, lax.axis_index("zb"), 2, False).reshape(8, 128)
    gain_local = lax.dynamic_slice_in_dim(gain, lax.axis_index(OCTET), 1)

    shared, in_second, first_grad, adapters = call(
        adapter_kernel,
        (shape((8, 2 * seq, 128), BF16), block, block, grads_block),
        interpret,
    )(sums, out_first, out_second, grad_first, grad_second, adapter_up, down_t)
    gathered = lax.all_to_all(shared, OCTET, 0, 0)
    weights = (own, *here, *(swap(piece, "c") for piece in here))

    quads = shape((4, seq + 16, 512), BF16)
    projected, adapters = call(
        project_kernel,
        (quads, grads_block),
        interpret,
        48,
        in_specs=[smem] + [vmem] * 4 + [hbm] * 9,
        out_specs=(hbm, vmem),
        scratch_shapes=[
            held,
            pltpu.VMEM((seq, 1024), BF16),
            pltpu.VMEM((seq, 1024), BF16),
            pltpu.VMEM(quads.shape, BF16),
            pltpu.SemaphoreType.DMA((25,)),
            pltpu.SemaphoreType.DMA((4,)),
        ],
    )(place, gathered, gain, adapters, swap(adapters, "c"), *weights)

    projected = lax.all_to_all(projected, QUAD, 0, 0)
    grads, inv_rms = call(
        functools.partial(attention_kernel, width),
        (quads, shape((seq, 128), F32)),
        interpret,
        48,
        out_specs=(hbm, vmem),
        scratch_shapes=[pltpu.VMEM(quads.shape[1:], BF16), pltpu.SemaphoreType.DMA((4,))],
    )(projected)
    grads = lax.all_to_all(grads, QUAD, 0, 0)
    octets = shape((8, 2 * seq + 16, 128), BF16)
    outward, adapters = call(
        spread_kernel,
        (octets, grads_block),
        interpret,
        48,
        in_specs=[smem, vmem, vmem] + [hbm] * 9,
        out_specs=(hbm, vmem),
        scratch_shapes=[
            held,
            pltpu.VMEM((seq, 1024), F32),
            pltpu.VMEM((seq, 1024), F32),
            pltpu.VMEM(octets.shape, BF16),
            pltpu.SemaphoreType.DMA((25,)),
            pltpu.SemaphoreType.DMA((8,)),
        ],
    )(place, grads, adapters, *weights)
    inward = lax.all_to_all(outward, OCTET, 0, 0)
    adapters = adapters + swap(adapters, "x", 2)
    adapters = adapters + swap(adapters, "x", 1)
    in_first, second_grad, down_grad, up_grad = call(
        functools.partial(finish_kernel, width),
        (block, block, shape((RANK, 128), F32), shape((RANK, 128), F32)),
        interpret,
    )(inward, inv_rms, out_first, in_second, grad_second, gain_local, adapters, swap(adapters, "yh"))
    return (in_first, in_second, first_grad, second_grad, down_grad.T, up_grad)


def over(mesh, interpret=False):
    rows, columns = P(SEQS, PLANE), P(None, PLANE)
    return jax.shard_map(
        functools.partial(shards, interpret),
        mesh=mesh,
        in_specs=(rows, rows, rows, rows, P(), columns, columns, columns, P(PLANE, None), P(PLANE, None), columns),
        out_specs=(rows, rows, rows, rows, P(PLANE, None), columns),
        check_vma=False,
    )


def solution(mesh):
    devices = mesh.devices.reshape(2, 4, 2, 2, 2, 4, 2)
    return over(Mesh(devices, SEQS + PLANE))
```

```python
import functools

import jax
import jax.numpy as jnp
from jax import lax
from jax.experimental import pallas as pl
from jax.experimental.pallas import tpu as pltpu
from jax.sharding import Mesh, PartitionSpec as P

HEAD_DIM = 128
RANK = 64
EPS = 1e-05
MASKED = -1e30

QUAD = ("zb", "yb")
SQUARE = ("yb", "zb")
OCTET = ("ya", "za")
PLANE = ("ya", "yb", "za", "zb")
SEQS = ("yh", "x", "c")
QKV, OUT = slice(0, 384), slice(384, 512)
F32 = jnp.float32
BF16 = jnp.bfloat16


def dot(a, b, dims=((1,), (0,)), precision=None):
    return lax.dot_general(a, b, (dims, ((), ())), preferred_element_type=F32, precision=precision)


NT = ((1,), (1,))
TN = ((0,), (0,))


def row_sums(wide):
    sums = dot(jnp.ones((8, 128), F32), wide, NT, lax.Precision.HIGHEST)
    lead = sums.astype(BF16)
    rest = (sums - lead.astype(F32)).astype(BF16)
    return lead, rest


def to_column(row):
    return jnp.broadcast_to(row, (128, row.shape[1])).T


def call(body, out_shapes, interpret, vmem=16, **kwargs):
    return pl.pallas_call(
        body,
        out_shape=out_shapes,
        compiler_params=pltpu.CompilerParams(vmem_limit_bytes=vmem * 1024 * 1024),
        interpret=interpret,
        **kwargs,
    )


def fetch(pairs, sems):
    copies = [pltpu.make_async_copy(src, dst, sems.at[i]) for i, (src, dst) in enumerate(pairs)]
    for copy in copies:
        copy.start()
    return copies


def bottleneck_kernel(first_ref, gsecond_ref, downt_ref, up_ref, partial_ref, first, gsecond, downt, up, sems):
    copies = fetch(((downt_ref, downt), (up_ref, up), (first_ref, first), (gsecond_ref, gsecond)), sems)
    for copy in copies:
        copy.wait()
    partial_ref[:, :RANK] = dot(first[...], downt[...], NT)
    partial_ref[:, RANK:] = dot(gsecond[...], up[...], NT)


def pack_kernel(place_ref, query_ref, key_ref, value_ref, output_ref, one_ref, two_ref, three_ref, sems):
    core, quad, plane = place_ref[0], place_ref[1], place_ref[2]
    pairs = []
    for k, piece in ((1, one_ref), (2, two_ref), (3, three_ref)):
        zb, yb = lax.div(quad, 2) ^ (k // 2), lax.rem(quad, 2) ^ (k % 2)
        for w, matrix in enumerate((query_ref, key_ref, value_ref)):
            pairs.append((matrix.at[core, yb, plane, zb], piece.at[:, w * 128 : w * 128 + 128]))
        start = (((core * 2 + yb) * 4 + plane) * 2 + zb) * 128
        pairs.append((output_ref.at[:, pl.ds(pl.multiple_of(start, 128), 128)], piece.at[:, OUT]))
    for copy in fetch(pairs, sems):
        copy.wait()


def assemble_kernel(place_ref, query_ref, key_ref, value_ref, output_ref, *refs):
    pieces, (stored_ref, out_ref, own_out, sems, store_sem) = refs[:8], refs[8:]
    core, quad, plane = place_ref[0], place_ref[1], place_ref[2]
    zb, yb = lax.div(quad, 2), lax.rem(quad, 2)
    pairs = []
    for y in range(2):
        for w, matrix in enumerate((query_ref, key_ref, value_ref)):
            pairs.append(
                (matrix.at[y, yb, :, zb], out_ref.at[y * 4 : y * 4 + 4, :, w * 128 : w * 128 + 128])
            )
        for z in range(4):
            start = (((y * 2 + yb) * 4 + z) * 2 + zb) * 128
            pairs.append((output_ref.at[:, pl.ds(pl.multiple_of(start, 128), 128)], own_out.at[y * 4 + z]))
    copies = fetch(pairs, sems)
    eye = (
        lax.broadcasted_iota(jnp.int32, (128, 128), 0) == lax.broadcasted_iota(jnp.int32, (128, 128), 1)
    ).astype(BF16)
    for i, ref in enumerate(pieces):
        f = (core ^ (i // 4)) * 4 + lax.rem(plane + 4 - i % 4, 4)
        for k in (1, 2, 3):
            out_ref[f, :, k * 384 : k * 384 + 384] = ref[k - 1, :, QKV]
            out_ref[f, :, 1536 + k * 128 : 1664 + k * 128] = dot(eye, ref[k - 1, :, OUT], NT).astype(BF16)
    for copy in copies:
        copy.wait()
    for f in range(8):
        out_ref[f, :, 1536:1664] = dot(eye, own_out[f], NT).astype(BF16)
    store = pltpu.make_async_copy(out_ref, stored_ref, store_sem)
    store.start()
    store.wait()


def add_up_kernel(terms_ref, out_ref):
    total = jnp.sum(terms_ref[...], 0)
    for i in range(out_ref.shape[0]):
        out_ref[i] = total


def adapter_kernel(
    sums_ref, first_ref, second_ref, gfirst_ref, gsecond_ref, up_ref, downt_ref,
    shared_ref, in_second_ref, first_grad_ref, adapters_ref,
):
    seq = first_ref.shape[0]
    sums = sums_ref[...]
    pre_act = sums[:, :RANK]
    back_sum = pltpu.roll(sums, RANK, 1)[:, :RANK]
    logistic = 1.0 / (1.0 + jnp.exp(-pre_act))
    activation = (pre_act * logistic).astype(BF16)
    pre_grad = (back_sum * (logistic * (1.0 + pre_act * (1.0 - logistic)))).astype(BF16)
    in_second = (second_ref[...].astype(F32) - dot(activation, up_ref[...])).astype(BF16)
    first_grad = (gfirst_ref[...].astype(F32) + dot(pre_grad, downt_ref[...])).astype(BF16)
    in_second_ref[...] = in_second
    first_grad_ref[...] = first_grad
    for s in range(8):
        shared_ref[s, :seq] = in_second
        shared_ref[s, seq:] = first_grad
    adapters_ref[:RANK] = dot(pre_grad, first_ref[...], TN)
    adapters_ref[RANK:] = dot(activation, gsecond_ref[...], TN)


def project_kernel(
    place_ref, gathered_ref, gain_ref, adapters_ref, arrived_ref, weights_ref, partial_ref, adapters_out_ref,
    weights, x_ref, g_ref, out, in_sems, out_sems,
):
    seq, quad = x_ref.shape[0], place_ref[1]
    parts = [slice(k * 384, k * 384 + 384) for k in range(4)] + [slice(1536, 2048)]
    arriving = fetch([(weights_ref.at[:, :, part], weights.at[:, :, part]) for part in parts], in_sems)
    adapters_out_ref[...] = adapters_ref[...] + arrived_ref[...]
    squares = jnp.zeros((seq, 128), F32)
    for f in range(8):
        lanes = slice(f * 128, f * 128 + 128)
        wide = gathered_ref[f, :seq].astype(F32)
        squares = squares + wide * wide
        x_ref[:, lanes] = (wide * gain_ref[f : f + 1, :]).astype(BF16)
        g_ref[:, lanes] = gathered_ref[f, seq:]
    lead, rest = row_sums(squares)
    tail = jnp.concatenate([lead, rest], 0)
    for k in range(4):
        arriving[k].wait()
        out[k, :seq, QKV] = dot(x_ref[...], weights[:, :, parts[k]].reshape(1024, 384)).astype(BF16)
        out[k, seq:, :seq] = tail
        out[k, seq:, seq:] = jnp.zeros((16, 512 - seq), BF16)
    arriving[4].wait()
    ctx = dot(g_ref[...], weights[:, :, 1536:].reshape(1024, 512)).astype(BF16)
    leaving = []
    for k in range(4):
        out[k, :seq, OUT] = ctx[:, k * 128 : k * 128 + 128]
        leaving.append(pltpu.make_async_copy(out.at[k], partial_ref.at[quad ^ k], out_sems.at[k]))
        leaving[-1].start()
    for copy in leaving:
        copy.wait()


def attention_kernel(width, partial_ref, grads_ref, inv_ref, out, sems):
    seq = inv_ref.shape[0]
    scale = HEAD_DIM ** (-0.5)

    def total(lo, hi):
        rows = partial_ref[0, :seq, lo:hi].astype(F32)
        for s in range(1, 4):
            rows = rows + partial_ref[s, :seq, lo:hi].astype(F32)
        return rows

    square = jnp.zeros((1, seq), F32)
    for s in range(4):
        tail = partial_ref[s, seq:, :seq].astype(F32)
        square = square + tail[:1] + tail[8:9]
    inv = to_column(lax.rsqrt(square / width + EPS))
    inv_ref[...] = inv
    query_wide, key_wide, value_wide = total(0, 128) * inv, total(128, 256) * inv, total(256, 384) * inv
    query, key, value = query_wide.astype(BF16), key_wide.astype(BF16), value_wide.astype(BF16)
    back_ctx = total(384, 512).astype(BF16)
    scores = dot(query, key, NT) * scale
    query_pos = lax.broadcasted_iota(jnp.int32, (seq, seq), 0)
    key_pos = lax.broadcasted_iota(jnp.int32, (seq, seq), 1)
    scores = jnp.where(key_pos <= query_pos, scores, MASKED)
    weights = jnp.exp(scores - jnp.max(scores, axis=1, keepdims=True))
    probs = (weights / jnp.sum(weights, axis=1, keepdims=True)).astype(BF16)
    context = dot(probs, value).astype(BF16)
    value_grad = dot(probs, back_ctx, TN).astype(BF16)
    prob_grad = dot(back_ctx, value, NT)
    prob_wide = probs.astype(F32)
    inner = jnp.sum(prob_grad * prob_wide, axis=1, keepdims=True)
    score_grad = (prob_wide * (prob_grad - inner) * scale).astype(BF16)
    query_grad = dot(score_grad, key).astype(BF16)
    key_grad = dot(score_grad, query, TN).astype(BF16)
    stat = (
        query_grad.astype(F32) * query_wide + key_grad.astype(F32) * key_wide + value_grad.astype(F32) * value_wide
    )
    lead, rest = row_sums(stat)
    tail = jnp.concatenate([lead, rest], 0)
    out[:seq, :128] = query_grad
    out[:seq, 128:256] = key_grad
    out[:seq, 256:384] = value_grad
    out[:seq, OUT] = context
    out[seq:, :seq] = tail
    out[seq:, seq:] = jnp.zeros((16, 512 - seq), BF16)
    for copy in fetch([(out, grads_ref.at[s]) for s in range(4)], sems):
        copy.wait()


def spread_kernel(
    place_ref, grads_ref, adapters_ref, weights_ref, terms_ref, adapters_out_ref,
    weights, grads, context, out, in_sems, out_sems,
):
    quad = place_ref[1]
    arriving = fetch([(weights_ref.at[2 * j : 2 * j + 2], weights.at[2 * j : 2 * j + 2]) for j in range(4)], in_sems)
    adapters_out_ref[...] = adapters_ref[...]
    seq = grads_ref.shape[1] - 16
    stat = jnp.zeros((8, seq), F32)
    for k in range(4):
        h = quad ^ k
        grads[:, k * 384 : k * 384 + 384] = grads_ref[h, :seq, QKV]
        context[:, k * 128 : k * 128 + 128] = grads_ref[h, :seq, OUT]
        tail = grads_ref[h, seq:, :seq].astype(F32)
        stat = stat + tail[:8] + tail[8:]
    halves = []
    for lanes in (slice(0, 128), slice(128, 256)):
        lead = stat[:4, lanes].astype(BF16)
        halves += [lead, (stat[:4, lanes] - lead.astype(F32)).astype(BF16)]
    tail = jnp.concatenate([half.astype(F32) for half in halves], 0).astype(BF16)
    leaving = []
    for j in range(4):
        arriving[j].wait()
        norm = dot(grads[...], weights[2 * j : 2 * j + 2, :, :1536].reshape(256, 1536), NT).astype(BF16)
        attn = dot(context[...], weights[2 * j : 2 * j + 2, :, 1536:].reshape(256, 512), NT).astype(BF16)
        for f in (2 * j, 2 * j + 1):
            lanes = slice(f % 2 * 128, f % 2 * 128 + 128)
            out[f, :seq] = attn[:, lanes]
            out[f, seq : 2 * seq] = norm[:, lanes]
            out[f, 2 * seq :] = tail
            leaving.append(pltpu.make_async_copy(out.at[f], terms_ref.at[f], out_sems.at[f]))
            leaving[-1].start()
    for copy in leaving:
        copy.wait()


def finish_kernel(
    width, terms_ref, inv_ref, first_ref, in_second_ref, gsecond_ref, gain_ref, adapters_ref, arrived_ref,
    in_first_ref, second_grad_ref, down_grad_ref, up_grad_ref,
):
    down_grad_ref[...] = adapters_ref[:RANK] + arrived_ref[:RANK]
    up_grad_ref[...] = adapters_ref[RANK:] + arrived_ref[RANK:]
    seq = first_ref.shape[0]
    total = terms_ref[0].astype(F32)
    for s in range(1, 8):
        total = total + terms_ref[s].astype(F32)
    in_first_ref[...] = (first_ref[...].astype(F32) - total[:seq]).astype(BF16)
    halves = [total[2 * seq + i : 2 * seq + i + 1] + total[2 * seq + i + 4 : 2 * seq + i + 5] for i in (0, 8)]
    stat = jnp.concatenate([to_column(half) for half in halves], 0) / width
    inv = inv_ref[...]
    gain_grad = gain_ref[...] * total[seq : 2 * seq]
    second = in_second_ref[...].astype(F32)
    second_grad_ref[...] = (gsecond_ref[...].astype(F32) + inv * (gain_grad - second * stat * inv)).astype(BF16)


def shards(
    interpret,
    out_first,
    out_second,
    grad_first,
    grad_second,
    norm_gain,
    query_proj,
    key_proj,
    value_proj,
    output_proj,
    adapter_down,
    adapter_up,
):
    seq = out_first.shape[0]
    width = query_proj.shape[0]
    shape = jax.ShapeDtypeStruct
    place = jnp.stack([lax.axis_index("c"), lax.axis_index(QUAD), lax.axis_index("x")]).astype(jnp.int32)
    smem, hbm, vmem = (pl.BlockSpec(memory_space=m) for m in (pltpu.SMEM, pltpu.HBM, pltpu.VMEM))
    down_t = adapter_down.T
    block, grads_block = shape((seq, 128), BF16), shape((2 * RANK, 128), F32)

    def swap(array, axis, bit=1):
        return lax.ppermute(array, axis, [(i, i ^ bit) for i in range(4 if axis in ("x", SQUARE) else 2)])

    partial = call(
        bottleneck_kernel,
        shape((seq, 128), F32),
        interpret,
        56,
        in_specs=[hbm] * 4,
        scratch_shapes=[pltpu.VMEM((seq, 128), BF16)] * 2
        + [pltpu.VMEM((RANK, 128), BF16)] * 2
        + [pltpu.SemaphoreType.DMA((4,))],
    )(out_first, grad_second, down_t, adapter_up)
    terms = lax.all_to_all(partial.reshape(32, seq // 32, 128), PLANE, 0, 0)
    mine = call(add_up_kernel, shape(terms.shape, F32), interpret)(terms)

    tiles = (2, 2, 4, 2, 128, 128)
    matrices = (query_proj.reshape(tiles), key_proj.reshape(tiles), value_proj.reshape(tiles), output_proj)
    pieces = call(
        pack_kernel,
        (shape((128, 512), BF16),) * 3,
        interpret,
        56,
        in_specs=[smem] + [hbm] * 4,
        scratch_shapes=[pltpu.SemaphoreType.DMA((12,))],
    )(place, *matrices)
    fetched = jnp.stack([swap(piece, SQUARE, bit) for piece, bit in zip(pieces, (2, 1, 3))])
    mine, fetched = lax.optimization_barrier((mine, fetched))
    here = [fetched] + [lax.ppermute(fetched, "x", [(i, (i + s) % 4) for i in range(4)]) for s in (1, 3, 2)]
    here = [here[0], here[1], here[3], here[2]]
    sums = lax.all_to_all(mine, PLANE, 0, 0).reshape(seq, 128)
    held = pltpu.VMEM((8, 128, 2048), BF16)

    gain = norm_gain.astype(F32).reshape(2, 2, 4, 2, 128)
    gain = lax.dynamic_index_in_dim(gain, lax.axis_index("yb"), 1, False)
    gain = lax.dynamic_index_in_dim(gain, lax.axis_index("zb"), 2, False).reshape(8, 128)
    gain_local = lax.dynamic_slice_in_dim(gain, lax.axis_index(OCTET), 1)

    shared, in_second, first_grad, adapters = call(
        adapter_kernel,
        (shape((8, 2 * seq, 128), BF16), block, block, grads_block),
        interpret,
    )(sums, out_first, out_second, grad_first, grad_second, adapter_up, down_t)
    gathered = lax.all_to_all(shared, OCTET, 0, 0)
    weights = call(
        assemble_kernel,
        shape((8, 128, 2048), BF16),
        interpret,
        54,
        in_specs=[smem] + [hbm] * 4 + [vmem] * 8,
        out_specs=hbm,
        scratch_shapes=[
            held,
            pltpu.VMEM((8, 128, 128), BF16),
            pltpu.SemaphoreType.DMA((14,)),
            pltpu.SemaphoreType.DMA,
        ],
    )(place, *matrices, *here, *(swap(piece, "c") for piece in here))

    quads = shape((4, seq + 16, 512), BF16)
    projected, adapters = call(
        project_kernel,
        (quads, grads_block),
        interpret,
        48,
        in_specs=[smem] + [vmem] * 4 + [hbm],
        out_specs=(hbm, vmem),
        scratch_shapes=[
            held,
            pltpu.VMEM((seq, 1024), BF16),
            pltpu.VMEM((seq, 1024), BF16),
            pltpu.VMEM(quads.shape, BF16),
            pltpu.SemaphoreType.DMA((5,)),
            pltpu.SemaphoreType.DMA((4,)),
        ],
    )(place, gathered, gain, adapters, swap(adapters, "c"), weights)
    projected = lax.all_to_all(projected, QUAD, 0, 0)
    grads, inv_rms = call(
        functools.partial(attention_kernel, width),
        (quads, shape((seq, 128), F32)),
        interpret,
        48,
        out_specs=(hbm, vmem),
        scratch_shapes=[pltpu.VMEM(quads.shape[1:], BF16), pltpu.SemaphoreType.DMA((4,))],
    )(projected)
    grads = lax.all_to_all(grads, QUAD, 0, 0)
    octets = shape((8, 2 * seq + 16, 128), BF16)
    outward, adapters = call(
        spread_kernel,
        (octets, grads_block),
        interpret,
        48,
        in_specs=[smem, vmem, vmem, hbm],
        out_specs=(hbm, vmem),
        scratch_shapes=[
            held,
            pltpu.VMEM((seq, 1536), BF16),
            pltpu.VMEM((seq, 512), BF16),
            pltpu.VMEM(octets.shape, BF16),
            pltpu.SemaphoreType.DMA((4,)),
            pltpu.SemaphoreType.DMA((8,)),
        ],
    )(place, grads, adapters, weights)
    inward = lax.all_to_all(outward, OCTET, 0, 0)
    adapters = adapters + swap(adapters, "x", 2)
    adapters = adapters + swap(adapters, "x", 1)
    in_first, second_grad, down_grad, up_grad = call(
        functools.partial(finish_kernel, width),
        (block, block, shape((RANK, 128), F32), shape((RANK, 128), F32)),
        interpret,
    )(inward, inv_rms, out_first, in_second, grad_second, gain_local, adapters, swap(adapters, "yh"))
    return (in_first, in_second, first_grad, second_grad, down_grad.T, up_grad)


def over(mesh, interpret=False):
    rows, columns = P(SEQS, PLANE), P(None, PLANE)
    return jax.shard_map(
        functools.partial(shards, interpret),
        mesh=mesh,
        in_specs=(rows, rows, rows, rows, P(), columns, columns, columns, P(PLANE, None), P(PLANE, None), columns),
        out_specs=(rows, rows, rows, rows, P(PLANE, None), columns),
        check_vma=False,
    )


def solution(mesh):
    devices = mesh.devices.reshape(2, 4, 2, 2, 2, 4, 2)
    return over(Mesh(devices, SEQS + PLANE))
```

```python
import functools

import jax
import jax.numpy as jnp
from jax import lax
from jax.experimental import pallas as pl
from jax.experimental.pallas import tpu as pltpu
from jax.sharding import Mesh, PartitionSpec as P

HEAD_DIM = 128
RANK = 64
EPS = 1e-05
MASKED = -1e30

QUAD = ("yb", "zb")
OCTET = ("ya", "za")
PLANE = ("ya", "yb", "za", "zb")
SEQS = ("yh", "x", "c")
QKV, OUT = slice(0, 384), slice(384, 512)
F32 = jnp.float32
BF16 = jnp.bfloat16


def dot(a, b, dims=((1,), (0,)), precision=None):
    return lax.dot_general(a, b, (dims, ((), ())), preferred_element_type=F32, precision=precision)


NT = ((1,), (1,))
TN = ((0,), (0,))


def row_sums(wide):
    sums = dot(jnp.ones((8, 128), F32), wide, NT, lax.Precision.HIGHEST)
    lead = sums.astype(BF16)
    rest = (sums - lead.astype(F32)).astype(BF16)
    return lead, rest


def to_column(row):
    return jnp.broadcast_to(row, (128, row.shape[1])).T


def call(body, out_shapes, interpret, vmem=16, **kwargs):
    return pl.pallas_call(
        body,
        out_shape=out_shapes,
        compiler_params=pltpu.CompilerParams(vmem_limit_bytes=vmem * 1024 * 1024),
        interpret=interpret,
        **kwargs,
    )


def fetch(pairs, sems):
    copies = [pltpu.make_async_copy(src, dst, sems.at[i]) for i, (src, dst) in enumerate(pairs)]
    for copy in copies:
        copy.start()
    return copies


def share_kernel(second_ref, gfirst_ref, up_ref, downt_ref, shared_ref, streams, sems, out_sems):
    seq = second_ref.shape[0]
    copies = fetch(
        (
            (second_ref, streams.at[:seq]),
            (gfirst_ref, streams.at[seq : 2 * seq]),
            (up_ref, streams.at[2 * seq : 2 * seq + RANK]),
            (downt_ref, streams.at[2 * seq + RANK :]),
        ),
        sems,
    )
    for copy in copies:
        copy.wait()
    for copy in fetch([(streams, shared_ref.at[s]) for s in range(8)], out_sems):
        copy.wait()


def bottleneck_kernel(first_ref, gsecond_ref, downt_ref, up_ref, partial_ref, first, gsecond, downt, up, sems):
    copies = fetch(((downt_ref, downt), (up_ref, up), (first_ref, first), (gsecond_ref, gsecond)), sems)
    for copy in copies:
        copy.wait()
    partial_ref[:, :RANK] = dot(first[...], downt[...], NT)
    partial_ref[:, RANK:] = dot(gsecond[...], up[...], NT)


def pack_kernel(place_ref, query_ref, key_ref, value_ref, output_ref, one_ref, two_ref, three_ref, sems):
    core, quad, plane = place_ref[0], place_ref[1], place_ref[2]
    pairs = []
    for k, piece in ((1, one_ref), (2, two_ref), (3, three_ref)):
        yb, zb = lax.div(quad, 2) ^ (k // 2), lax.rem(quad, 2) ^ (k % 2)
        for w, matrix in enumerate((query_ref, key_ref, value_ref)):
            pairs.append((matrix.at[core, yb, plane, zb], piece.at[:, w * 128 : w * 128 + 128]))
        start = (((core * 2 + yb) * 4 + plane) * 2 + zb) * 128
        pairs.append((output_ref.at[:, pl.ds(pl.multiple_of(start, 128), 128)], piece.at[:, OUT]))
    for copy in fetch(pairs, sems):
        copy.wait()


def assemble_kernel(place_ref, query_ref, key_ref, value_ref, output_ref, *refs):
    pieces, (stored_ref, out_ref, own_out, sems, store_sems) = refs[:8], refs[8:]
    core, quad, plane = place_ref[0], place_ref[1], place_ref[2]
    yb, zb = lax.div(quad, 2), lax.rem(quad, 2)
    pairs = []
    for y in range(2):
        for w, matrix in enumerate((query_ref, key_ref, value_ref)):
            pairs.append(
                (matrix.at[y, yb, :, zb], out_ref.at[quad, y * 4 : y * 4 + 4, :, w * 128 : w * 128 + 128])
            )
        for z in range(4):
            start = (((y * 2 + yb) * 4 + z) * 2 + zb) * 128
            pairs.append((output_ref.at[:, pl.ds(pl.multiple_of(start, 128), 128)], own_out.at[y * 4 + z]))
    copies = fetch(pairs, sems)
    eye = (
        lax.broadcasted_iota(jnp.int32, (128, 128), 0) == lax.broadcasted_iota(jnp.int32, (128, 128), 1)
    ).astype(BF16)
    stores = []
    for k in (1, 2, 3):
        h = quad ^ k
        for i, ref in enumerate(pieces):
            f = (core ^ (i // 4)) * 4 + lax.rem(plane + 4 - i % 4, 4)
            out_ref[h, f, :, QKV] = ref[k - 1, :, QKV]
            out_ref[h, f, :, OUT] = dot(eye, ref[k - 1, :, OUT], NT).astype(BF16)
        stores.append(pltpu.make_async_copy(out_ref.at[h], stored_ref.at[h], store_sems.at[k]))
        stores[-1].start()
    for copy in copies:
        copy.wait()
    for f in range(8):
        out_ref[quad, f, :, OUT] = dot(eye, own_out[f], NT).astype(BF16)
    stores.append(pltpu.make_async_copy(out_ref.at[quad], stored_ref.at[quad], store_sems.at[0]))
    stores[-1].start()
    for store in stores:
        store.wait()


def add_up_kernel(terms_ref, out_ref):
    total = jnp.sum(terms_ref[...], 0)
    for i in range(out_ref.shape[0]):
        out_ref[i] = total


def bottleneck(sums):
    pre_act = sums[:, :RANK]
    back_sum = pltpu.roll(sums, RANK, 1)[:, :RANK]
    logistic = 1.0 / (1.0 + jnp.exp(-pre_act))
    activation = (pre_act * logistic).astype(BF16)
    pre_grad = (back_sum * (logistic * (1.0 + pre_act * (1.0 - logistic)))).astype(BF16)
    return activation, pre_grad


def adapter_kernel(
    sums_ref, first_ref, second_ref, gfirst_ref, gsecond_ref, up_ref, downt_ref,
    in_second_ref, first_grad_ref, adapters_ref,
):
    activation, pre_grad = bottleneck(sums_ref[...])
    in_second = (second_ref[...].astype(F32) - dot(activation, up_ref[...])).astype(BF16)
    first_grad = (gfirst_ref[...].astype(F32) + dot(pre_grad, downt_ref[...])).astype(BF16)
    in_second_ref[...] = in_second
    first_grad_ref[...] = first_grad
    adapters_ref[:RANK] = dot(pre_grad, first_ref[...], TN)
    adapters_ref[RANK:] = dot(activation, gsecond_ref[...], TN)


def project_kernel(
    sums_ref, gathered_ref, gain_ref, weights_ref, partial_ref, weights, x_ref, g_ref, out, in_sems, out_sems
):
    arriving = fetch([(weights_ref.at[h], weights.at[h]) for h in range(4)], in_sems)
    activation, pre_grad = bottleneck(sums_ref[...])
    seq = x_ref.shape[0]
    squares = jnp.zeros((seq, 128), F32)
    for f in range(8):
        lanes = slice(f * 128, f * 128 + 128)
        wide = gathered_ref[f, :seq].astype(F32) - dot(activation, gathered_ref[f, 2 * seq : 2 * seq + RANK])
        wide = wide.astype(BF16).astype(F32)
        squares = squares + wide * wide
        x_ref[:, lanes] = (wide * gain_ref[f : f + 1, :]).astype(BF16)
        wide = gathered_ref[f, seq : 2 * seq].astype(F32) + dot(pre_grad, gathered_ref[f, 2 * seq + RANK :])
        g_ref[:, lanes] = wide.astype(BF16)
    lead, rest = row_sums(squares)
    tail = jnp.concatenate([lead, rest], 0)
    leaving = []
    for h in range(4):
        arriving[h].wait()
        out[h, :seq, QKV] = dot(x_ref[...], weights[h, :, :, QKV].reshape(1024, 384)).astype(BF16)
        out[h, :seq, OUT] = dot(g_ref[...], weights[h, :, :, OUT].reshape(1024, 128)).astype(BF16)
        out[h, seq:, :seq] = tail
        out[h, seq:, seq:] = jnp.zeros((16, 512 - seq), BF16)
        leaving.append(pltpu.make_async_copy(out.at[h], partial_ref.at[h], out_sems.at[h]))
        leaving[-1].start()
    for copy in leaving:
        copy.wait()


def attention_kernel(width, partial_ref, grads_ref, inv_ref, out, sems):
    seq = inv_ref.shape[0]
    scale = HEAD_DIM ** (-0.5)

    def total(lo, hi):
        rows = partial_ref[0, :seq, lo:hi].astype(F32)
        for s in range(1, 4):
            rows = rows + partial_ref[s, :seq, lo:hi].astype(F32)
        return rows

    square = jnp.zeros((1, seq), F32)
    for s in range(4):
        tail = partial_ref[s, seq:, :seq].astype(F32)
        square = square + tail[:1] + tail[8:9]
    inv = to_column(lax.rsqrt(square / width + EPS))
    inv_ref[...] = inv
    query_wide, key_wide, value_wide = total(0, 128) * inv, total(128, 256) * inv, total(256, 384) * inv
    query, key, value = query_wide.astype(BF16), key_wide.astype(BF16), value_wide.astype(BF16)
    back_ctx = total(384, 512).astype(BF16)
    scores = dot(query, key, NT) * scale
    query_pos = lax.broadcasted_iota(jnp.int32, (seq, seq), 0)
    key_pos = lax.broadcasted_iota(jnp.int32, (seq, seq), 1)
    scores = jnp.where(key_pos <= query_pos, scores, MASKED)
    weights = jnp.exp(scores - jnp.max(scores, axis=1, keepdims=True))
    probs = (weights / jnp.sum(weights, axis=1, keepdims=True)).astype(BF16)
    context = dot(probs, value).astype(BF16)
    value_grad = dot(probs, back_ctx, TN).astype(BF16)
    prob_grad = dot(back_ctx, value, NT)
    prob_wide = probs.astype(F32)
    inner = jnp.sum(prob_grad * prob_wide, axis=1, keepdims=True)
    score_grad = (prob_wide * (prob_grad - inner) * scale).astype(BF16)
    query_grad = dot(score_grad, key).astype(BF16)
    key_grad = dot(score_grad, query, TN).astype(BF16)
    stat = (
        query_grad.astype(F32) * query_wide + key_grad.astype(F32) * key_wide + value_grad.astype(F32) * value_wide
    )
    lead, rest = row_sums(stat)
    tail = jnp.concatenate([lead, rest], 0)
    out[:seq, :128] = query_grad
    out[:seq, 128:256] = key_grad
    out[:seq, 256:384] = value_grad
    out[:seq, OUT] = context
    out[seq:, :seq] = tail
    out[seq:, seq:] = jnp.zeros((16, 512 - seq), BF16)
    for copy in fetch([(out, grads_ref.at[s]) for s in range(4)], sems):
        copy.wait()


def spread_kernel(
    grads_ref, adapters_ref, arrived_ref, weights_ref, terms_ref, adapters_out_ref,
    weights, norm, attn, out, in_sems, out_sems,
):
    arriving = fetch([(weights_ref.at[h], weights.at[h]) for h in range(4)], in_sems)
    adapters_out_ref[...] = adapters_ref[...] + arrived_ref[...]
    seq = grads_ref.shape[1] - 16
    stat = jnp.zeros((8, seq), F32)
    for h in range(4):
        tail = grads_ref[h, seq:, :seq].astype(F32)
        stat = stat + tail[:8] + tail[8:]
    halves = []
    for lanes in (slice(0, 128), slice(128, 256)):
        lead = stat[:4, lanes].astype(BF16)
        halves += [lead, (stat[:4, lanes] - lead.astype(F32)).astype(BF16)]
    tail = jnp.concatenate([half.astype(F32) for half in halves], 0).astype(BF16)
    for h in range(4):
        arriving[h].wait()
        into_norm = dot(grads_ref[h, :seq, QKV], weights[h, :, :, QKV].reshape(1024, 384), NT)
        into_attn = dot(grads_ref[h, :seq, OUT], weights[h, :, :, OUT].reshape(1024, 128), NT)
        norm[...] = norm[...] + into_norm if h else into_norm
        attn[...] = attn[...] + into_attn if h else into_attn
    leaving = []
    for f in range(8):
        lanes = slice(f * 128, f * 128 + 128)
        out[f, :seq] = attn[:, lanes].astype(BF16)
        out[f, seq : 2 * seq] = norm[:, lanes].astype(BF16)
        out[f, 2 * seq :] = tail
        leaving.append(pltpu.make_async_copy(out.at[f], terms_ref.at[f], out_sems.at[f]))
        leaving[-1].start()
    for copy in leaving:
        copy.wait()


def finish_kernel(
    width, terms_ref, inv_ref, first_ref, in_second_ref, gsecond_ref, gain_ref, adapters_ref, arrived_ref,
    in_first_ref, second_grad_ref, down_grad_ref, up_grad_ref,
):
    down_grad_ref[...] = adapters_ref[:RANK] + arrived_ref[:RANK]
    up_grad_ref[...] = adapters_ref[RANK:] + arrived_ref[RANK:]
    seq = first_ref.shape[0]
    total = terms_ref[0].astype(F32)
    for s in range(1, 8):
        total = total + terms_ref[s].astype(F32)
    in_first_ref[...] = (first_ref[...].astype(F32) - total[:seq]).astype(BF16)
    halves = [total[2 * seq + i : 2 * seq + i + 1] + total[2 * seq + i + 4 : 2 * seq + i + 5] for i in (0, 8)]
    stat = jnp.concatenate([to_column(half) for half in halves], 0) / width
    inv = inv_ref[...]
    gain_grad = gain_ref[...] * total[seq : 2 * seq]
    second = in_second_ref[...].astype(F32)
    second_grad_ref[...] = (gsecond_ref[...].astype(F32) + inv * (gain_grad - second * stat * inv)).astype(BF16)


def shards(
    interpret,
    out_first,
    out_second,
    grad_first,
    grad_second,
    norm_gain,
    query_proj,
    key_proj,
    value_proj,
    output_proj,
    adapter_down,
    adapter_up,
):
    seq = out_first.shape[0]
    width = query_proj.shape[0]
    shape = jax.ShapeDtypeStruct
    place = jnp.stack([lax.axis_index("c"), lax.axis_index(QUAD), lax.axis_index("x")]).astype(jnp.int32)
    smem, hbm, vmem = (pl.BlockSpec(memory_space=m) for m in (pltpu.SMEM, pltpu.HBM, pltpu.VMEM))
    down_t = adapter_down.T
    block, grads_block = shape((seq, 128), BF16), shape((2 * RANK, 128), F32)

    def swap(array, axis, bit=1):
        return lax.ppermute(array, axis, [(i, i ^ bit) for i in range(4 if axis in ("x", QUAD) else 2)])

    streams = (2 * seq + 2 * RANK, 128)
    shared = call(
        share_kernel,
        shape((8, *streams), BF16),
        interpret,
        56,
        in_specs=[hbm] * 4,
        out_specs=hbm,
        scratch_shapes=[pltpu.VMEM(streams, BF16), pltpu.SemaphoreType.DMA((4,)), pltpu.SemaphoreType.DMA((8,))],
    )(out_second, grad_first, adapter_up, down_t)
    gathered = lax.all_to_all(shared, OCTET, 0, 0)

    tiles = (2, 2, 4, 2, 128, 128)
    matrices = (query_proj.reshape(tiles), key_proj.reshape(tiles), value_proj.reshape(tiles), output_proj)
    pieces = call(
        pack_kernel,
        (shape((128, 512), BF16),) * 3,
        interpret,
        56,
        in_specs=[smem] + [hbm] * 4,
        scratch_shapes=[pltpu.SemaphoreType.DMA((12,))],
    )(place, *matrices)
    fetched = jnp.stack([swap(piece, QUAD, k) for k, piece in enumerate(pieces, 1)])
    here = [fetched] + [lax.ppermute(fetched, "x", [(i, (i + s) % 4) for i in range(4)]) for s in (1, 3, 2)]
    here = [here[0], here[1], here[3], here[2]]

    partial = call(
        bottleneck_kernel,
        shape((seq, 128), F32),
        interpret,
        56,
        in_specs=[hbm] * 4,
        scratch_shapes=[pltpu.VMEM((seq, 128), BF16)] * 2
        + [pltpu.VMEM((RANK, 128), BF16)] * 2
        + [pltpu.SemaphoreType.DMA((4,))],
    )(out_first, grad_second, down_t, adapter_up)
    there = [swap(here[s], "c") for s in (0, 1, 3)]
    partial, gathered, here, there = lax.optimization_barrier((partial, gathered, here, there))
    terms = lax.all_to_all(partial.reshape(32, seq // 32, 128), PLANE, 0, 0)
    mine = call(add_up_kernel, shape(terms.shape, F32), interpret)(terms)

    there.insert(2, swap(here[2], "c"))
    sums = lax.all_to_all(mine, PLANE, 0, 0).reshape(seq, 128)
    held = pltpu.VMEM((4, 8, 128, 512), BF16)

    gain = norm_gain.astype(F32).reshape(2, 2, 4, 2, 128)
    gain = lax.dynamic_index_in_dim(gain, lax.axis_index("yb"), 1, False)
    gain = lax.dynamic_index_in_dim(gain, lax.axis_index("zb"), 2, False).reshape(8, 128)
    gain_local = lax.dynamic_slice_in_dim(gain, lax.axis_index(OCTET), 1)

    in_second, first_grad, adapters = call(
        adapter_kernel,
        (block, block, grads_block),
        interpret,
    )(sums, out_first, out_second, grad_first, grad_second, adapter_up, down_t)
    weights = call(
        assemble_kernel,
        shape((4, 8, 128, 512), BF16),
        interpret,
        54,
        in_specs=[smem] + [hbm] * 4 + [vmem] * 8,
        out_specs=hbm,
        scratch_shapes=[
            held,
            pltpu.VMEM((8, 128, 128), BF16),
            pltpu.SemaphoreType.DMA((14,)),
            pltpu.SemaphoreType.DMA((4,)),
        ],
    )(place, *matrices, *here, *there)

    quads = shape((4, seq + 16, 512), BF16)
    projected = call(
        project_kernel,
        quads,
        interpret,
        48,
        in_specs=[vmem] * 3 + [hbm],
        out_specs=hbm,
        scratch_shapes=[
            held,
            pltpu.VMEM((seq, 1024), BF16),
            pltpu.VMEM((seq, 1024), BF16),
            pltpu.VMEM(quads.shape, BF16),
            pltpu.SemaphoreType.DMA((4,)),
            pltpu.SemaphoreType.DMA((4,)),
        ],
    )(sums, gathered, gain, weights)
    projected = lax.all_to_all(projected, QUAD, 0, 0)
    grads, inv_rms = call(
        functools.partial(attention_kernel, width),
        (quads, shape((seq, 128), F32)),
        interpret,
        48,
        out_specs=(hbm, vmem),
        scratch_shapes=[pltpu.VMEM(quads.shape[1:], BF16), pltpu.SemaphoreType.DMA((4,))],
    )(projected)
    grads = lax.all_to_all(grads, QUAD, 0, 0)
    octets = shape((8, 2 * seq + 16, 128), BF16)
    outward, adapters = call(
        spread_kernel,
        (octets, grads_block),
        interpret,
        48,
        in_specs=[vmem, vmem, vmem, hbm],
        out_specs=(hbm, vmem),
        scratch_shapes=[
            held,
            pltpu.VMEM((seq, 1024), F32),
            pltpu.VMEM((seq, 1024), F32),
            pltpu.VMEM(octets.shape, BF16),
            pltpu.SemaphoreType.DMA((4,)),
            pltpu.SemaphoreType.DMA((8,)),
        ],
    )(grads, adapters, swap(adapters, "c"), weights)
    inward = lax.all_to_all(outward, OCTET, 0, 0)
    adapters = adapters + swap(adapters, "x", 2)
    adapters = adapters + swap(adapters, "x", 1)
    in_first, second_grad, down_grad, up_grad = call(
        functools.partial(finish_kernel, width),
        (block, block, shape((RANK, 128), F32), shape((RANK, 128), F32)),
        interpret,
    )(inward, inv_rms, out_first, in_second, grad_second, gain_local, adapters, swap(adapters, "yh"))
    return (in_first, in_second, first_grad, second_grad, down_grad.T, up_grad)


def over(mesh, interpret=False):
    rows, columns = P(SEQS, PLANE), P(None, PLANE)
    return jax.shard_map(
        functools.partial(shards, interpret),
        mesh=mesh,
        in_specs=(rows, rows, rows, rows, P(), columns, columns, columns, P(PLANE, None), P(PLANE, None), columns),
        out_specs=(rows, rows, rows, rows, P(PLANE, None), columns),
        check_vma=False,
    )


def solution(mesh):
    devices = mesh.devices.reshape(2, 4, 2, 2, 2, 4, 2)
    return over(Mesh(devices, SEQS + PLANE))
```

```python
import functools

import jax
import jax.numpy as jnp
from jax import lax
from jax.experimental import pallas as pl
from jax.experimental.pallas import tpu as pltpu
from jax.sharding import Mesh, PartitionSpec as P

HEAD_DIM = 128
RANK = 64
EPS = 1e-05
MASKED = -1e30

QUAD = ("yb", "zb")
OCTET = ("ya", "za")
PLANE = ("ya", "yb", "za", "zb")
SEQS = ("yh", "x", "c")
QKV, OUT = slice(0, 384), slice(384, 512)
F32 = jnp.float32
BF16 = jnp.bfloat16


def dot(a, b, dims=((1,), (0,)), precision=None):
    return lax.dot_general(a, b, (dims, ((), ())), preferred_element_type=F32, precision=precision)


NT = ((1,), (1,))
TN = ((0,), (0,))


def row_sums(wide):
    sums = dot(jnp.ones((8, 128), F32), wide, NT, lax.Precision.HIGHEST)
    lead = sums.astype(BF16)
    rest = (sums - lead.astype(F32)).astype(BF16)
    return lead, rest


def to_column(row):
    return jnp.broadcast_to(row, (128, row.shape[1])).T


def call(body, out_shapes, interpret, vmem=16, **kwargs):
    return pl.pallas_call(
        body,
        out_shape=out_shapes,
        compiler_params=pltpu.CompilerParams(vmem_limit_bytes=vmem * 1024 * 1024),
        interpret=interpret,
        **kwargs,
    )


def fetch(pairs, sems):
    copies = [pltpu.make_async_copy(src, dst, sems.at[i]) for i, (src, dst) in enumerate(pairs)]
    for copy in copies:
        copy.start()
    return copies


def bottleneck_kernel(first_ref, gsecond_ref, downt_ref, up_ref, partial_ref, first, gsecond, downt, up, sems):
    copies = fetch(((downt_ref, downt), (up_ref, up), (first_ref, first), (gsecond_ref, gsecond)), sems)
    for copy in copies:
        copy.wait()
    partial_ref[:, :RANK] = dot(first[...], downt[...], NT)
    partial_ref[:, RANK:] = dot(gsecond[...], up[...], NT)


def pack_kernel(place_ref, query_ref, key_ref, value_ref, output_ref, one_ref, two_ref, three_ref, sems):
    core, quad, plane = place_ref[0], place_ref[1], place_ref[2]
    pairs = []
    for k, piece in ((1, one_ref), (2, two_ref), (3, three_ref)):
        yb, zb = lax.div(quad, 2) ^ (k // 2), lax.rem(quad, 2) ^ (k % 2)
        for w, matrix in enumerate((query_ref, key_ref, value_ref)):
            pairs.append((matrix.at[core, yb, plane, zb], piece.at[:, w * 128 : w * 128 + 128]))
        start = (((core * 2 + yb) * 4 + plane) * 2 + zb) * 128
        pairs.append((output_ref.at[:, pl.ds(pl.multiple_of(start, 128), 128)], piece.at[:, OUT]))
    for copy in fetch(pairs, sems):
        copy.wait()


def assemble_kernel(place_ref, query_ref, key_ref, value_ref, output_ref, *refs):
    pieces, (stored_ref, out_ref, own_out, sems, store_sems) = refs[:8], refs[8:]
    core, quad, plane = place_ref[0], place_ref[1], place_ref[2]
    yb, zb = lax.div(quad, 2), lax.rem(quad, 2)
    pairs = []
    for y in range(2):
        for w, matrix in enumerate((query_ref, key_ref, value_ref)):
            pairs.append(
                (matrix.at[y, yb, :, zb], out_ref.at[quad, y * 4 : y * 4 + 4, :, w * 128 : w * 128 + 128])
            )
        for z in range(4):
            start = (((y * 2 + yb) * 4 + z) * 2 + zb) * 128
            pairs.append((output_ref.at[:, pl.ds(pl.multiple_of(start, 128), 128)], own_out.at[y * 4 + z]))
    copies = fetch(pairs, sems)
    eye = (
        lax.broadcasted_iota(jnp.int32, (128, 128), 0) == lax.broadcasted_iota(jnp.int32, (128, 128), 1)
    ).astype(BF16)
    stores = []
    for k in (1, 2, 3):
        h = quad ^ k
        for i, ref in enumerate(pieces):
            f = (core ^ (i // 4)) * 4 + lax.rem(plane + 4 - i % 4, 4)
            out_ref[h, f, :, QKV] = ref[k - 1, :, QKV]
            out_ref[h, f, :, OUT] = dot(eye, ref[k - 1, :, OUT], NT).astype(BF16)
        stores.append(pltpu.make_async_copy(out_ref.at[h], stored_ref.at[h], store_sems.at[k]))
        stores[-1].start()
    for copy in copies:
        copy.wait()
    for f in range(8):
        out_ref[quad, f, :, OUT] = dot(eye, own_out[f], NT).astype(BF16)
    stores.append(pltpu.make_async_copy(out_ref.at[quad], stored_ref.at[quad], store_sems.at[0]))
    stores[-1].start()
    for store in stores:
        store.wait()


def add_up_kernel(terms_ref, out_ref):
    total = jnp.sum(terms_ref[...], 0)
    for i in range(out_ref.shape[0]):
        out_ref[i] = total


def adapter_kernel(
    sums_ref, first_ref, second_ref, gfirst_ref, gsecond_ref, up_ref, downt_ref,
    shared_ref, in_second_ref, first_grad_ref, adapters_ref,
):
    seq = first_ref.shape[0]
    sums = sums_ref[...]
    pre_act = sums[:, :RANK]
    back_sum = pltpu.roll(sums, RANK, 1)[:, :RANK]
    logistic = 1.0 / (1.0 + jnp.exp(-pre_act))
    activation = (pre_act * logistic).astype(BF16)
    pre_grad = (back_sum * (logistic * (1.0 + pre_act * (1.0 - logistic)))).astype(BF16)
    in_second = (second_ref[...].astype(F32) - dot(activation, up_ref[...])).astype(BF16)
    first_grad = (gfirst_ref[...].astype(F32) + dot(pre_grad, downt_ref[...])).astype(BF16)
    in_second_ref[...] = in_second
    first_grad_ref[...] = first_grad
    for s in range(8):
        shared_ref[s, :seq] = in_second
        shared_ref[s, seq:] = first_grad
    adapters_ref[:RANK] = dot(pre_grad, first_ref[...], TN)
    adapters_ref[RANK:] = dot(activation, gsecond_ref[...], TN)


def project_kernel(
    gathered_ref, gain_ref, adapters_ref, arrived_ref, weights_ref, partial_ref, adapters_out_ref,
    weights, x_ref, g_ref, out, in_sems, out_sems,
):
    seq = x_ref.shape[0]
    arriving = fetch([(weights_ref.at[h], weights.at[h]) for h in range(4)], in_sems)
    adapters_out_ref[...] = adapters_ref[...] + arrived_ref[...]
    squares = jnp.zeros((seq, 128), F32)
    for f in range(8):
        lanes = slice(f * 128, f * 128 + 128)
        wide = gathered_ref[f, :seq].astype(F32)
        squares = squares + wide * wide
        x_ref[:, lanes] = (wide * gain_ref[f : f + 1, :]).astype(BF16)
        g_ref[:, lanes] = gathered_ref[f, seq:]
    lead, rest = row_sums(squares)
    tail = jnp.concatenate([lead, rest], 0)
    leaving = []
    for h in range(4):
        arriving[h].wait()
        out[h, :seq, QKV] = dot(x_ref[...], weights[h, :, :, QKV].reshape(1024, 384)).astype(BF16)
        out[h, :seq, OUT] = dot(g_ref[...], weights[h, :, :, OUT].reshape(1024, 128)).astype(BF16)
        out[h, seq:, :seq] = tail
        out[h, seq:, seq:] = jnp.zeros((16, 512 - seq), BF16)
        leaving.append(pltpu.make_async_copy(out.at[h], partial_ref.at[h], out_sems.at[h]))
        leaving[-1].start()
    for copy in leaving:
        copy.wait()


def attention_kernel(width, partial_ref, grads_ref, inv_ref, out, sems):
    seq = inv_ref.shape[0]
    scale = HEAD_DIM ** (-0.5)

    def total(lo, hi):
        rows = partial_ref[0, :seq, lo:hi].astype(F32)
        for s in range(1, 4):
            rows = rows + partial_ref[s, :seq, lo:hi].astype(F32)
        return rows

    square = jnp.zeros((1, seq), F32)
    for s in range(4):
        tail = partial_ref[s, seq:, :seq].astype(F32)
        square = square + tail[:1] + tail[8:9]
    inv = to_column(lax.rsqrt(square / width + EPS))
    inv_ref[...] = inv
    query_wide, key_wide, value_wide = total(0, 128) * inv, total(128, 256) * inv, total(256, 384) * inv
    query, key, value = query_wide.astype(BF16), key_wide.astype(BF16), value_wide.astype(BF16)
    back_ctx = total(384, 512).astype(BF16)
    scores = dot(query, key, NT) * scale
    query_pos = lax.broadcasted_iota(jnp.int32, (seq, seq), 0)
    key_pos = lax.broadcasted_iota(jnp.int32, (seq, seq), 1)
    scores = jnp.where(key_pos <= query_pos, scores, MASKED)
    weights = jnp.exp(scores - jnp.max(scores, axis=1, keepdims=True))
    probs = (weights / jnp.sum(weights, axis=1, keepdims=True)).astype(BF16)
    context = dot(probs, value).astype(BF16)
    value_grad = dot(probs, back_ctx, TN).astype(BF16)
    prob_grad = dot(back_ctx, value, NT)
    prob_wide = probs.astype(F32)
    inner = jnp.sum(prob_grad * prob_wide, axis=1, keepdims=True)
    score_grad = (prob_wide * (prob_grad - inner) * scale).astype(BF16)
    query_grad = dot(score_grad, key).astype(BF16)
    key_grad = dot(score_grad, query, TN).astype(BF16)
    stat = (
        query_grad.astype(F32) * query_wide + key_grad.astype(F32) * key_wide + value_grad.astype(F32) * value_wide
    )
    lead, rest = row_sums(stat)
    tail = jnp.concatenate([lead, rest], 0)
    out[:seq, :128] = query_grad
    out[:seq, 128:256] = key_grad
    out[:seq, 256:384] = value_grad
    out[:seq, OUT] = context
    out[seq:, :seq] = tail
    out[seq:, seq:] = jnp.zeros((16, 512 - seq), BF16)
    for copy in fetch([(out, grads_ref.at[s]) for s in range(4)], sems):
        copy.wait()


def spread_kernel(
    grads_ref, adapters_ref, weights_ref, terms_ref, adapters_out_ref,
    weights, norm, attn, out, in_sems, out_sems,
):
    arriving = fetch([(weights_ref.at[h], weights.at[h]) for h in range(4)], in_sems)
    adapters_out_ref[...] = adapters_ref[...]
    seq = grads_ref.shape[1] - 16
    stat = jnp.zeros((8, seq), F32)
    for h in range(4):
        tail = grads_ref[h, seq:, :seq].astype(F32)
        stat = stat + tail[:8] + tail[8:]
    halves = []
    for lanes in (slice(0, 128), slice(128, 256)):
        lead = stat[:4, lanes].astype(BF16)
        halves += [lead, (stat[:4, lanes] - lead.astype(F32)).astype(BF16)]
    tail = jnp.concatenate([half.astype(F32) for half in halves], 0).astype(BF16)
    for h in range(4):
        arriving[h].wait()
        into_norm = dot(grads_ref[h, :seq, QKV], weights[h, :, :, QKV].reshape(1024, 384), NT)
        into_attn = dot(grads_ref[h, :seq, OUT], weights[h, :, :, OUT].reshape(1024, 128), NT)
        norm[...] = norm[...] + into_norm if h else into_norm
        attn[...] = attn[...] + into_attn if h else into_attn
    leaving = []
    for f in range(8):
        lanes = slice(f * 128, f * 128 + 128)
        out[f, :seq] = attn[:, lanes].astype(BF16)
        out[f, seq : 2 * seq] = norm[:, lanes].astype(BF16)
        out[f, 2 * seq :] = tail
        leaving.append(pltpu.make_async_copy(out.at[f], terms_ref.at[f], out_sems.at[f]))
        leaving[-1].start()
    for copy in leaving:
        copy.wait()


def finish_kernel(
    width, terms_ref, inv_ref, first_ref, in_second_ref, gsecond_ref, gain_ref, adapters_ref, arrived_ref,
    in_first_ref, second_grad_ref, down_grad_ref, up_grad_ref,
):
    down_grad_ref[...] = adapters_ref[:RANK] + arrived_ref[:RANK]
    up_grad_ref[...] = adapters_ref[RANK:] + arrived_ref[RANK:]
    seq = first_ref.shape[0]
    total = terms_ref[0].astype(F32)
    for s in range(1, 8):
        total = total + terms_ref[s].astype(F32)
    in_first_ref[...] = (first_ref[...].astype(F32) - total[:seq]).astype(BF16)
    halves = [total[2 * seq + i : 2 * seq + i + 1] + total[2 * seq + i + 4 : 2 * seq + i + 5] for i in (0, 8)]
    stat = jnp.concatenate([to_column(half) for half in halves], 0) / width
    inv = inv_ref[...]
    gain_grad = gain_ref[...] * total[seq : 2 * seq]
    second = in_second_ref[...].astype(F32)
    second_grad_ref[...] = (gsecond_ref[...].astype(F32) + inv * (gain_grad - second * stat * inv)).astype(BF16)


def shards(
    interpret,
    out_first,
    out_second,
    grad_first,
    grad_second,
    norm_gain,
    query_proj,
    key_proj,
    value_proj,
    output_proj,
    adapter_down,
    adapter_up,
):
    seq = out_first.shape[0]
    width = query_proj.shape[0]
    shape = jax.ShapeDtypeStruct
    place = jnp.stack([lax.axis_index("c"), lax.axis_index(QUAD), lax.axis_index("x")]).astype(jnp.int32)
    smem, hbm, vmem = (pl.BlockSpec(memory_space=m) for m in (pltpu.SMEM, pltpu.HBM, pltpu.VMEM))
    down_t = adapter_down.T
    block, grads_block = shape((seq, 128), BF16), shape((2 * RANK, 128), F32)

    def swap(array, axis, bit=1):
        return lax.ppermute(array, axis, [(i, i ^ bit) for i in range(4 if axis in ("x", QUAD) else 2)])

    partial = call(
        bottleneck_kernel,
        shape((seq, 128), F32),
        interpret,
        56,
        in_specs=[hbm] * 4,
        scratch_shapes=[pltpu.VMEM((seq, 128), BF16)] * 2
        + [pltpu.VMEM((RANK, 128), BF16)] * 2
        + [pltpu.SemaphoreType.DMA((4,))],
    )(out_first, grad_second, down_t, adapter_up)
    terms = lax.all_to_all(partial.reshape(32, seq // 32, 128), PLANE, 0, 0)
    mine = call(add_up_kernel, shape(terms.shape, F32), interpret)(terms)

    tiles = (2, 2, 4, 2, 128, 128)
    matrices = (query_proj.reshape(tiles), key_proj.reshape(tiles), value_proj.reshape(tiles), output_proj)
    pieces = call(
        pack_kernel,
        (shape((128, 512), BF16),) * 3,
        interpret,
        56,
        in_specs=[smem] + [hbm] * 4,
        scratch_shapes=[pltpu.SemaphoreType.DMA((12,))],
    )(place, *matrices)
    mine, pieces = lax.optimization_barrier((mine, pieces))
    fetched = [swap(piece, QUAD, k) for k, piece in enumerate(pieces, 1)]
    sums = lax.all_to_all(mine, PLANE, 0, 0).reshape(seq, 128)
    sums, fetched = lax.optimization_barrier((sums, fetched))
    fetched = jnp.stack(fetched)
    here = [fetched] + [lax.ppermute(fetched, "x", [(i, (i + s) % 4) for i in range(4)]) for s in (1, 3, 2)]
    here = [here[0], here[1], here[3], here[2]]
    held = pltpu.VMEM((4, 8, 128, 512), BF16)

    gain = norm_gain.astype(F32).reshape(2, 2, 4, 2, 128)
    gain = lax.dynamic_index_in_dim(gain, lax.axis_index("yb"), 1, False)
    gain = lax.dynamic_index_in_dim(gain, lax.axis_index("zb"), 2, False).reshape(8, 128)
    gain_local = lax.dynamic_slice_in_dim(gain, lax.axis_index(OCTET), 1)

    shared, in_second, first_grad, adapters = call(
        adapter_kernel,
        (shape((8, 2 * seq, 128), BF16), block, block, grads_block),
        interpret,
    )(sums, out_first, out_second, grad_first, grad_second, adapter_up, down_t)
    gathered = lax.all_to_all(shared, OCTET, 0, 0)
    weights = call(
        assemble_kernel,
        shape((4, 8, 128, 512), BF16),
        interpret,
        54,
        in_specs=[smem] + [hbm] * 4 + [vmem] * 8,
        out_specs=hbm,
        scratch_shapes=[
            held,
            pltpu.VMEM((8, 128, 128), BF16),
            pltpu.SemaphoreType.DMA((14,)),
            pltpu.SemaphoreType.DMA((4,)),
        ],
    )(place, *matrices, *here, *(swap(piece, "c") for piece in here))

    quads = shape((4, seq + 16, 512), BF16)
    projected, adapters = call(
        project_kernel,
        (quads, grads_block),
        interpret,
        48,
        in_specs=[vmem] * 4 + [hbm],
        out_specs=(hbm, vmem),
        scratch_shapes=[
            held,
            pltpu.VMEM((seq, 1024), BF16),
            pltpu.VMEM((seq, 1024), BF16),
            pltpu.VMEM(quads.shape, BF16),
            pltpu.SemaphoreType.DMA((4,)),
            pltpu.SemaphoreType.DMA((4,)),
        ],
    )(gathered, gain, adapters, swap(adapters, "c"), weights)
    projected = lax.all_to_all(projected, QUAD, 0, 0)
    grads, inv_rms = call(
        functools.partial(attention_kernel, width),
        (quads, shape((seq, 128), F32)),
        interpret,
        48,
        out_specs=(hbm, vmem),
        scratch_shapes=[pltpu.VMEM(quads.shape[1:], BF16), pltpu.SemaphoreType.DMA((4,))],
    )(projected)
    grads = lax.all_to_all(grads, QUAD, 0, 0)
    octets = shape((8, 2 * seq + 16, 128), BF16)
    outward, adapters = call(
        spread_kernel,
        (octets, grads_block),
        interpret,
        48,
        in_specs=[vmem, vmem, hbm],
        out_specs=(hbm, vmem),
        scratch_shapes=[
            held,
            pltpu.VMEM((seq, 1024), F32),
            pltpu.VMEM((seq, 1024), F32),
            pltpu.VMEM(octets.shape, BF16),
            pltpu.SemaphoreType.DMA((4,)),
            pltpu.SemaphoreType.DMA((8,)),
        ],
    )(grads, adapters, weights)
    inward = lax.all_to_all(outward, OCTET, 0, 0)
    adapters = adapters + swap(adapters, "x", 2)
    adapters = adapters + swap(adapters, "x", 1)
    in_first, second_grad, down_grad, up_grad = call(
        functools.partial(finish_kernel, width),
        (block, block, shape((RANK, 128), F32), shape((RANK, 128), F32)),
        interpret,
    )(inward, inv_rms, out_first, in_second, grad_second, gain_local, adapters, swap(adapters, "yh"))
    return (in_first, in_second, first_grad, second_grad, down_grad.T, up_grad)


def over(mesh, interpret=False):
    rows, columns = P(SEQS, PLANE), P(None, PLANE)
    return jax.shard_map(
        functools.partial(shards, interpret),
        mesh=mesh,
        in_specs=(rows, rows, rows, rows, P(), columns, columns, columns, P(PLANE, None), P(PLANE, None), columns),
        out_specs=(rows, rows, rows, rows, P(PLANE, None), columns),
        check_vma=False,
    )


def solution(mesh):
    devices = mesh.devices.reshape(2, 4, 2, 2, 2, 4, 2)
    return over(Mesh(devices, SEQS + PLANE))
```

```python
import functools

import jax
import jax.numpy as jnp
from jax import lax
from jax.experimental import pallas as pl
from jax.experimental.pallas import tpu as pltpu
from jax.sharding import Mesh, PartitionSpec as P

HEAD_DIM = 128
RANK = 64
EPS = 1e-05
MASKED = -1e30

QUAD = ("yb", "zb")
OCTET = ("ya", "za")
PLANE = ("ya", "yb", "za", "zb")
SEQS = ("yh", "x", "c")
QKV, OUT = slice(0, 384), slice(384, 512)
F32 = jnp.float32
BF16 = jnp.bfloat16


def dot(a, b, dims=((1,), (0,)), precision=None):
    return lax.dot_general(a, b, (dims, ((), ())), preferred_element_type=F32, precision=precision)


NT = ((1,), (1,))
TN = ((0,), (0,))


def row_sums(wide):
    sums = dot(jnp.ones((8, 128), F32), wide, NT, lax.Precision.HIGHEST)
    lead = sums.astype(BF16)
    rest = (sums - lead.astype(F32)).astype(BF16)
    return lead, rest


def to_column(row):
    return jnp.broadcast_to(row, (128, row.shape[1])).T


def call(body, out_shapes, interpret, vmem=16, **kwargs):
    return pl.pallas_call(
        body,
        out_shape=out_shapes,
        compiler_params=pltpu.CompilerParams(vmem_limit_bytes=vmem * 1024 * 1024),
        interpret=interpret,
        **kwargs,
    )


def fetch(pairs, sems):
    copies = [pltpu.make_async_copy(src, dst, sems.at[i]) for i, (src, dst) in enumerate(pairs)]
    for copy in copies:
        copy.start()
    return copies


def bottleneck_kernel(first_ref, gsecond_ref, downt_ref, up_ref, partial_ref, first, gsecond, downt, up, sems):
    copies = fetch(((downt_ref, downt), (up_ref, up), (first_ref, first), (gsecond_ref, gsecond)), sems)
    for copy in copies:
        copy.wait()
    partial_ref[:, :RANK] = dot(first[...], downt[...], NT)
    partial_ref[:, RANK:] = dot(gsecond[...], up[...], NT)


def pack_kernel(
    place_ref, query_ref, key_ref, value_ref, output_ref, own_ref, one_ref, two_ref, three_ref, outs, sems, out_sems
):
    core, quad, plane = place_ref[0], place_ref[1], place_ref[2]
    pairs, out_pairs, targets = [], [], []

    def out_tile(y, yb, z, zb, target):
        start = (((y * 2 + yb) * 4 + z) * 2 + zb) * 128
        out_pairs.append((output_ref.at[:, pl.ds(pl.multiple_of(start, 128), 128)], outs.at[len(targets)]))
        targets.append(target)

    for k, piece in ((1, one_ref), (2, two_ref), (3, three_ref)):
        yb, zb = lax.div(quad, 2) ^ (k // 2), lax.rem(quad, 2) ^ (k % 2)
        for w, matrix in enumerate((query_ref, key_ref, value_ref)):
            pairs.append((matrix.at[core, yb, plane, zb], piece.at[:, w * 128 : w * 128 + 128]))
        out_tile(core, yb, plane, zb, piece)
    yb, zb = lax.div(quad, 2), lax.rem(quad, 2)
    for y in range(2):
        for w, matrix in enumerate((query_ref, key_ref, value_ref)):
            pairs.append((matrix.at[y, yb, :, zb], own_ref.at[y * 4 : y * 4 + 4, :, w * 128 : w * 128 + 128]))
        for z in range(4):
            out_tile(y, yb, z, zb, own_ref.at[y * 4 + z])
    out_copies = fetch(out_pairs, out_sems)
    copies = fetch(pairs, sems)
    eye = (
        lax.broadcasted_iota(jnp.int32, (128, 128), 0) == lax.broadcasted_iota(jnp.int32, (128, 128), 1)
    ).astype(BF16)
    for i, (copy, target) in enumerate(zip(out_copies, targets)):
        copy.wait()
        target[:, OUT] = dot(eye, outs[i], NT).astype(BF16)
    for copy in copies:
        copy.wait()


def assemble_kernel(place_ref, *refs):
    pieces, (out_ref, sems) = refs[:8], refs[8:]
    core, plane = place_ref[0], place_ref[2]
    pairs = []
    for i, ref in enumerate(pieces):
        f = (core ^ (i // 4)) * 4 + lax.rem(plane + 4 - i % 4, 4)
        pairs.append((ref, out_ref.at[:, f]))
    for copy in fetch(pairs, sems):
        copy.wait()


def fetch_heads(own_ref, rest_ref, weights, sems):
    return fetch([(own_ref, weights.at[0])] + [(rest_ref.at[k - 1], weights.at[k]) for k in (1, 2, 3)], sems)


def add_up_kernel(terms_ref, out_ref):
    total = jnp.sum(terms_ref[...], 0)
    for i in range(out_ref.shape[0]):
        out_ref[i] = total


def adapter_kernel(
    sums_ref, first_ref, second_ref, gfirst_ref, gsecond_ref, up_ref, downt_ref,
    shared_ref, in_second_ref, first_grad_ref, adapters_ref,
):
    seq = first_ref.shape[0]
    sums = sums_ref[...]
    pre_act = sums[:, :RANK]
    back_sum = pltpu.roll(sums, RANK, 1)[:, :RANK]
    logistic = 1.0 / (1.0 + jnp.exp(-pre_act))
    activation = (pre_act * logistic).astype(BF16)
    pre_grad = (back_sum * (logistic * (1.0 + pre_act * (1.0 - logistic)))).astype(BF16)
    in_second = (second_ref[...].astype(F32) - dot(activation, up_ref[...])).astype(BF16)
    first_grad = (gfirst_ref[...].astype(F32) + dot(pre_grad, downt_ref[...])).astype(BF16)
    in_second_ref[...] = in_second
    first_grad_ref[...] = first_grad
    for s in range(8):
        shared_ref[s, :seq] = in_second
        shared_ref[s, seq:] = first_grad
    adapters_ref[:RANK] = dot(pre_grad, first_ref[...], TN)
    adapters_ref[RANK:] = dot(activation, gsecond_ref[...], TN)


def project_kernel(
    place_ref, gathered_ref, gain_ref, own_ref, rest_ref, partial_ref,
    weights, x_ref, g_ref, out, in_sems, out_sems,
):
    seq, quad = x_ref.shape[0], place_ref[1]
    arriving = fetch_heads(own_ref, rest_ref, weights, in_sems)
    squares = jnp.zeros((seq, 128), F32)
    for f in range(8):
        lanes = slice(f * 128, f * 128 + 128)
        wide = gathered_ref[f, :seq].astype(F32)
        squares = squares + wide * wide
        x_ref[:, lanes] = (wide * gain_ref[f : f + 1, :]).astype(BF16)
        g_ref[:, lanes] = gathered_ref[f, seq:]
    lead, rest = row_sums(squares)
    tail = jnp.concatenate([lead, rest], 0)
    leaving = []
    for k in range(4):
        arriving[k].wait()
        out[k, :seq, QKV] = dot(x_ref[...], weights[k, :, :, QKV].reshape(1024, 384)).astype(BF16)
        out[k, :seq, OUT] = dot(g_ref[...], weights[k, :, :, OUT].reshape(1024, 128)).astype(BF16)
        out[k, seq:, :seq] = tail
        out[k, seq:, seq:] = jnp.zeros((16, 512 - seq), BF16)
        leaving.append(pltpu.make_async_copy(out.at[k], partial_ref.at[quad ^ k], out_sems.at[k]))
        leaving[-1].start()
    for copy in leaving:
        copy.wait()


def attention_kernel(width, partial_ref, grads_ref, inv_ref, out, sems):
    seq = inv_ref.shape[0]
    scale = HEAD_DIM ** (-0.5)

    def total(lo, hi):
        rows = partial_ref[0, :seq, lo:hi].astype(F32)
        for s in range(1, 4):
            rows = rows + partial_ref[s, :seq, lo:hi].astype(F32)
        return rows

    square = jnp.zeros((1, seq), F32)
    for s in range(4):
        tail = partial_ref[s, seq:, :seq].astype(F32)
        square = square + tail[:1] + tail[8:9]
    inv = to_column(lax.rsqrt(square / width + EPS))
    inv_ref[...] = inv
    query_wide, key_wide, value_wide = total(0, 128) * inv, total(128, 256) * inv, total(256, 384) * inv
    query, key, value = query_wide.astype(BF16), key_wide.astype(BF16), value_wide.astype(BF16)
    back_ctx = total(384, 512).astype(BF16)
    scores = dot(query, key, NT) * scale
    query_pos = lax.broadcasted_iota(jnp.int32, (seq, seq), 0)
    key_pos = lax.broadcasted_iota(jnp.int32, (seq, seq), 1)
    scores = jnp.where(key_pos <= query_pos, scores, MASKED)
    weights = jnp.exp(scores - jnp.max(scores, axis=1, keepdims=True))
    probs = (weights / jnp.sum(weights, axis=1, keepdims=True)).astype(BF16)
    context = dot(probs, value).astype(BF16)
    value_grad = dot(probs, back_ctx, TN).astype(BF16)
    prob_grad = dot(back_ctx, value, NT)
    prob_wide = probs.astype(F32)
    inner = jnp.sum(prob_grad * prob_wide, axis=1, keepdims=True)
    score_grad = (prob_wide * (prob_grad - inner) * scale).astype(BF16)
    query_grad = dot(score_grad, key).astype(BF16)
    key_grad = dot(score_grad, query, TN).astype(BF16)
    stat = (
        query_grad.astype(F32) * query_wide + key_grad.astype(F32) * key_wide + value_grad.astype(F32) * value_wide
    )
    lead, rest = row_sums(stat)
    tail = jnp.concatenate([lead, rest], 0)
    out[:seq, :128] = query_grad
    out[:seq, 128:256] = key_grad
    out[:seq, 256:384] = value_grad
    out[:seq, OUT] = context
    out[seq:, :seq] = tail
    out[seq:, seq:] = jnp.zeros((16, 512 - seq), BF16)
    for copy in fetch([(out, grads_ref.at[s]) for s in range(4)], sems):
        copy.wait()


def spread_kernel(
    place_ref, grads_ref, adapters_ref, arrived_ref, own_ref, rest_ref, terms_ref, adapters_out_ref,
    weights, norm, attn, out, in_sems, out_sems,
):
    quad = place_ref[1]
    arriving = fetch_heads(own_ref, rest_ref, weights, in_sems)
    adapters_out_ref[...] = adapters_ref[...] + arrived_ref[...]
    seq = grads_ref.shape[1] - 16
    stat = jnp.zeros((8, seq), F32)
    for h in range(4):
        tail = grads_ref[h, seq:, :seq].astype(F32)
        stat = stat + tail[:8] + tail[8:]
    halves = []
    for lanes in (slice(0, 128), slice(128, 256)):
        lead = stat[:4, lanes].astype(BF16)
        halves += [lead, (stat[:4, lanes] - lead.astype(F32)).astype(BF16)]
    tail = jnp.concatenate([half.astype(F32) for half in halves], 0).astype(BF16)
    for k in range(4):
        h = quad ^ k
        arriving[k].wait()
        into_norm = dot(grads_ref[h, :seq, QKV], weights[k, :, :, QKV].reshape(1024, 384), NT)
        into_attn = dot(grads_ref[h, :seq, OUT], weights[k, :, :, OUT].reshape(1024, 128), NT)
        norm[...] = norm[...] + into_norm if k else into_norm
        attn[...] = attn[...] + into_attn if k else into_attn
    leaving = []
    for f in range(8):
        lanes = slice(f * 128, f * 128 + 128)
        out[f, :seq] = attn[:, lanes].astype(BF16)
        out[f, seq : 2 * seq] = norm[:, lanes].astype(BF16)
        out[f, 2 * seq :] = tail
        leaving.append(pltpu.make_async_copy(out.at[f], terms_ref.at[f], out_sems.at[f]))
        leaving[-1].start()
    for copy in leaving:
        copy.wait()


def finish_kernel(
    width, terms_ref, inv_ref, first_ref, in_second_ref, gsecond_ref, gain_ref, adapters_ref, arrived_ref,
    in_first_ref, second_grad_ref, down_grad_ref, up_grad_ref,
):
    down_grad_ref[...] = adapters_ref[:RANK] + arrived_ref[:RANK]
    up_grad_ref[...] = adapters_ref[RANK:] + arrived_ref[RANK:]
    seq = first_ref.shape[0]
    total = terms_ref[0].astype(F32)
    for s in range(1, 8):
        total = total + terms_ref[s].astype(F32)
    in_first_ref[...] = (first_ref[...].astype(F32) - total[:seq]).astype(BF16)
    halves = [total[2 * seq + i : 2 * seq + i + 1] + total[2 * seq + i + 4 : 2 * seq + i + 5] for i in (0, 8)]
    stat = jnp.concatenate([to_column(half) for half in halves], 0) / width
    inv = inv_ref[...]
    gain_grad = gain_ref[...] * total[seq : 2 * seq]
    second = in_second_ref[...].astype(F32)
    second_grad_ref[...] = (gsecond_ref[...].astype(F32) + inv * (gain_grad - second * stat * inv)).astype(BF16)


def shards(
    interpret,
    out_first,
    out_second,
    grad_first,
    grad_second,
    norm_gain,
    query_proj,
    key_proj,
    value_proj,
    output_proj,
    adapter_down,
    adapter_up,
):
    seq = out_first.shape[0]
    width = query_proj.shape[0]
    shape = jax.ShapeDtypeStruct
    place = jnp.stack([lax.axis_index("c"), lax.axis_index(QUAD), lax.axis_index("x")]).astype(jnp.int32)
    smem, hbm, vmem = (pl.BlockSpec(memory_space=m) for m in (pltpu.SMEM, pltpu.HBM, pltpu.VMEM))
    down_t = adapter_down.T
    block, grads_block = shape((seq, 128), BF16), shape((2 * RANK, 128), F32)

    def swap(array, axis, bit=1):
        return lax.ppermute(array, axis, [(i, i ^ bit) for i in range(4 if axis in ("x", QUAD) else 2)])

    partial = call(
        bottleneck_kernel,
        shape((seq, 128), F32),
        interpret,
        56,
        in_specs=[hbm] * 4,
        scratch_shapes=[pltpu.VMEM((seq, 128), BF16)] * 2
        + [pltpu.VMEM((RANK, 128), BF16)] * 2
        + [pltpu.SemaphoreType.DMA((4,))],
    )(out_first, grad_second, down_t, adapter_up)
    terms = lax.all_to_all(partial.reshape(32, seq // 32, 128), PLANE, 0, 0)
    mine = call(add_up_kernel, shape(terms.shape, F32), interpret)(terms)

    tiles = (2, 2, 4, 2, 128, 128)
    matrices = (query_proj.reshape(tiles), key_proj.reshape(tiles), value_proj.reshape(tiles), output_proj)
    own, *pieces = call(
        pack_kernel,
        (shape((8, 128, 512), BF16),) + (shape((128, 512), BF16),) * 3,
        interpret,
        56,
        in_specs=[smem] + [hbm] * 4,
        scratch_shapes=[
            pltpu.VMEM((11, 128, 128), BF16),
            pltpu.SemaphoreType.DMA((15,)),
            pltpu.SemaphoreType.DMA((11,)),
        ],
    )(place, *matrices)
    mine, pieces = lax.optimization_barrier((mine, pieces))
    fetched = [swap(piece, QUAD, k) for k, piece in enumerate(pieces, 1)]
    sums = lax.all_to_all(mine, PLANE, 0, 0).reshape(seq, 128)
    sums, fetched = lax.optimization_barrier((sums, fetched))
    fetched = jnp.stack(fetched)
    here = [fetched] + [lax.ppermute(fetched, "x", [(i, (i + s) % 4) for i in range(4)]) for s in (1, 3, 2)]
    here = [here[0], here[1], here[3], here[2]]
    held = pltpu.VMEM((4, 8, 128, 512), BF16)

    gain = norm_gain.astype(F32).reshape(2, 2, 4, 2, 128)
    gain = lax.dynamic_index_in_dim(gain, lax.axis_index("yb"), 1, False)
    gain = lax.dynamic_index_in_dim(gain, lax.axis_index("zb"), 2, False).reshape(8, 128)
    gain_local = lax.dynamic_slice_in_dim(gain, lax.axis_index(OCTET), 1)

    shared, in_second, first_grad, adapters = call(
        adapter_kernel,
        (shape((8, 2 * seq, 128), BF16), block, block, grads_block),
        interpret,
    )(sums, out_first, out_second, grad_first, grad_second, adapter_up, down_t)
    gathered = lax.all_to_all(shared, OCTET, 0, 0)
    rest = call(
        assemble_kernel,
        shape((3, 8, 128, 512), BF16),
        interpret,
        60,
        in_specs=[smem] + [hbm] * 8,
        out_specs=hbm,
        scratch_shapes=[pltpu.SemaphoreType.DMA((8,))],
    )(place, *here, *(swap(piece, "c") for piece in here))

    quads = shape((4, seq + 16, 512), BF16)
    projected = call(
        project_kernel,
        quads,
        interpret,
        48,
        in_specs=[smem, vmem, vmem, hbm, hbm],
        out_specs=hbm,
        scratch_shapes=[
            held,
            pltpu.VMEM((seq, 1024), BF16),
            pltpu.VMEM((seq, 1024), BF16),
            pltpu.VMEM(quads.shape, BF16),
            pltpu.SemaphoreType.DMA((4,)),
            pltpu.SemaphoreType.DMA((4,)),
        ],
    )(place, gathered, gain, own, rest)
    projected = lax.all_to_all(projected, QUAD, 0, 0)
    grads, inv_rms = call(
        functools.partial(attention_kernel, width),
        (quads, shape((seq, 128), F32)),
        interpret,
        48,
        out_specs=(hbm, vmem),
        scratch_shapes=[pltpu.VMEM(quads.shape[1:], BF16), pltpu.SemaphoreType.DMA((4,))],
    )(projected)
    grads = lax.all_to_all(grads, QUAD, 0, 0)
    octets = shape((8, 2 * seq + 16, 128), BF16)
    outward, adapters = call(
        spread_kernel,
        (octets, grads_block),
        interpret,
        48,
        in_specs=[smem, vmem, vmem, vmem, hbm, hbm],
        out_specs=(hbm, vmem),
        scratch_shapes=[
            held,
            pltpu.VMEM((seq, 1024), F32),
            pltpu.VMEM((seq, 1024), F32),
            pltpu.VMEM(octets.shape, BF16),
            pltpu.SemaphoreType.DMA((4,)),
            pltpu.SemaphoreType.DMA((8,)),
        ],
    )(place, grads, adapters, swap(adapters, "c"), own, rest)
    inward = lax.all_to_all(outward, OCTET, 0, 0)
    adapters = adapters + swap(adapters, "x", 2)
    adapters = adapters + swap(adapters, "x", 1)
    in_first, second_grad, down_grad, up_grad = call(
        functools.partial(finish_kernel, width),
        (block, block, shape((RANK, 128), F32), shape((RANK, 128), F32)),
        interpret,
    )(inward, inv_rms, out_first, in_second, grad_second, gain_local, adapters, swap(adapters, "yh"))
    return (in_first, in_second, first_grad, second_grad, down_grad.T, up_grad)


def over(mesh, interpret=False):
    rows, columns = P(SEQS, PLANE), P(None, PLANE)
    return jax.shard_map(
        functools.partial(shards, interpret),
        mesh=mesh,
        in_specs=(rows, rows, rows, rows, P(), columns, columns, columns, P(PLANE, None), P(PLANE, None), columns),
        out_specs=(rows, rows, rows, rows, P(PLANE, None), columns),
        check_vma=False,
    )


def solution(mesh):
    devices = mesh.devices.reshape(2, 4, 2, 2, 2, 4, 2)
    return over(Mesh(devices, SEQS + PLANE))
```

```python
import functools

import jax
import jax.numpy as jnp
from jax import lax
from jax.experimental import pallas as pl
from jax.experimental.pallas import tpu as pltpu
from jax.sharding import Mesh, PartitionSpec as P

HEAD_DIM = 128
RANK = 64
EPS = 1e-05
MASKED = -1e30

QUAD = ("yb", "zb")
OCTET = ("ya", "za")
PLANE = ("ya", "yb", "za", "zb")
SEQS = ("yh", "x", "c")
QKV, OUT = slice(0, 384), slice(384, 512)
F32 = jnp.float32
BF16 = jnp.bfloat16


def dot(a, b, dims=((1,), (0,)), precision=None):
    return lax.dot_general(a, b, (dims, ((), ())), preferred_element_type=F32, precision=precision)


NT = ((1,), (1,))
TN = ((0,), (0,))


def row_sums(wide):
    sums = dot(jnp.ones((8, 128), F32), wide, NT, lax.Precision.HIGHEST)
    lead = sums.astype(BF16)
    rest = (sums - lead.astype(F32)).astype(BF16)
    return lead, rest


def to_column(row):
    return jnp.broadcast_to(row, (128, row.shape[1])).T


def call(body, out_shapes, interpret, vmem=16, **kwargs):
    return pl.pallas_call(
        body,
        out_shape=out_shapes,
        compiler_params=pltpu.CompilerParams(vmem_limit_bytes=vmem * 1024 * 1024),
        interpret=interpret,
        **kwargs,
    )


def fetch(pairs, sems):
    copies = [pltpu.make_async_copy(src, dst, sems.at[i]) for i, (src, dst) in enumerate(pairs)]
    for copy in copies:
        copy.start()
    return copies


def bottleneck_kernel(first_ref, gsecond_ref, downt_ref, up_ref, partial_ref, first, gsecond, downt, up, sems):
    copies = fetch(((downt_ref, downt), (up_ref, up), (first_ref, first), (gsecond_ref, gsecond)), sems)
    for copy in copies:
        copy.wait()
    partial_ref[:, :RANK] = dot(first[...], downt[...], NT)
    partial_ref[:, RANK:] = dot(gsecond[...], up[...], NT)


def pack_kernel(
    place_ref, query_ref, key_ref, value_ref, output_ref, own_ref, one_ref, two_ref, three_ref, outs, sems, out_sems
):
    core, quad, plane = place_ref[0], place_ref[1], place_ref[2]
    pairs, out_pairs, targets = [], [], []

    def out_tile(y, yb, z, zb, target):
        start = (((y * 2 + yb) * 4 + z) * 2 + zb) * 128
        out_pairs.append((output_ref.at[:, pl.ds(pl.multiple_of(start, 128), 128)], outs.at[len(targets)]))
        targets.append(target)

    for k, piece in ((1, one_ref), (2, two_ref), (3, three_ref)):
        yb, zb = lax.div(quad, 2) ^ (k // 2), lax.rem(quad, 2) ^ (k % 2)
        for w, matrix in enumerate((query_ref, key_ref, value_ref)):
            pairs.append((matrix.at[core, yb, plane, zb], piece.at[:, w * 128 : w * 128 + 128]))
        out_tile(core, yb, plane, zb, piece)
    yb, zb = lax.div(quad, 2), lax.rem(quad, 2)
    for y in range(2):
        for w, matrix in enumerate((query_ref, key_ref, value_ref)):
            pairs.append((matrix.at[y, yb, :, zb], own_ref.at[y * 4 : y * 4 + 4, :, w * 128 : w * 128 + 128]))
        for z in range(4):
            out_tile(y, yb, z, zb, own_ref.at[y * 4 + z])
    out_copies = fetch(out_pairs, out_sems)
    copies = fetch(pairs, sems)
    eye = (
        lax.broadcasted_iota(jnp.int32, (128, 128), 0) == lax.broadcasted_iota(jnp.int32, (128, 128), 1)
    ).astype(BF16)
    for i, (copy, target) in enumerate(zip(out_copies, targets)):
        copy.wait()
        target[:, OUT] = dot(eye, outs[i], NT).astype(BF16)
    for copy in copies:
        copy.wait()


def assemble_kernel(place_ref, *refs):
    pieces, (out_ref, held, sems) = refs[:8], refs[8:]
    core, plane = place_ref[0], place_ref[2]
    copies = []
    for k in range(3):
        for i, ref in enumerate(pieces):
            held[k, (core ^ (i // 4)) * 4 + lax.rem(plane + 4 - i % 4, 4)] = ref[k]
        copies.append(pltpu.make_async_copy(held.at[k], out_ref.at[k], sems.at[k]))
        copies[-1].start()
    for copy in copies:
        copy.wait()


def fetch_heads(own_ref, rest_ref, weights, sems):
    return fetch([(own_ref, weights.at[0])] + [(rest_ref.at[k - 1], weights.at[k]) for k in (1, 2, 3)], sems)


def add_up_kernel(terms_ref, out_ref):
    total = jnp.sum(terms_ref[...], 0)
    for i in range(out_ref.shape[0]):
        out_ref[i] = total


def adapter_kernel(
    sums_ref, first_ref, second_ref, gfirst_ref, gsecond_ref, up_ref, downt_ref,
    shared_ref, in_second_ref, first_grad_ref, adapters_ref,
):
    seq = first_ref.shape[0]
    sums = sums_ref[...]
    pre_act = sums[:, :RANK]
    back_sum = pltpu.roll(sums, RANK, 1)[:, :RANK]
    logistic = 1.0 / (1.0 + jnp.exp(-pre_act))
    activation = (pre_act * logistic).astype(BF16)
    pre_grad = (back_sum * (logistic * (1.0 + pre_act * (1.0 - logistic)))).astype(BF16)
    in_second = (second_ref[...].astype(F32) - dot(activation, up_ref[...])).astype(BF16)
    first_grad = (gfirst_ref[...].astype(F32) + dot(pre_grad, downt_ref[...])).astype(BF16)
    in_second_ref[...] = in_second
    first_grad_ref[...] = first_grad
    for s in range(8):
        shared_ref[s, :seq] = in_second
        shared_ref[s, seq:] = first_grad
    adapters_ref[:RANK] = dot(pre_grad, first_ref[...], TN)
    adapters_ref[RANK:] = dot(activation, gsecond_ref[...], TN)


def project_kernel(
    place_ref, gathered_ref, gain_ref, own_ref, rest_ref, partial_ref,
    weights, x_ref, g_ref, out, in_sems, out_sems,
):
    seq, quad = x_ref.shape[0], place_ref[1]
    arriving = fetch_heads(own_ref, rest_ref, weights, in_sems)
    squares = jnp.zeros((seq, 128), F32)
    for f in range(8):
        lanes = slice(f * 128, f * 128 + 128)
        wide = gathered_ref[f, :seq].astype(F32)
        squares = squares + wide * wide
        x_ref[:, lanes] = (wide * gain_ref[f : f + 1, :]).astype(BF16)
        g_ref[:, lanes] = gathered_ref[f, seq:]
    lead, rest = row_sums(squares)
    tail = jnp.concatenate([lead, rest], 0)
    leaving = []
    for k in range(4):
        arriving[k].wait()
        out[k, :seq, QKV] = dot(x_ref[...], weights[k, :, :, QKV].reshape(1024, 384)).astype(BF16)
        out[k, :seq, OUT] = dot(g_ref[...], weights[k, :, :, OUT].reshape(1024, 128)).astype(BF16)
        out[k, seq:, :seq] = tail
        out[k, seq:, seq:] = jnp.zeros((16, 512 - seq), BF16)
        leaving.append(pltpu.make_async_copy(out.at[k], partial_ref.at[quad ^ k], out_sems.at[k]))
        leaving[-1].start()
    for copy in leaving:
        copy.wait()


def attention_kernel(width, partial_ref, grads_ref, inv_ref, out, sems):
    seq = inv_ref.shape[0]
    scale = HEAD_DIM ** (-0.5)

    def total(lo, hi):
        rows = partial_ref[0, :seq, lo:hi].astype(F32)
        for s in range(1, 4):
            rows = rows + partial_ref[s, :seq, lo:hi].astype(F32)
        return rows

    square = jnp.zeros((1, seq), F32)
    for s in range(4):
        tail = partial_ref[s, seq:, :seq].astype(F32)
        square = square + tail[:1] + tail[8:9]
    inv = to_column(lax.rsqrt(square / width + EPS))
    inv_ref[...] = inv
    query_wide, key_wide, value_wide = total(0, 128) * inv, total(128, 256) * inv, total(256, 384) * inv
    query, key, value = query_wide.astype(BF16), key_wide.astype(BF16), value_wide.astype(BF16)
    back_ctx = total(384, 512).astype(BF16)
    scores = dot(query, key, NT) * scale
    query_pos = lax.broadcasted_iota(jnp.int32, (seq, seq), 0)
    key_pos = lax.broadcasted_iota(jnp.int32, (seq, seq), 1)
    scores = jnp.where(key_pos <= query_pos, scores, MASKED)
    weights = jnp.exp(scores - jnp.max(scores, axis=1, keepdims=True))
    probs = (weights / jnp.sum(weights, axis=1, keepdims=True)).astype(BF16)
    context = dot(probs, value).astype(BF16)
    value_grad = dot(probs, back_ctx, TN).astype(BF16)
    prob_grad = dot(back_ctx, value, NT)
    prob_wide = probs.astype(F32)
    inner = jnp.sum(prob_grad * prob_wide, axis=1, keepdims=True)
    score_grad = (prob_wide * (prob_grad - inner) * scale).astype(BF16)
    query_grad = dot(score_grad, key).astype(BF16)
    key_grad = dot(score_grad, query, TN).astype(BF16)
    stat = (
        query_grad.astype(F32) * query_wide + key_grad.astype(F32) * key_wide + value_grad.astype(F32) * value_wide
    )
    lead, rest = row_sums(stat)
    tail = jnp.concatenate([lead, rest], 0)
    out[:seq, :128] = query_grad
    out[:seq, 128:256] = key_grad
    out[:seq, 256:384] = value_grad
    out[:seq, OUT] = context
    out[seq:, :seq] = tail
    out[seq:, seq:] = jnp.zeros((16, 512 - seq), BF16)
    for copy in fetch([(out, grads_ref.at[s]) for s in range(4)], sems):
        copy.wait()


def spread_kernel(
    place_ref, grads_ref, adapters_ref, arrived_ref, own_ref, rest_ref, terms_ref, adapters_out_ref,
    weights, norm, attn, out, in_sems, out_sems,
):
    quad = place_ref[1]
    arriving = fetch_heads(own_ref, rest_ref, weights, in_sems)
    adapters_out_ref[...] = adapters_ref[...] + arrived_ref[...]
    seq = grads_ref.shape[1] - 16
    stat = jnp.zeros((8, seq), F32)
    for h in range(4):
        tail = grads_ref[h, seq:, :seq].astype(F32)
        stat = stat + tail[:8] + tail[8:]
    halves = []
    for lanes in (slice(0, 128), slice(128, 256)):
        lead = stat[:4, lanes].astype(BF16)
        halves += [lead, (stat[:4, lanes] - lead.astype(F32)).astype(BF16)]
    tail = jnp.concatenate([half.astype(F32) for half in halves], 0).astype(BF16)
    for k in range(4):
        h = quad ^ k
        arriving[k].wait()
        into_norm = dot(grads_ref[h, :seq, QKV], weights[k, :, :, QKV].reshape(1024, 384), NT)
        into_attn = dot(grads_ref[h, :seq, OUT], weights[k, :, :, OUT].reshape(1024, 128), NT)
        norm[...] = norm[...] + into_norm if k else into_norm
        attn[...] = attn[...] + into_attn if k else into_attn
    leaving = []
    for f in range(8):
        lanes = slice(f * 128, f * 128 + 128)
        out[f, :seq] = attn[:, lanes].astype(BF16)
        out[f, seq : 2 * seq] = norm[:, lanes].astype(BF16)
        out[f, 2 * seq :] = tail
        leaving.append(pltpu.make_async_copy(out.at[f], terms_ref.at[f], out_sems.at[f]))
        leaving[-1].start()
    for copy in leaving:
        copy.wait()


def finish_kernel(
    width, terms_ref, inv_ref, first_ref, in_second_ref, gsecond_ref, gain_ref, adapters_ref, arrived_ref,
    in_first_ref, second_grad_ref, down_grad_ref, up_grad_ref,
):
    down_grad_ref[...] = adapters_ref[:RANK] + arrived_ref[:RANK]
    up_grad_ref[...] = adapters_ref[RANK:] + arrived_ref[RANK:]
    seq = first_ref.shape[0]
    total = terms_ref[0].astype(F32)
    for s in range(1, 8):
        total = total + terms_ref[s].astype(F32)
    in_first_ref[...] = (first_ref[...].astype(F32) - total[:seq]).astype(BF16)
    halves = [total[2 * seq + i : 2 * seq + i + 1] + total[2 * seq + i + 4 : 2 * seq + i + 5] for i in (0, 8)]
    stat = jnp.concatenate([to_column(half) for half in halves], 0) / width
    inv = inv_ref[...]
    gain_grad = gain_ref[...] * total[seq : 2 * seq]
    second = in_second_ref[...].astype(F32)
    second_grad_ref[...] = (gsecond_ref[...].astype(F32) + inv * (gain_grad - second * stat * inv)).astype(BF16)


def shards(
    interpret,
    out_first,
    out_second,
    grad_first,
    grad_second,
    norm_gain,
    query_proj,
    key_proj,
    value_proj,
    output_proj,
    adapter_down,
    adapter_up,
):
    seq = out_first.shape[0]
    width = query_proj.shape[0]
    shape = jax.ShapeDtypeStruct
    place = jnp.stack([lax.axis_index("c"), lax.axis_index(QUAD), lax.axis_index("x")]).astype(jnp.int32)
    smem, hbm, vmem = (pl.BlockSpec(memory_space=m) for m in (pltpu.SMEM, pltpu.HBM, pltpu.VMEM))
    down_t = adapter_down.T
    block, grads_block = shape((seq, 128), BF16), shape((2 * RANK, 128), F32)

    def swap(array, axis, bit=1):
        return lax.ppermute(array, axis, [(i, i ^ bit) for i in range(4 if axis in ("x", QUAD) else 2)])

    partial = call(
        bottleneck_kernel,
        shape((seq, 128), F32),
        interpret,
        56,
        in_specs=[hbm] * 4,
        scratch_shapes=[pltpu.VMEM((seq, 128), BF16)] * 2
        + [pltpu.VMEM((RANK, 128), BF16)] * 2
        + [pltpu.SemaphoreType.DMA((4,))],
    )(out_first, grad_second, down_t, adapter_up)
    terms = lax.all_to_all(partial.reshape(32, seq // 32, 128), PLANE, 0, 0)
    mine = call(add_up_kernel, shape(terms.shape, F32), interpret)(terms)

    tiles = (2, 2, 4, 2, 128, 128)
    matrices = (query_proj.reshape(tiles), key_proj.reshape(tiles), value_proj.reshape(tiles), output_proj)
    own, *pieces = call(
        pack_kernel,
        (shape((8, 128, 512), BF16),) + (shape((128, 512), BF16),) * 3,
        interpret,
        56,
        in_specs=[smem] + [hbm] * 4,
        scratch_shapes=[
            pltpu.VMEM((11, 128, 128), BF16),
            pltpu.SemaphoreType.DMA((15,)),
            pltpu.SemaphoreType.DMA((11,)),
        ],
    )(place, *matrices)
    mine, pieces = lax.optimization_barrier((mine, pieces))
    fetched = [swap(piece, QUAD, k) for k, piece in enumerate(pieces, 1)]
    sums = lax.all_to_all(mine, PLANE, 0, 0).reshape(seq, 128)
    sums, fetched = lax.optimization_barrier((sums, fetched))
    fetched = jnp.stack(fetched)
    here = [fetched] + [lax.ppermute(fetched, "x", [(i, (i + s) % 4) for i in range(4)]) for s in (1, 3, 2)]
    here = [here[0], here[1], here[3], here[2]]
    held = pltpu.VMEM((4, 8, 128, 512), BF16)

    gain = norm_gain.astype(F32).reshape(2, 2, 4, 2, 128)
    gain = lax.dynamic_index_in_dim(gain, lax.axis_index("yb"), 1, False)
    gain = lax.dynamic_index_in_dim(gain, lax.axis_index("zb"), 2, False).reshape(8, 128)
    gain_local = lax.dynamic_slice_in_dim(gain, lax.axis_index(OCTET), 1)

    shared, in_second, first_grad, adapters = call(
        adapter_kernel,
        (shape((8, 2 * seq, 128), BF16), block, block, grads_block),
        interpret,
    )(sums, out_first, out_second, grad_first, grad_second, adapter_up, down_t)
    gathered = lax.all_to_all(shared, OCTET, 0, 0)
    rest = call(
        assemble_kernel,
        shape((3, 8, 128, 512), BF16),
        interpret,
        54,
        in_specs=[smem] + [vmem] * 8,
        out_specs=hbm,
        scratch_shapes=[pltpu.VMEM((3, 8, 128, 512), BF16), pltpu.SemaphoreType.DMA((3,))],
    )(place, *here, *(swap(piece, "c") for piece in here))

    quads = shape((4, seq + 16, 512), BF16)
    projected = call(
        project_kernel,
        quads,
        interpret,
        48,
        in_specs=[smem, vmem, vmem, hbm, hbm],
        out_specs=hbm,
        scratch_shapes=[
            held,
            pltpu.VMEM((seq, 1024), BF16),
            pltpu.VMEM((seq, 1024), BF16),
            pltpu.VMEM(quads.shape, BF16),
            pltpu.SemaphoreType.DMA((4,)),
            pltpu.SemaphoreType.DMA((4,)),
        ],
    )(place, gathered, gain, own, rest)
    projected = lax.all_to_all(projected, QUAD, 0, 0)
    grads, inv_rms = call(
        functools.partial(attention_kernel, width),
        (quads, shape((seq, 128), F32)),
        interpret,
        48,
        out_specs=(hbm, vmem),
        scratch_shapes=[pltpu.VMEM(quads.shape[1:], BF16), pltpu.SemaphoreType.DMA((4,))],
    )(projected)
    grads = lax.all_to_all(grads, QUAD, 0, 0)
    octets = shape((8, 2 * seq + 16, 128), BF16)
    outward, adapters = call(
        spread_kernel,
        (octets, grads_block),
        interpret,
        48,
        in_specs=[smem, vmem, vmem, vmem, hbm, hbm],
        out_specs=(hbm, vmem),
        scratch_shapes=[
            held,
            pltpu.VMEM((seq, 1024), F32),
            pltpu.VMEM((seq, 1024), F32),
            pltpu.VMEM(octets.shape, BF16),
            pltpu.SemaphoreType.DMA((4,)),
            pltpu.SemaphoreType.DMA((8,)),
        ],
    )(place, grads, adapters, swap(adapters, "c"), own, rest)
    inward = lax.all_to_all(outward, OCTET, 0, 0)
    adapters = adapters + swap(adapters, "x", 2)
    adapters = adapters + swap(adapters, "x", 1)
    in_first, second_grad, down_grad, up_grad = call(
        functools.partial(finish_kernel, width),
        (block, block, shape((RANK, 128), F32), shape((RANK, 128), F32)),
        interpret,
    )(inward, inv_rms, out_first, in_second, grad_second, gain_local, adapters, swap(adapters, "yh"))
    return (in_first, in_second, first_grad, second_grad, down_grad.T, up_grad)


def over(mesh, interpret=False):
    rows, columns = P(SEQS, PLANE), P(None, PLANE)
    return jax.shard_map(
        functools.partial(shards, interpret),
        mesh=mesh,
        in_specs=(rows, rows, rows, rows, P(), columns, columns, columns, P(PLANE, None), P(PLANE, None), columns),
        out_specs=(rows, rows, rows, rows, P(PLANE, None), columns),
        check_vma=False,
    )


def solution(mesh):
    devices = mesh.devices.reshape(2, 4, 2, 2, 2, 4, 2)
    return over(Mesh(devices, SEQS + PLANE))
```

```python
import functools

import jax
import jax.numpy as jnp
from jax import lax
from jax.experimental import pallas as pl
from jax.experimental.pallas import tpu as pltpu
from jax.sharding import Mesh, PartitionSpec as P

HEAD_DIM = 128
RANK = 64
EPS = 1e-05
MASKED = -1e30

QUAD = ("yb", "zb")
OCTET = ("ya", "za")
PLANE = ("ya", "yb", "za", "zb")
SEQS = ("yh", "x", "c")
QKV, OUT = slice(0, 384), slice(384, 512)
F32 = jnp.float32
BF16 = jnp.bfloat16


def dot(a, b, dims=((1,), (0,)), precision=None):
    return lax.dot_general(a, b, (dims, ((), ())), preferred_element_type=F32, precision=precision)


NT = ((1,), (1,))
TN = ((0,), (0,))


def row_sums(wide):
    sums = dot(jnp.ones((8, 128), F32), wide, NT, lax.Precision.HIGHEST)
    lead = sums.astype(BF16)
    rest = (sums - lead.astype(F32)).astype(BF16)
    return lead, rest


def to_column(row):
    return jnp.broadcast_to(row, (128, row.shape[1])).T


def call(body, out_shapes, interpret, vmem=16, **kwargs):
    return pl.pallas_call(
        body,
        out_shape=out_shapes,
        compiler_params=pltpu.CompilerParams(vmem_limit_bytes=vmem * 1024 * 1024),
        interpret=interpret,
        **kwargs,
    )


def fetch(pairs, sems):
    copies = [pltpu.make_async_copy(src, dst, sems.at[i]) for i, (src, dst) in enumerate(pairs)]
    for copy in copies:
        copy.start()
    return copies


def bottleneck_kernel(first_ref, gsecond_ref, downt_ref, up_ref, partial_ref, first, gsecond, downt, up, sems):
    copies = fetch(((downt_ref, downt), (up_ref, up), (first_ref, first), (gsecond_ref, gsecond)), sems)
    for copy in copies:
        copy.wait()
    partial_ref[:, :RANK] = dot(first[...], downt[...], NT)
    partial_ref[:, RANK:] = dot(gsecond[...], up[...], NT)


def pack_kernel(
    place_ref, query_ref, key_ref, value_ref, output_ref, own_ref, one_ref, two_ref, three_ref, outs, sems, out_sems
):
    core, quad, plane = place_ref[0], place_ref[1], place_ref[2]
    pairs, out_pairs, targets = [], [], []

    def out_tile(y, yb, z, zb, target):
        start = (((y * 2 + yb) * 4 + z) * 2 + zb) * 128
        out_pairs.append((output_ref.at[:, pl.ds(pl.multiple_of(start, 128), 128)], outs.at[len(targets)]))
        targets.append(target)

    for k, piece in ((1, one_ref), (2, two_ref), (3, three_ref)):
        yb, zb = lax.div(quad, 2) ^ (k // 2), lax.rem(quad, 2) ^ (k % 2)
        for w, matrix in enumerate((query_ref, key_ref, value_ref)):
            pairs.append((matrix.at[core, yb, plane, zb], piece.at[:, w * 128 : w * 128 + 128]))
        out_tile(core, yb, plane, zb, piece)
    yb, zb = lax.div(quad, 2), lax.rem(quad, 2)
    for y in range(2):
        for w, matrix in enumerate((query_ref, key_ref, value_ref)):
            pairs.append((matrix.at[y, yb, :, zb], own_ref.at[y * 4 : y * 4 + 4, :, w * 128 : w * 128 + 128]))
        for z in range(4):
            out_tile(y, yb, z, zb, own_ref.at[y * 4 + z])
    out_copies = fetch(out_pairs, out_sems)
    copies = fetch(pairs, sems)
    eye = (
        lax.broadcasted_iota(jnp.int32, (128, 128), 0) == lax.broadcasted_iota(jnp.int32, (128, 128), 1)
    ).astype(BF16)
    for i, (copy, target) in enumerate(zip(out_copies, targets)):
        copy.wait()
        target[:, OUT] = dot(eye, outs[i], NT).astype(BF16)
    for copy in copies:
        copy.wait()


def assemble_kernel(place_ref, *refs):
    pieces, (out_ref, held, sems) = refs[:8], refs[8:]
    core, plane = place_ref[0], place_ref[2]
    copies = []
    for k in range(3):
        for i, ref in enumerate(pieces):
            held[k, (core ^ (i // 4)) * 4 + lax.rem(plane + 4 - i % 4, 4)] = ref[k]
        copies.append(pltpu.make_async_copy(held.at[k], out_ref.at[k], sems.at[k]))
        copies[-1].start()
    for copy in copies:
        copy.wait()


def fetch_heads(own_ref, rest_ref, weights, sems):
    return fetch([(own_ref, weights.at[0])] + [(rest_ref.at[k - 1], weights.at[k]) for k in (1, 2, 3)], sems)


def add_up_kernel(terms_ref, out_ref):
    total = jnp.sum(terms_ref[...], 0)
    for i in range(out_ref.shape[0]):
        out_ref[i] = total


def adapter_kernel(
    sums_ref, first_ref, second_ref, gfirst_ref, gsecond_ref, up_ref, downt_ref,
    shared_ref, in_second_ref, first_grad_ref, adapters_ref,
):
    seq = first_ref.shape[0]
    sums = sums_ref[...]
    pre_act = sums[:, :RANK]
    back_sum = pltpu.roll(sums, RANK, 1)[:, :RANK]
    logistic = 1.0 / (1.0 + jnp.exp(-pre_act))
    activation = (pre_act * logistic).astype(BF16)
    pre_grad = (back_sum * (logistic * (1.0 + pre_act * (1.0 - logistic)))).astype(BF16)
    in_second = (second_ref[...].astype(F32) - dot(activation, up_ref[...])).astype(BF16)
    first_grad = (gfirst_ref[...].astype(F32) + dot(pre_grad, downt_ref[...])).astype(BF16)
    in_second_ref[...] = in_second
    first_grad_ref[...] = first_grad
    for s in range(8):
        shared_ref[s, :seq] = in_second
        shared_ref[s, seq:] = first_grad
    adapters_ref[:RANK] = dot(pre_grad, first_ref[...], TN)
    adapters_ref[RANK:] = dot(activation, gsecond_ref[...], TN)


def project_kernel(
    place_ref, gathered_ref, gain_ref, own_ref, rest_ref, partial_ref,
    weights, x_ref, g_ref, out, in_sems, out_sems,
):
    seq, quad = x_ref.shape[0], place_ref[1]
    arriving = fetch_heads(own_ref, rest_ref, weights, in_sems)
    squares = jnp.zeros((seq, 128), F32)
    for f in range(8):
        lanes = slice(f * 128, f * 128 + 128)
        wide = gathered_ref[f, :seq].astype(F32)
        squares = squares + wide * wide
        x_ref[:, lanes] = (wide * gain_ref[f : f + 1, :]).astype(BF16)
        g_ref[:, lanes] = gathered_ref[f, seq:]
    lead, rest = row_sums(squares)
    tail = jnp.concatenate([lead, rest], 0)
    leaving = []
    for k in range(4):
        arriving[k].wait()
        out[k, :seq, QKV] = dot(x_ref[...], weights[k, :, :, QKV].reshape(1024, 384)).astype(BF16)
        out[k, :seq, OUT] = dot(g_ref[...], weights[k, :, :, OUT].reshape(1024, 128)).astype(BF16)
        out[k, seq:, :seq] = tail
        out[k, seq:, seq:] = jnp.zeros((16, 512 - seq), BF16)
        leaving.append(pltpu.make_async_copy(out.at[k], partial_ref.at[quad ^ k], out_sems.at[k]))
        leaving[-1].start()
    for copy in leaving:
        copy.wait()


def attention_kernel(width, partial_ref, grads_ref, inv_ref, out, sems):
    seq = inv_ref.shape[0]
    scale = HEAD_DIM ** (-0.5)

    def total(lo, hi):
        rows = partial_ref[0, :seq, lo:hi].astype(F32)
        for s in range(1, 4):
            rows = rows + partial_ref[s, :seq, lo:hi].astype(F32)
        return rows

    square = jnp.zeros((1, seq), F32)
    for s in range(4):
        tail = partial_ref[s, seq:, :seq].astype(F32)
        square = square + tail[:1] + tail[8:9]
    inv = to_column(lax.rsqrt(square / width + EPS))
    inv_ref[...] = inv
    query_wide, key_wide, value_wide = total(0, 128) * inv, total(128, 256) * inv, total(256, 384) * inv
    query, key, value = query_wide.astype(BF16), key_wide.astype(BF16), value_wide.astype(BF16)
    back_ctx = total(384, 512).astype(BF16)
    scores = dot(query, key, NT) * scale
    query_pos = lax.broadcasted_iota(jnp.int32, (seq, seq), 0)
    key_pos = lax.broadcasted_iota(jnp.int32, (seq, seq), 1)
    scores = jnp.where(key_pos <= query_pos, scores, MASKED)
    weights = jnp.exp(scores - jnp.max(scores, axis=1, keepdims=True))
    probs = (weights / jnp.sum(weights, axis=1, keepdims=True)).astype(BF16)
    context = dot(probs, value).astype(BF16)
    value_grad = dot(probs, back_ctx, TN).astype(BF16)
    prob_grad = dot(back_ctx, value, NT)
    prob_wide = probs.astype(F32)
    inner = jnp.sum(prob_grad * prob_wide, axis=1, keepdims=True)
    score_grad = (prob_wide * (prob_grad - inner) * scale).astype(BF16)
    query_grad = dot(score_grad, key).astype(BF16)
    key_grad = dot(score_grad, query, TN).astype(BF16)
    stat = (
        query_grad.astype(F32) * query_wide + key_grad.astype(F32) * key_wide + value_grad.astype(F32) * value_wide
    )
    lead, rest = row_sums(stat)
    tail = jnp.concatenate([lead, rest], 0)
    out[:seq, :128] = query_grad
    out[:seq, 128:256] = key_grad
    out[:seq, 256:384] = value_grad
    out[:seq, OUT] = context
    out[seq:, :seq] = tail
    out[seq:, seq:] = jnp.zeros((16, 512 - seq), BF16)
    for copy in fetch([(out, grads_ref.at[s]) for s in range(4)], sems):
        copy.wait()


def spread_kernel(
    place_ref, grads_ref, adapters_ref, arrived_ref, own_ref, rest_ref, terms_ref, adapters_out_ref,
    weights, norm, attn, out, in_sems, out_sems,
):
    quad = place_ref[1]
    arriving = fetch_heads(own_ref, rest_ref, weights, in_sems)
    adapters_out_ref[...] = adapters_ref[...] + arrived_ref[...]
    seq = grads_ref.shape[1] - 16
    stat = jnp.zeros((8, seq), F32)
    for h in range(4):
        tail = grads_ref[h, seq:, :seq].astype(F32)
        stat = stat + tail[:8] + tail[8:]
    halves = []
    for lanes in (slice(0, 128), slice(128, 256)):
        lead = stat[:4, lanes].astype(BF16)
        halves += [lead, (stat[:4, lanes] - lead.astype(F32)).astype(BF16)]
    tail = jnp.concatenate([half.astype(F32) for half in halves], 0).astype(BF16)
    for k in range(4):
        h = quad ^ k
        arriving[k].wait()
        into_norm = dot(grads_ref[h, :seq, QKV], weights[k, :, :, QKV].reshape(1024, 384), NT)
        into_attn = dot(grads_ref[h, :seq, OUT], weights[k, :, :, OUT].reshape(1024, 128), NT)
        norm[...] = norm[...] + into_norm if k else into_norm
        attn[...] = attn[...] + into_attn if k else into_attn
    leaving = []
    for f in range(8):
        lanes = slice(f * 128, f * 128 + 128)
        out[f, :seq] = attn[:, lanes].astype(BF16)
        out[f, seq : 2 * seq] = norm[:, lanes].astype(BF16)
        out[f, 2 * seq :] = tail
        leaving.append(pltpu.make_async_copy(out.at[f], terms_ref.at[f], out_sems.at[f]))
        leaving[-1].start()
    for copy in leaving:
        copy.wait()


def finish_kernel(
    width, terms_ref, inv_ref, first_ref, in_second_ref, gsecond_ref, gain_ref, adapters_ref, arrived_ref,
    in_first_ref, second_grad_ref, down_grad_ref, up_grad_ref,
):
    down_grad_ref[...] = adapters_ref[:RANK].astype(F32) + arrived_ref[:RANK].astype(F32)
    up_grad_ref[...] = adapters_ref[RANK:].astype(F32) + arrived_ref[RANK:].astype(F32)
    seq = first_ref.shape[0]
    total = terms_ref[0].astype(F32)
    for s in range(1, 8):
        total = total + terms_ref[s].astype(F32)
    in_first_ref[...] = (first_ref[...].astype(F32) - total[:seq]).astype(BF16)
    halves = [total[2 * seq + i : 2 * seq + i + 1] + total[2 * seq + i + 4 : 2 * seq + i + 5] for i in (0, 8)]
    stat = jnp.concatenate([to_column(half) for half in halves], 0) / width
    inv = inv_ref[...]
    gain_grad = gain_ref[...] * total[seq : 2 * seq]
    second = in_second_ref[...].astype(F32)
    second_grad_ref[...] = (gsecond_ref[...].astype(F32) + inv * (gain_grad - second * stat * inv)).astype(BF16)


def shards(
    interpret,
    out_first,
    out_second,
    grad_first,
    grad_second,
    norm_gain,
    query_proj,
    key_proj,
    value_proj,
    output_proj,
    adapter_down,
    adapter_up,
):
    seq = out_first.shape[0]
    width = query_proj.shape[0]
    shape = jax.ShapeDtypeStruct
    place = jnp.stack([lax.axis_index("c"), lax.axis_index(QUAD), lax.axis_index("x")]).astype(jnp.int32)
    smem, hbm, vmem = (pl.BlockSpec(memory_space=m) for m in (pltpu.SMEM, pltpu.HBM, pltpu.VMEM))
    down_t = adapter_down.T
    block, grads_block = shape((seq, 128), BF16), shape((2 * RANK, 128), F32)

    def swap(array, axis, bit=1):
        return lax.ppermute(array, axis, [(i, i ^ bit) for i in range(4 if axis in ("x", QUAD) else 2)])

    partial = call(
        bottleneck_kernel,
        shape((seq, 128), F32),
        interpret,
        56,
        in_specs=[hbm] * 4,
        scratch_shapes=[pltpu.VMEM((seq, 128), BF16)] * 2
        + [pltpu.VMEM((RANK, 128), BF16)] * 2
        + [pltpu.SemaphoreType.DMA((4,))],
    )(out_first, grad_second, down_t, adapter_up)
    terms = lax.all_to_all(partial.reshape(32, seq // 32, 128), PLANE, 0, 0)
    mine = call(add_up_kernel, shape(terms.shape, F32), interpret)(terms)

    tiles = (2, 2, 4, 2, 128, 128)
    matrices = (query_proj.reshape(tiles), key_proj.reshape(tiles), value_proj.reshape(tiles), output_proj)
    own, *pieces = call(
        pack_kernel,
        (shape((8, 128, 512), BF16),) + (shape((128, 512), BF16),) * 3,
        interpret,
        56,
        in_specs=[smem] + [hbm] * 4,
        scratch_shapes=[
            pltpu.VMEM((11, 128, 128), BF16),
            pltpu.SemaphoreType.DMA((15,)),
            pltpu.SemaphoreType.DMA((11,)),
        ],
    )(place, *matrices)
    fetched = [swap(piece, QUAD, k) for k, piece in enumerate(pieces, 1)]
    mine, fetched[0] = lax.optimization_barrier((mine, fetched[0]))
    sums = lax.all_to_all(mine, PLANE, 0, 0).reshape(seq, 128)
    sums, fetched = lax.optimization_barrier((sums, fetched))
    fetched = jnp.stack(fetched)
    here = [fetched] + [lax.ppermute(fetched, "x", [(i, (i + s) % 4) for i in range(4)]) for s in (1, 3, 2)]
    here = [here[0], here[1], here[3], here[2]]
    held = pltpu.VMEM((4, 8, 128, 512), BF16)

    gain = norm_gain.astype(F32).reshape(2, 2, 4, 2, 128)
    gain = lax.dynamic_index_in_dim(gain, lax.axis_index("yb"), 1, False)
    gain = lax.dynamic_index_in_dim(gain, lax.axis_index("zb"), 2, False).reshape(8, 128)
    gain_local = lax.dynamic_slice_in_dim(gain, lax.axis_index(OCTET), 1)

    shared, in_second, first_grad, adapters = call(
        adapter_kernel,
        (shape((8, 2 * seq, 128), BF16), block, block, grads_block),
        interpret,
    )(sums, out_first, out_second, grad_first, grad_second, adapter_up, down_t)
    gathered = lax.all_to_all(shared, OCTET, 0, 0)
    rest = call(
        assemble_kernel,
        shape((3, 8, 128, 512), BF16),
        interpret,
        54,
        in_specs=[smem] + [vmem] * 8,
        out_specs=hbm,
        scratch_shapes=[pltpu.VMEM((3, 8, 128, 512), BF16), pltpu.SemaphoreType.DMA((3,))],
    )(place, *here, *(swap(piece, "c") for piece in here))

    quads = shape((4, seq + 16, 512), BF16)
    projected = call(
        project_kernel,
        quads,
        interpret,
        48,
        in_specs=[smem, vmem, vmem, hbm, hbm],
        out_specs=hbm,
        scratch_shapes=[
            held,
            pltpu.VMEM((seq, 1024), BF16),
            pltpu.VMEM((seq, 1024), BF16),
            pltpu.VMEM(quads.shape, BF16),
            pltpu.SemaphoreType.DMA((4,)),
            pltpu.SemaphoreType.DMA((4,)),
        ],
    )(place, gathered, gain, own, rest)
    projected = lax.all_to_all(projected, QUAD, 0, 0)
    grads, inv_rms = call(
        functools.partial(attention_kernel, width),
        (quads, shape((seq, 128), F32)),
        interpret,
        48,
        out_specs=(hbm, vmem),
        scratch_shapes=[pltpu.VMEM(quads.shape[1:], BF16), pltpu.SemaphoreType.DMA((4,))],
    )(projected)
    grads = lax.all_to_all(grads, QUAD, 0, 0)
    octets = shape((8, 2 * seq + 16, 128), BF16)
    outward, adapters = call(
        spread_kernel,
        (octets, grads_block),
        interpret,
        48,
        in_specs=[smem, vmem, vmem, vmem, hbm, hbm],
        out_specs=(hbm, vmem),
        scratch_shapes=[
            held,
            pltpu.VMEM((seq, 1024), F32),
            pltpu.VMEM((seq, 1024), F32),
            pltpu.VMEM(octets.shape, BF16),
            pltpu.SemaphoreType.DMA((4,)),
            pltpu.SemaphoreType.DMA((8,)),
        ],
    )(place, grads, adapters, swap(adapters, "c"), own, rest)
    inward = lax.all_to_all(outward, OCTET, 0, 0)
    adapters = adapters + swap(adapters, "x", 2)
    adapters = adapters + swap(adapters, "x", 1)
    adapters = adapters.astype(BF16)
    in_first, second_grad, down_grad, up_grad = call(
        functools.partial(finish_kernel, width),
        (block, block, shape((RANK, 128), F32), shape((RANK, 128), F32)),
        interpret,
    )(inward, inv_rms, out_first, in_second, grad_second, gain_local, adapters, swap(adapters, "yh"))
    return (in_first, in_second, first_grad, second_grad, down_grad.T, up_grad)


def over(mesh, interpret=False):
    rows, columns = P(SEQS, PLANE), P(None, PLANE)
    return jax.shard_map(
        functools.partial(shards, interpret),
        mesh=mesh,
        in_specs=(rows, rows, rows, rows, P(), columns, columns, columns, P(PLANE, None), P(PLANE, None), columns),
        out_specs=(rows, rows, rows, rows, P(PLANE, None), columns),
        check_vma=False,
    )


def solution(mesh):
    devices = mesh.devices.reshape(2, 4, 2, 2, 2, 4, 2)
    return over(Mesh(devices, SEQS + PLANE))
```

```python
import functools

import jax
import jax.numpy as jnp
from jax import lax
from jax.experimental import pallas as pl
from jax.experimental.pallas import tpu as pltpu
from jax.sharding import Mesh, PartitionSpec as P

HEAD_DIM = 128
RANK = 64
EPS = 1e-05
MASKED = -1e30

QUAD = ("yb", "zb")
OCTET = ("ya", "za")
PLANE = ("ya", "yb", "za", "zb")
SEQS = ("yh", "x", "c")
QKV, OUT = slice(0, 384), slice(384, 512)
F32 = jnp.float32
BF16 = jnp.bfloat16


def dot(a, b, dims=((1,), (0,)), precision=None):
    return lax.dot_general(a, b, (dims, ((), ())), preferred_element_type=F32, precision=precision)


NT = ((1,), (1,))
TN = ((0,), (0,))


def row_sums(wide):
    sums = dot(jnp.ones((8, 128), F32), wide, NT, lax.Precision.HIGHEST)
    lead = sums.astype(BF16)
    rest = (sums - lead.astype(F32)).astype(BF16)
    return lead, rest


def to_column(row):
    return jnp.broadcast_to(row, (128, row.shape[1])).T


def call(body, out_shapes, interpret, vmem=16, **kwargs):
    return pl.pallas_call(
        body,
        out_shape=out_shapes,
        compiler_params=pltpu.CompilerParams(vmem_limit_bytes=vmem * 1024 * 1024),
        interpret=interpret,
        **kwargs,
    )


def fetch(pairs, sems):
    copies = [pltpu.make_async_copy(src, dst, sems.at[i]) for i, (src, dst) in enumerate(pairs)]
    for copy in copies:
        copy.start()
    return copies


def bottleneck_kernel(first_ref, gsecond_ref, downt_ref, up_ref, partial_ref, first, gsecond, downt, up, sems):
    copies = fetch(((downt_ref, downt), (up_ref, up), (first_ref, first), (gsecond_ref, gsecond)), sems)
    for copy in copies:
        copy.wait()
    partial_ref[:, :RANK] = dot(first[...], downt[...], NT)
    partial_ref[:, RANK:] = dot(gsecond[...], up[...], NT)


def pack_kernel(
    place_ref, query_ref, key_ref, value_ref, output_ref, own_ref, one_ref, two_ref, three_ref, outs, sems, out_sems
):
    core, quad, plane = place_ref[0], place_ref[1], place_ref[2]
    pairs, out_pairs, targets = [], [], []

    def out_tile(y, yb, z, zb, target):
        start = (((y * 2 + yb) * 4 + z) * 2 + zb) * 128
        out_pairs.append((output_ref.at[:, pl.ds(pl.multiple_of(start, 128), 128)], outs.at[len(targets)]))
        targets.append(target)

    for k, piece in ((1, one_ref), (2, two_ref), (3, three_ref)):
        yb, zb = lax.div(quad, 2) ^ (k // 2), lax.rem(quad, 2) ^ (k % 2)
        for w, matrix in enumerate((query_ref, key_ref, value_ref)):
            pairs.append((matrix.at[core, yb, plane, zb], piece.at[:, w * 128 : w * 128 + 128]))
        out_tile(core, yb, plane, zb, piece)
    yb, zb = lax.div(quad, 2), lax.rem(quad, 2)
    for y in range(2):
        for w, matrix in enumerate((query_ref, key_ref, value_ref)):
            pairs.append((matrix.at[y, yb, :, zb], own_ref.at[y * 4 : y * 4 + 4, :, w * 128 : w * 128 + 128]))
        for z in range(4):
            out_tile(y, yb, z, zb, own_ref.at[y * 4 + z])
    out_copies = fetch(out_pairs, out_sems)
    copies = fetch(pairs, sems)
    eye = (
        lax.broadcasted_iota(jnp.int32, (128, 128), 0) == lax.broadcasted_iota(jnp.int32, (128, 128), 1)
    ).astype(BF16)
    for i, (copy, target) in enumerate(zip(out_copies, targets)):
        copy.wait()
        target[:, OUT] = dot(eye, outs[i], NT).astype(BF16)
    for copy in copies:
        copy.wait()


def assemble_kernel(place_ref, *refs):
    pieces, (out_ref, held, sems) = refs[:8], refs[8:]
    core, plane = place_ref[0], place_ref[2]
    copies = []
    for k in range(3):
        for i, ref in enumerate(pieces):
            held[k, (core ^ (i // 4)) * 4 + lax.rem(plane + 4 - i % 4, 4)] = ref[k]
        copies.append(pltpu.make_async_copy(held.at[k], out_ref.at[k], sems.at[k]))
        copies[-1].start()
    for copy in copies:
        copy.wait()


def fetch_heads(own_ref, rest_ref, weights, sems):
    return fetch([(own_ref, weights.at[0])] + [(rest_ref.at[k - 1], weights.at[k]) for k in (1, 2, 3)], sems)


def add_up_kernel(terms_ref, out_ref):
    total = jnp.sum(terms_ref[...], 0)
    for i in range(out_ref.shape[0]):
        out_ref[i] = total


def adapter_kernel(
    sums_ref, first_ref, second_ref, gfirst_ref, gsecond_ref, up_ref, downt_ref,
    shared_ref, in_second_ref, first_grad_ref, adapters_ref,
):
    seq = first_ref.shape[0]
    sums = sums_ref[...]
    pre_act = sums[:, :RANK]
    back_sum = pltpu.roll(sums, RANK, 1)[:, :RANK]
    logistic = 1.0 / (1.0 + jnp.exp(-pre_act))
    activation = (pre_act * logistic).astype(BF16)
    pre_grad = (back_sum * (logistic * (1.0 + pre_act * (1.0 - logistic)))).astype(BF16)
    in_second = (second_ref[...].astype(F32) - dot(activation, up_ref[...])).astype(BF16)
    first_grad = (gfirst_ref[...].astype(F32) + dot(pre_grad, downt_ref[...])).astype(BF16)
    in_second_ref[...] = in_second
    first_grad_ref[...] = first_grad
    for s in range(8):
        shared_ref[s, :seq] = in_second
        shared_ref[s, seq:] = first_grad
    adapters_ref[:RANK] = dot(pre_grad, first_ref[...], TN)
    adapters_ref[RANK:] = dot(activation, gsecond_ref[...], TN)


def project_kernel(
    place_ref, gathered_ref, gain_ref, own_ref, rest_ref, partial_ref,
    weights, x_ref, g_ref, out, in_sems, out_sems,
):
    seq, quad = x_ref.shape[0], place_ref[1]
    arriving = fetch_heads(own_ref, rest_ref, weights, in_sems)
    squares = jnp.zeros((seq, 128), F32)
    for f in range(8):
        lanes = slice(f * 128, f * 128 + 128)
        wide = gathered_ref[f, :seq].astype(F32)
        squares = squares + wide * wide
        x_ref[:, lanes] = (wide * gain_ref[f : f + 1, :]).astype(BF16)
        g_ref[:, lanes] = gathered_ref[f, seq:]
    lead, rest = row_sums(squares)
    tail = jnp.concatenate([lead, rest], 0)
    leaving = []
    for k in range(4):
        arriving[k].wait()
        out[k, :seq, QKV] = dot(x_ref[...], weights[k, :, :, QKV].reshape(1024, 384)).astype(BF16)
        out[k, :seq, OUT] = dot(g_ref[...], weights[k, :, :, OUT].reshape(1024, 128)).astype(BF16)
        out[k, seq:, :seq] = tail
        out[k, seq:, seq:] = jnp.zeros((16, 512 - seq), BF16)
        leaving.append(pltpu.make_async_copy(out.at[k], partial_ref.at[quad ^ k], out_sems.at[k]))
        leaving[-1].start()
    for copy in leaving:
        copy.wait()


def attention_kernel(width, partial_ref, grads_ref, inv_ref, out, sems):
    seq = inv_ref.shape[0]
    scale = HEAD_DIM ** (-0.5)

    def total(lo, hi):
        rows = partial_ref[0, :seq, lo:hi].astype(F32)
        for s in range(1, 4):
            rows = rows + partial_ref[s, :seq, lo:hi].astype(F32)
        return rows

    square = jnp.zeros((1, seq), F32)
    for s in range(4):
        tail = partial_ref[s, seq:, :seq].astype(F32)
        square = square + tail[:1] + tail[8:9]
    inv = to_column(lax.rsqrt(square / width + EPS))
    inv_ref[...] = inv
    query_wide, key_wide, value_wide = total(0, 128) * inv, total(128, 256) * inv, total(256, 384) * inv
    query, key, value = query_wide.astype(BF16), key_wide.astype(BF16), value_wide.astype(BF16)
    back_ctx = total(384, 512).astype(BF16)
    scores = dot(query, key, NT) * scale
    query_pos = lax.broadcasted_iota(jnp.int32, (seq, seq), 0)
    key_pos = lax.broadcasted_iota(jnp.int32, (seq, seq), 1)
    scores = jnp.where(key_pos <= query_pos, scores, MASKED)
    weights = jnp.exp(scores - jnp.max(scores, axis=1, keepdims=True))
    probs = (weights / jnp.sum(weights, axis=1, keepdims=True)).astype(BF16)
    context = dot(probs, value).astype(BF16)
    value_grad = dot(probs, back_ctx, TN).astype(BF16)
    prob_grad = dot(back_ctx, value, NT)
    prob_wide = probs.astype(F32)
    inner = jnp.sum(prob_grad * prob_wide, axis=1, keepdims=True)
    score_grad = (prob_wide * (prob_grad - inner) * scale).astype(BF16)
    query_grad = dot(score_grad, key).astype(BF16)
    key_grad = dot(score_grad, query, TN).astype(BF16)
    stat = (
        query_grad.astype(F32) * query_wide + key_grad.astype(F32) * key_wide + value_grad.astype(F32) * value_wide
    )
    lead, rest = row_sums(stat)
    tail = jnp.concatenate([lead, rest], 0)
    out[:seq, :128] = query_grad
    out[:seq, 128:256] = key_grad
    out[:seq, 256:384] = value_grad
    out[:seq, OUT] = context
    out[seq:, :seq] = tail
    out[seq:, seq:] = jnp.zeros((16, 512 - seq), BF16)
    for copy in fetch([(out, grads_ref.at[s]) for s in range(4)], sems):
        copy.wait()


def spread_kernel(
    place_ref, grads_ref, adapters_ref, arrived_ref, own_ref, rest_ref, terms_ref, adapters_out_ref,
    weights, norm, attn, out, in_sems, out_sems,
):
    quad = place_ref[1]
    arriving = fetch_heads(own_ref, rest_ref, weights, in_sems)
    adapters_out_ref[...] = adapters_ref[...] + arrived_ref[...]
    seq = grads_ref.shape[1] - 16
    stat = jnp.zeros((8, seq), F32)
    for h in range(4):
        tail = grads_ref[h, seq:, :seq].astype(F32)
        stat = stat + tail[:8] + tail[8:]
    halves = []
    for lanes in (slice(0, 128), slice(128, 256)):
        lead = stat[:4, lanes].astype(BF16)
        halves += [lead, (stat[:4, lanes] - lead.astype(F32)).astype(BF16)]
    tail = jnp.concatenate([half.astype(F32) for half in halves], 0).astype(BF16)
    for k in range(4):
        h = quad ^ k
        arriving[k].wait()
        into_norm = dot(grads_ref[h, :seq, QKV], weights[k, :, :, QKV].reshape(1024, 384), NT)
        into_attn = dot(grads_ref[h, :seq, OUT], weights[k, :, :, OUT].reshape(1024, 128), NT)
        norm[...] = norm[...] + into_norm if k else into_norm
        attn[...] = attn[...] + into_attn if k else into_attn
    leaving = []
    for f in range(8):
        lanes = slice(f * 128, f * 128 + 128)
        out[f, :seq] = attn[:, lanes].astype(BF16)
        out[f, seq : 2 * seq] = norm[:, lanes].astype(BF16)
        out[f, 2 * seq :] = tail
        leaving.append(pltpu.make_async_copy(out.at[f], terms_ref.at[f], out_sems.at[f]))
        leaving[-1].start()
    for copy in leaving:
        copy.wait()


def finish_kernel(
    width, terms_ref, inv_ref, first_ref, in_second_ref, gsecond_ref, gain_ref, adapters_ref, arrived_ref,
    in_first_ref, second_grad_ref, down_grad_ref, up_grad_ref,
):
    down_grad_ref[...] = adapters_ref[:RANK].astype(F32) + arrived_ref[:RANK].astype(F32)
    up_grad_ref[...] = adapters_ref[RANK:].astype(F32) + arrived_ref[RANK:].astype(F32)
    seq = first_ref.shape[0]
    total = terms_ref[0].astype(F32)
    for s in range(1, 8):
        total = total + terms_ref[s].astype(F32)
    in_first_ref[...] = (first_ref[...].astype(F32) - total[:seq]).astype(BF16)
    halves = [total[2 * seq + i : 2 * seq + i + 1] + total[2 * seq + i + 4 : 2 * seq + i + 5] for i in (0, 8)]
    stat = jnp.concatenate([to_column(half) for half in halves], 0) / width
    inv = inv_ref[...]
    gain_grad = gain_ref[...] * total[seq : 2 * seq]
    second = in_second_ref[...].astype(F32)
    second_grad_ref[...] = (gsecond_ref[...].astype(F32) + inv * (gain_grad - second * stat * inv)).astype(BF16)


def shards(
    interpret,
    out_first,
    out_second,
    grad_first,
    grad_second,
    norm_gain,
    query_proj,
    key_proj,
    value_proj,
    output_proj,
    adapter_down,
    adapter_up,
):
    seq = out_first.shape[0]
    width = query_proj.shape[0]
    shape = jax.ShapeDtypeStruct
    place = jnp.stack([lax.axis_index("c"), lax.axis_index(QUAD), lax.axis_index("x")]).astype(jnp.int32)
    smem, hbm, vmem = (pl.BlockSpec(memory_space=m) for m in (pltpu.SMEM, pltpu.HBM, pltpu.VMEM))
    down_t = adapter_down.T
    block, grads_block = shape((seq, 128), BF16), shape((2 * RANK, 128), F32)

    def swap(array, axis, bit=1):
        return lax.ppermute(array, axis, [(i, i ^ bit) for i in range(4 if axis in ("x", QUAD) else 2)])

    partial = call(
        bottleneck_kernel,
        shape((seq, 128), F32),
        interpret,
        56,
        in_specs=[hbm] * 4,
        scratch_shapes=[pltpu.VMEM((seq, 128), BF16)] * 2
        + [pltpu.VMEM((RANK, 128), BF16)] * 2
        + [pltpu.SemaphoreType.DMA((4,))],
    )(out_first, grad_second, down_t, adapter_up)
    terms = lax.all_to_all(partial.reshape(32, seq // 32, 128), PLANE, 0, 0)
    mine = call(add_up_kernel, shape(terms.shape, F32), interpret)(terms)

    tiles = (2, 2, 4, 2, 128, 128)
    matrices = (query_proj.reshape(tiles), key_proj.reshape(tiles), value_proj.reshape(tiles), output_proj)
    own, *pieces = call(
        pack_kernel,
        (shape((8, 128, 512), BF16),) + (shape((128, 512), BF16),) * 3,
        interpret,
        56,
        in_specs=[smem] + [hbm] * 4,
        scratch_shapes=[
            pltpu.VMEM((11, 128, 128), BF16),
            pltpu.SemaphoreType.DMA((15,)),
            pltpu.SemaphoreType.DMA((11,)),
        ],
    )(place, *matrices)
    mine, pieces = lax.optimization_barrier((mine, pieces))
    fetched = [swap(piece, QUAD, k) for k, piece in enumerate(pieces, 1)]
    sums = lax.all_to_all(mine, PLANE, 0, 0).reshape(seq, 128)
    sums, fetched = lax.optimization_barrier((sums, fetched))
    fetched = jnp.stack(fetched)
    here = [fetched] + [lax.ppermute(fetched, "x", [(i, (i + s) % 4) for i in range(4)]) for s in (1, 3, 2)]
    here = [here[0], here[1], here[3], here[2]]
    held = pltpu.VMEM((4, 8, 128, 512), BF16)

    gain = norm_gain.astype(F32).reshape(2, 2, 4, 2, 128)
    gain = lax.dynamic_index_in_dim(gain, lax.axis_index("yb"), 1, False)
    gain = lax.dynamic_index_in_dim(gain, lax.axis_index("zb"), 2, False).reshape(8, 128)
    gain_local = lax.dynamic_slice_in_dim(gain, lax.axis_index(OCTET), 1)

    shared, in_second, first_grad, adapters = call(
        adapter_kernel,
        (shape((8, 2 * seq, 128), BF16), block, block, grads_block),
        interpret,
    )(sums, out_first, out_second, grad_first, grad_second, adapter_up, down_t)
    gathered = lax.all_to_all(shared, OCTET, 0, 0)
    rest = call(
        assemble_kernel,
        shape((3, 8, 128, 512), BF16),
        interpret,
        54,
        in_specs=[smem] + [vmem] * 8,
        out_specs=hbm,
        scratch_shapes=[pltpu.VMEM((3, 8, 128, 512), BF16), pltpu.SemaphoreType.DMA((3,))],
    )(place, *here, *(swap(piece, "c") for piece in here))

    quads = shape((4, seq + 16, 512), BF16)
    projected = call(
        project_kernel,
        quads,
        interpret,
        48,
        in_specs=[smem, vmem, vmem, hbm, hbm],
        out_specs=hbm,
        scratch_shapes=[
            held,
            pltpu.VMEM((seq, 1024), BF16),
            pltpu.VMEM((seq, 1024), BF16),
            pltpu.VMEM(quads.shape, BF16),
            pltpu.SemaphoreType.DMA((4,)),
            pltpu.SemaphoreType.DMA((4,)),
        ],
    )(place, gathered, gain, own, rest)
    projected = lax.all_to_all(projected, QUAD, 0, 0)
    grads, inv_rms = call(
        functools.partial(attention_kernel, width),
        (quads, shape((seq, 128), F32)),
        interpret,
        48,
        out_specs=(hbm, vmem),
        scratch_shapes=[pltpu.VMEM(quads.shape[1:], BF16), pltpu.SemaphoreType.DMA((4,))],
    )(projected)
    grads = lax.all_to_all(grads, QUAD, 0, 0)
    octets = shape((8, 2 * seq + 16, 128), BF16)
    outward, adapters = call(
        spread_kernel,
        (octets, grads_block),
        interpret,
        48,
        in_specs=[smem, vmem, vmem, vmem, hbm, hbm],
        out_specs=(hbm, vmem),
        scratch_shapes=[
            held,
            pltpu.VMEM((seq, 1024), F32),
            pltpu.VMEM((seq, 1024), F32),
            pltpu.VMEM(octets.shape, BF16),
            pltpu.SemaphoreType.DMA((4,)),
            pltpu.SemaphoreType.DMA((8,)),
        ],
    )(place, grads, adapters, swap(adapters, "c"), own, rest)
    inward = lax.all_to_all(outward, OCTET, 0, 0)
    adapters = adapters + swap(adapters, "x", 2)
    adapters = adapters + swap(adapters, "x", 1)
    adapters = adapters.astype(BF16)
    in_first, second_grad, down_grad, up_grad = call(
        functools.partial(finish_kernel, width),
        (block, block, shape((RANK, 128), F32), shape((RANK, 128), F32)),
        interpret,
    )(inward, inv_rms, out_first, in_second, grad_second, gain_local, adapters, swap(adapters, "yh"))
    return (in_first, in_second, first_grad, second_grad, down_grad.T, up_grad)


def over(mesh, interpret=False):
    rows, columns = P(SEQS, PLANE), P(None, PLANE)
    return jax.shard_map(
        functools.partial(shards, interpret),
        mesh=mesh,
        in_specs=(rows, rows, rows, rows, P(), columns, columns, columns, P(PLANE, None), P(PLANE, None), columns),
        out_specs=(rows, rows, rows, rows, P(PLANE, None), columns),
        check_vma=False,
    )


def solution(mesh):
    devices = mesh.devices.reshape(2, 4, 2, 2, 2, 4, 2)
    return over(Mesh(devices, SEQS + PLANE))
```
